256 devices in a mesh: seq: 64 (over y_hi, z, x), tp: 4 (over y_lo, core).
Axes of the slice: x: 4, y: 4 (y_hi: 2, y_lo: 2; y = y_hi * 2 + y_lo), z: 8, core: 2. Of those that a mesh axis runs over, the one named last changes fastest.
Arguments:
- frames: bfloat16 [65536, 2048], P(('seq', 'tp'))
- w_query: bfloat16 [2048, 2048], P(None, 'tp')
- w_key: bfloat16 [2048, 2048], P(None, 'tp')
- w_value: bfloat16 [2048, 2048], P(None, 'tp'), may hold values from -0.125 to 0.125
- w_out: bfloat16 [2048, 2048], P('tp'), may hold values from -0.125 to 0.125
- key_blocks: int32 [512, 8], P('seq'), may hold values from -1 to 511, as said below
Outputs:
- mixed: bfloat16 [65536, 2048], P(('seq', 'tp'))
The draws below stay inside these ranges and needn't reach their ends.
Inputs may be any that keep to these rules, and one draw needn't show every extreme that they name: `key_blocks`: blocks hold 128 frames. For row b let b0 = b - b % 4. Every entry is -1 or a block index k with b0 - 56 <= k <= b0 + 4; the entries of a row other than -1 are distinct and include the 4 blocks b0 to b0 + 3; -1 stands only where an entry would fall outside the recording. All rows with the same b0 list the same entries below b0, at most three of them. Every draw has rows that list b0 - 56 and rows that list b0 + 4.
All inputs are finite; a program needn't handle non-finite values.
Results may differ from the reference program's by a relative error of at most 0.015.
Values may be sent and summed in bfloat16 or wider, within the bound.
No kernel may reach another device: no remote copies, remote signals or barrier semaphores. Data moves between devices by JAX's collectives and lax.ppermute only.
A program may use at most 192 MiB of HBM per device.

```python
import jax
import jax.numpy as jnp
from jax import lax

D = 2048
HEADS = 32
HDIM = 64
BLOCK = 128
GROUP = 4
BLK_DEV = 8
REACH = 56
FRAMES = 65536
QBLOCKS = 512


def shared_base(key):
    return jax.random.normal(key, (D, D), jnp.float32)


def draw_w_query(key, part):
    base = shared_base(key)
    return (base * D ** (-0.5)).astype(jnp.bfloat16)


def draw_w_key(key, part):
    key = jax.random.fold_in(key, 5)
    first = jax.random.fold_in(key, 0)
    noise = jax.random.normal(first, (D, D), jnp.float32)
    return (noise * D ** (-0.5)).astype(jnp.bfloat16)


def draw_frames(key, part):
    key = jax.random.fold_in(key, 7)
    first = jax.random.fold_in(key, 0)
    return jax.random.normal(first, (FRAMES, D), jnp.float32).astype(jnp.bfloat16)


def draw_key_blocks(key, part):
    key = jax.random.fold_in(key, 11)
    first, second, third, fourth = jax.random.split(key, 4)
    shard_count = QBLOCKS // BLK_DEV
    depth = REACH // BLK_DEV
    segments = QBLOCKS // GROUP
    flagged = jax.random.randint(first, (shard_count,), 0, 3) == 0
    distance = jax.random.randint(second, (shard_count,), 1, depth + 1).astype(jnp.int32)
    run_start = jax.random.randint(third, (), 0, shard_count - depth)
    for step in range(depth):
        target = depth + (run_start + step) % (shard_count - depth)
        flagged = flagged.at[target].set(True)
        distance = distance.at[target].set(step + 1)
    seg_start = jnp.arange(segments, dtype=jnp.int32) * GROUP
    owner = seg_start // BLK_DEV
    segment_marker = flagged[owner]
    seg_dist = distance[owner]
    back = jnp.arange(1, REACH + 1, dtype=jnp.int32)
    candidate = seg_start[:, None] - back[None, :]
    raw = jax.random.randint(fourth, (segments, REACH), 0, 2 ** 18).astype(jnp.int32)
    logit_matrix = raw * REACH + (back - 1)[None, :]
    within_partition = jnp.floor_divide(candidate, BLK_DEV) == (owner - seg_dist)[:, None]
    score_offset_extra = jnp.where(segment_marker[:, None] & within_partition, 2 ** 28, 0)
    earliest_frame = segment_marker[:, None] & (seg_dist[:, None] == depth) & (back[None, :] == REACH)
    score_offset_extra = score_offset_extra + jnp.where(earliest_frame, 2 ** 29, 0)
    selected_blocks = lax.top_k((logit_matrix + score_offset_extra).astype(jnp.int32), 3)[1]
    memory = jnp.take_along_axis(candidate, selected_blocks, axis=1).astype(jnp.int32)
    memory_rows = jnp.repeat(memory, GROUP, axis=0)
    block = jnp.arange(QBLOCKS, dtype=jnp.int32)
    start = block - block % GROUP
    columns = []
    for offset in range(GROUP):
        columns.append(start + offset)
    columns.append(start + GROUP)
    listed = jnp.concatenate([memory_rows, jnp.stack(columns, axis=1)], axis=1).astype(jnp.int32)
    inside = (listed >= 0) & (listed < QBLOCKS)
    return jnp.where(inside, listed, -1).astype(jnp.int32)


def steps_of(own_key, dims, pieces, smallest, top_value):
    factor_of, own = 1.0, jax.random.fold_in(own_key, 6)
    for dim, parts in pieces:
        draws = jnp.exp(jax.random.uniform(jax.random.fold_in(own, dim), (parts,), jnp.float32, smallest / len(pieces), top_value / len(pieces)))
        factor_of = factor_of * jnp.repeat(draws, dims[dim] // parts).reshape([-1 if axis == dim else 1 for axis in range(len(dims))])
    return factor_of


def normal_values(own_key, dims, width, most, pieces=(), held_as=jnp.bfloat16):
    array = width * jax.random.normal(own_key, dims, jnp.float32)
    if pieces:
        array = array * steps_of(own_key, dims, pieces, -0.22, 0.18)
    return jnp.clip(array, -most, most).astype(held_as)


def setup_inputs(seed: int = 0) -> dict:
    arg_keys = jax.random.split(jax.random.key(seed), 7)
    frames = draw_frames(jax.random.fold_in(arg_keys[6], 71), 0)
    w_query = draw_w_query(jax.random.fold_in(arg_keys[6], 71), 0)
    w_key = draw_w_key(jax.random.fold_in(arg_keys[6], 71), 0)
    w_value = normal_values(arg_keys[3], (D, D), D ** -0.5, 0.125, ((1, 4),))
    w_out = normal_values(arg_keys[4], (D, D), D ** -0.5, 0.125, ((0, 4),))
    key_blocks = draw_key_blocks(jax.random.fold_in(arg_keys[6], 71), 0)
    return {"frames": frames, "w_query": w_query, "w_key": w_key, "w_value": w_value, "w_out": w_out, "key_blocks": key_blocks}


def rms_rows(rows):
    values = rows.astype(jnp.float32)
    power = lax.optimization_barrier(jnp.mean(values * values, axis=-1, keepdims=True))
    return (values * lax.rsqrt(power + 1e-05)).astype(jnp.bfloat16)

def reference(frames, w_query, w_key, w_value, w_out, key_blocks):
    normed = rms_rows(frames)
    query = jnp.dot(normed, w_query, preferred_element_type=jnp.float32).astype(jnp.bfloat16)
    key = jnp.dot(normed, w_key, preferred_element_type=jnp.float32).astype(jnp.bfloat16)
    value = jnp.dot(normed, w_value, preferred_element_type=jnp.float32).astype(jnp.bfloat16)
    query_blocks = query.reshape(QBLOCKS, BLOCK, HEADS, HDIM)
    key_table = key.reshape(QBLOCKS, BLOCK, HEADS, HDIM)
    value_table = value.reshape(QBLOCKS, BLOCK, HEADS, HDIM)
    scale = HDIM ** (-0.5)

    def attend(items):
        query_per_block, listed = items
        usable = listed >= 0
        selected_blocks = jnp.where(usable, listed, 0).astype(jnp.int32)
        keys_here = key_table[selected_blocks].astype(jnp.float32)
        values_here = value_table[selected_blocks].astype(jnp.float32)
        logit_matrix = jnp.einsum('qhd,kbhd->hqkb', query_per_block.astype(jnp.float32), keys_here) * scale
        logit_matrix = jnp.where(usable[None, None, :, None], logit_matrix, -1e+30)
        largest = lax.optimization_barrier(jnp.max(logit_matrix, axis=(2, 3), keepdims=True))
        weights = jnp.exp(logit_matrix - largest)
        total = lax.optimization_barrier(jnp.sum(weights, axis=(2, 3)))
        rounded = weights.astype(jnp.bfloat16).astype(jnp.float32)
        summed = jnp.einsum('hqkb,kbhd->qhd', rounded, values_here)
        attention_output = summed / jnp.transpose(total)[:, :, None]
        return attention_output.astype(jnp.bfloat16).reshape(BLOCK, D)
    attended = lax.map(attend, (query_blocks, key_blocks)).reshape(FRAMES, D)
    return jnp.dot(attended, w_out, preferred_element_type=jnp.float32).astype(jnp.bfloat16)
```

```python
import jax
import jax.numpy as jnp
from jax import lax
from jax.experimental import pallas as pl
from jax.experimental.pallas import tpu as pltpu
from jax.sharding import PartitionSpec as P

HDIM = 64
BLOCK = 128
GROUP = 4
ROW = 4
LOG2E = 1.4426950408889634


def x_ring(peers, by):
    return [(i, (i // ROW) * ROW + (i % ROW + by) % ROW) for i in range(peers)]


def z_next(peers, keep=None):
    return [
        (i, i + ROW)
        for i in range(peers - ROW)
        if keep is None or (i % ROW - keep) % ROW != 0
    ]


def tp_swap(x, mask):
    return lax.ppermute(x, "tp", [(i, i ^ mask) for i in range(4)])


def after(x, *others):
    return lax.optimization_barrier((x, *others))[0]


def rms_rows(rows):
    values = rows.astype(jnp.float32)
    power = jnp.mean(values * values, axis=-1, keepdims=True)
    return (values * lax.rsqrt(power + 1e-05)).astype(jnp.bfloat16)


def spread(place, own, core, across, diag):
    width = own.shape[1] // ROW

    def kernel(place_ref, own_ref, core_ref, across_ref, diag_ref, *rest):
        outs, sems = rest[:ROW], rest[ROW]
        frame = place_ref[0]
        part = place_ref[1]
        x = place_ref[2]
        copies = []
        for k in range(ROW):
            cols = pl.ds(pl.multiple_of(lax.rem(x + k, ROW) * width, width), width)
            for j in range(4):
                for b in range(2):
                    if j < 2:
                        rows = pl.ds(pl.multiple_of(b * BLOCK + frame, 32), 32)
                        src = (own_ref, core_ref)[j].at[rows, cols]
                    else:
                        rows = pl.ds(pl.multiple_of(part + b * 64, 32), 32)
                        src = (across_ref, diag_ref)[j - 2].at[rows, cols]
                    slot = j * 2 + b
                    copy = pltpu.make_async_copy(
                        src, outs[k].at[slot], sems.at[k * 8 + slot]
                    )
                    copy.start()
                    copies.append(copy)
        for copy in copies:
            copy.wait()

    any_spec = pl.BlockSpec(memory_space=pl.ANY)
    return pl.pallas_call(
        kernel,
        grid_spec=pltpu.PrefetchScalarGridSpec(
            num_scalar_prefetch=1,
            grid=(1,),
            in_specs=[any_spec] * 4,
            out_specs=[any_spec] * ROW,
            scratch_shapes=[pltpu.SemaphoreType.DMA((ROW * 8,))],
        ),
        out_shape=[jax.ShapeDtypeStruct((8, 32, width), own.dtype)] * ROW,
        name="spread",
    )(place, own, core, across, diag)


def pick(which, index, pieces):
    width = pieces[0].shape[2]
    count = len(pieces)

    def kernel(which_ref, index_ref, *rest):
        ins, outs, sems = rest[:count], rest[count : count + ROW], rest[count + ROW]
        for k in range(ROW):
            for i in range(6):
                n = k * 6 + i
                for a in range(count):

                    @pl.when(which_ref[n] == a)
                    def _():
                        pltpu.make_async_copy(
                            ins[a].at[index_ref[n]], outs[k].at[i], sems.at[n]
                        ).start()

        for k in range(ROW):
            for i in range(6):
                n = k * 6 + i
                pltpu.make_async_copy(ins[0].at[0], outs[k].at[i], sems.at[n]).wait()

    any_spec = pl.BlockSpec(memory_space=pl.ANY)
    return pl.pallas_call(
        kernel,
        grid_spec=pltpu.PrefetchScalarGridSpec(
            num_scalar_prefetch=2,
            grid=(1,),
            in_specs=[any_spec] * count,
            out_specs=[any_spec] * ROW,
            scratch_shapes=[pltpu.SemaphoreType.DMA((ROW * 6,))],
        ),
        out_shape=[jax.ShapeDtypeStruct((6, 32, width), pieces[0].dtype)] * ROW,
        name="pick",
    )(which, index, *pieces)


def attention(info, q, k, v, kn, vn, km, vm):
    rows, width = q.shape
    keys = 1024
    pair = 2 * HDIM

    def kernel(info_ref, q_ref, k_ref, v_ref, kn_ref, vn_ref, km_ref, vm_ref, o_ref, kc, vc):
        @pl.when(pl.program_id(0) == 0)
        def _():
            vc[:, pair:] = jnp.ones((keys, pair), jnp.bfloat16)

        for part in range(4):
            kc[part * 96 : part * 96 + 96] = km_ref[part, 0]
            vc[part * 96 : part * 96 + 96, :pair] = vm_ref[part, 0]
        kc[384:512] = kn_ref[...]
        vc[384:512, :pair] = vn_ref[...]
        kc[512:] = k_ref[...]
        vc[512:, :pair] = v_ref[...]
        lane = lax.broadcasted_iota(jnp.int32, (1, pair), 1)
        key = lax.broadcasted_iota(jnp.int32, (1, keys), 1)
        slot = lax.rem(lax.div(key, 32), 3)
        listed = jnp.where(
            key < 384,
            jnp.where(
                slot == 0,
                info_ref[1],
                jnp.where(slot == 1, info_ref[2], info_ref[3]),
            ),
            1,
        )
        for b in range(GROUP):
            here = jnp.where((key >= 384) & (key < 512), info_ref[4 + b], listed) > 0
            qb = q_ref[b * BLOCK : (b + 1) * BLOCK]
            results = []
            for h in range(2):
                mine = (lane < HDIM) if h == 0 else (lane >= HDIM)
                qh = jnp.where(mine, qb, jnp.zeros_like(qb))
                s = lax.dot_general(
                    qh, kc[...], (((1,), (1,)), ((), ())), preferred_element_type=jnp.float32
                )
                s = jnp.where(here, s, -1e30)
                m = jnp.max(s, axis=1, keepdims=True)
                p = jnp.exp2(s - m).astype(jnp.bfloat16)
                o = jnp.dot(p, vc[...], preferred_element_type=jnp.float32)
                results.append(o[:, :pair] / o[:, pair:])
            o_ref[b * BLOCK : (b + 1) * BLOCK] = jnp.where(
                lane < HDIM, results[0], results[1]
            ).astype(jnp.bfloat16)

    col = lambda h, info: (0, h)
    mem = lambda h, info: (0, info[0], 0, h)
    return pl.pallas_call(
        kernel,
        grid_spec=pltpu.PrefetchScalarGridSpec(
            num_scalar_prefetch=1,
            grid=(width // pair,),
            in_specs=[
                pl.BlockSpec((rows, pair), col),
                pl.BlockSpec((rows, pair), col),
                pl.BlockSpec((rows, pair), col),
                pl.BlockSpec((BLOCK, pair), col),
                pl.BlockSpec((BLOCK, pair), col),
                pl.BlockSpec((4, 1, 96, pair), mem),
                pl.BlockSpec((4, 1, 96, pair), mem),
            ],
            out_specs=pl.BlockSpec((rows, pair), col),
            scratch_shapes=[
                pltpu.VMEM((keys, pair), jnp.bfloat16),
                pltpu.VMEM((keys, 2 * pair), jnp.bfloat16),
            ],
        ),
        out_shape=jax.ShapeDtypeStruct((rows, width), jnp.bfloat16),
        cost_estimate=pl.CostEstimate(
            flops=rows * keys * width * 16, bytes_accessed=4 << 20, transcendentals=0
        ),
        compiler_params=pltpu.CompilerParams(vmem_limit_bytes=40 << 20),
        name="attention",
    )(info, q, k, v, kn, vn, km, vm)


def shards(frames, w_query, w_key, w_value, w_out, key_blocks):
    peers = lax.axis_size("seq")
    s = lax.axis_index("seq").astype(jnp.int32)
    t = lax.axis_index("tp").astype(jnp.int32)
    y, c, x, row = t // 2, t % 2, s % ROW, s // ROW
    scale = HDIM ** (-0.5) * LOG2E

    def project(normed, weight, by=None):
        out = jnp.dot(normed, weight, preferred_element_type=jnp.float32)
        return (out if by is None else out * by).astype(jnp.bfloat16)

    b0 = s * 8 + jnp.arange(2, dtype=jnp.int32)[:, None] * GROUP
    lists = key_blocks.reshape(2, GROUP, 8)
    first = lists[:, 0]
    valid = (first >= 0) & (first < b0)
    rank = jnp.cumsum(valid.astype(jnp.int32), axis=1) - 1
    slots = jnp.stack(
        [jnp.sum(jnp.where(valid & (rank == i), first + 1, 0), axis=1) for i in range(3)], axis=1
    ) - 1
    with_next = jnp.any(lists == (b0 + GROUP)[:, :, None], axis=2).astype(jnp.int32)
    info = jnp.concatenate(
        [jnp.arange(2, dtype=jnp.int32)[:, None], (slots >= 0).astype(jnp.int32), with_next], axis=1
    )
    tables = [slots.reshape(6)] + [
        lax.ppermute(slots, "seq", x_ring(peers, -k)).reshape(6) for k in range(1, ROW)
    ]
    wanted = jnp.concatenate(tables)
    used = wanted >= 0
    which = jnp.where(used, (row - wanted // 32) * ROW + (x - wanted // 8 % ROW) % ROW, 0)
    index = jnp.where(used, ((wanted % 8 // 2) ^ t) * 2 + wanted % 2, 0)

    halves = frames.reshape(2, 2, 64, -1)
    depth = frames.shape[1]
    core = tp_swap(frames, 1)
    across_a = tp_swap(
        lax.dynamic_index_in_dim(halves, 1 - y, 1, keepdims=False).reshape(128, depth), 2
    )
    diag_a = tp_swap(across_a, 1)
    rest = lax.dynamic_index_in_dim(halves, y, 1, keepdims=False).reshape(128, depth)
    across_b = tp_swap(after(rest, across_a), 2)
    diag_b = tp_swap(across_b, 1)

    place = jnp.stack([y * 64 + c * 32, c * 32, x])
    pieces = spread(place, frames, core, across_a, diag_a)
    row0 = [pieces[0]] + [lax.ppermute(pieces[k], "seq", x_ring(peers, k)) for k in (1, 2, 3)]
    row1 = [lax.ppermute(p, "seq", z_next(peers)) for p in row0]
    row2 = [lax.ppermute(p, "seq", z_next(peers, k)) for k, p in enumerate(row1)]
    chosen = pick(which, index, row0 + row1 + row2)
    back = [chosen[0]] + [lax.ppermute(chosen[k], "seq", x_ring(peers, k)) for k in (1, 2, 3)]
    back_y = [tp_swap(p, 2) for p in back]
    back_c = [tp_swap(p, 1) for p in back]
    back_d = [tp_swap(p, 1) for p in back_y]
    memory = jnp.concatenate(
        [
            jnp.concatenate([p.reshape(192, -1) for p in group], axis=1)
            for group in (back, back_c, back_y, back_d)
        ],
        axis=0,
    )

    def rolled(weight):
        parts = weight.reshape(ROW, -1, weight.shape[1])
        return jnp.concatenate(
            [lax.dynamic_index_in_dim(parts, (x - k) % ROW, 0, keepdims=False) for k in range(ROW)],
            axis=0,
        )

    roll_key, roll_value = rolled(w_key), rolled(w_value)
    memory = rms_rows(memory)
    mem_key = project(memory, roll_key).reshape(4, 2, 96, -1)
    mem_value = project(memory, roll_value).reshape(4, 2, 96, -1)

    def natural(a, b):
        a, b = a.reshape(2, 1, 64, depth), b.reshape(2, 1, 64, depth)
        low, high = jnp.where(y == 0, a, b), jnp.where(y == 0, b, a)
        return jnp.concatenate([low, high], axis=1).reshape(256, depth)

    near = rms_rows(jnp.concatenate([frames, core], axis=0))
    far = rms_rows(
        jnp.concatenate([natural(across_a, across_b), natural(diag_a, diag_b)], axis=0)
    )
    q_near, k_near, v_near = (
        project(near, w_query, scale),
        project(near, w_key),
        project(near, w_value),
    )
    q_far, k_far, v_far = (
        project(far, w_query, scale),
        project(far, w_key),
        project(far, w_value),
    )

    def block_at(near_part, far_part, pair_index):
        both = jnp.stack([near_part.reshape(2, 256, -1), far_part.reshape(2, 256, -1)])
        both = both.reshape(4, 256, -1)[:, :BLOCK]
        return lax.dynamic_index_in_dim(both, pair_index ^ t, 0, keepdims=False)

    head = jnp.concatenate([block_at(k_near, k_far, 0), block_at(v_near, v_far, 0)], axis=1)
    following = lax.ppermute(head, "seq", [(i, i - 1) for i in range(1, peers)])
    middle = jnp.concatenate([block_at(k_near, k_far, 2), block_at(v_near, v_far, 2)], axis=1)
    next_far = jnp.where(y == 0, following, middle)
    next_near = jnp.where(y == 0, middle, following)
    width = k_near.shape[1]

    info_far = lax.dynamic_index_in_dim(info, 1 - y, 0, keepdims=False)
    info_near = lax.dynamic_index_in_dim(info, y, 0, keepdims=False)
    att_far = attention(
        info_far, q_far, k_far, v_far, next_far[:, :width], next_far[:, width:], mem_key, mem_value
    )

    def mix(rows):
        return jnp.dot(rows, w_out, preferred_element_type=jnp.float32)

    far_other = tp_swap(mix(att_far[256:]).astype(jnp.bfloat16), 1)
    far_sum = (mix(att_far[:256]) + far_other.astype(jnp.float32)).astype(jnp.bfloat16)
    from_far = tp_swap(far_sum, 2)
    att_near = attention(
        info_near,
        q_near,
        k_near,
        v_near,
        next_near[:, :width],
        next_near[:, width:],
        mem_key,
        mem_value,
    )
    near_other = tp_swap(mix(att_near[256:]).astype(jnp.bfloat16), 1)
    total = mix(att_near[:256]) + near_other.astype(jnp.float32) + from_far.astype(jnp.float32)
    return total.astype(jnp.bfloat16)


def solution(mesh):
    return jax.shard_map(
        shards,
        mesh=mesh,
        in_specs=(
            P(("seq", "tp"), None),
            P(None, "tp"),
            P(None, "tp"),
            P(None, "tp"),
            P("tp", None),
            P("seq", None),
        ),
        out_specs=P(("seq", "tp"), None),
        check_vma=False,
    )
```

```python
import jax
import jax.numpy as jnp
from jax import lax
from jax.experimental import pallas as pl
from jax.experimental.pallas import tpu as pltpu
from jax.sharding import PartitionSpec as P

HDIM = 64
BLOCK = 128
GROUP = 4
ROW = 4
LOG2E = 1.4426950408889634


def x_ring(peers, by):
    return [(i, (i // ROW) * ROW + (i % ROW + by) % ROW) for i in range(peers)]


def z_next(peers, keep=None):
    return [
        (i, i + ROW)
        for i in range(peers - ROW)
        if keep is None or (i % ROW - keep) % ROW != 0
    ]


def tp_swap(x, mask):
    return lax.ppermute(x, "tp", [(i, i ^ mask) for i in range(4)])


def after(x, *others):
    return lax.optimization_barrier((x, *others))[0]


def rms_rows(rows):
    values = rows.astype(jnp.float32)
    power = jnp.mean(values * values, axis=-1, keepdims=True)
    return (values * lax.rsqrt(power + 1e-05)).astype(jnp.bfloat16)


def spread(place, own, core, across, diag):
    width = own.shape[1] // ROW

    def kernel(place_ref, own_ref, core_ref, across_ref, diag_ref, *outs):
        frame = place_ref[0]
        part = place_ref[1]
        x = place_ref[2]
        for k in range(ROW):
            cols = pl.ds(pl.multiple_of(lax.rem(x + k, ROW) * width, width), width)
            for j, ref in enumerate((own_ref, core_ref, across_ref, diag_ref)):
                for b in range(2):
                    start = b * BLOCK + frame if j < 2 else b * 64 + part
                    rows = pl.ds(pl.multiple_of(start, 32), 32)
                    outs[k][j * 2 + b] = ref[rows, cols]

    vmem = pl.BlockSpec(memory_space=pltpu.VMEM)
    return pl.pallas_call(
        kernel,
        in_specs=[pl.BlockSpec(memory_space=pltpu.SMEM)] + [vmem] * 4,
        out_specs=[vmem] * ROW,
        out_shape=[jax.ShapeDtypeStruct((8, 32, width), own.dtype)] * ROW,
        compiler_params=pltpu.CompilerParams(vmem_limit_bytes=24 << 20),
        name="spread",
    )(place, own, core, across, diag)


def pick(which, index, pieces):
    width = pieces[0].shape[2]
    count = len(pieces)

    def kernel(which_ref, index_ref, *rest):
        ins, outs = rest[:count], rest[count : count + ROW]
        held, sems = rest[count + ROW :]
        copies = [pltpu.make_async_copy(ins[a], held.at[a], sems.at[a]) for a in range(count)]
        for copy in copies:
            copy.start()
        for copy in copies:
            copy.wait()
        for k in range(ROW):
            for i in range(6):
                n = k * 6 + i
                outs[k][i] = held[which_ref[n], index_ref[n]]

    smem = pl.BlockSpec(memory_space=pltpu.SMEM)
    return pl.pallas_call(
        kernel,
        in_specs=[smem] * 2 + [pl.BlockSpec(memory_space=pl.ANY)] * count,
        out_specs=[pl.BlockSpec(memory_space=pltpu.VMEM)] * ROW,
        out_shape=[jax.ShapeDtypeStruct((6, 32, width), pieces[0].dtype)] * ROW,
        scratch_shapes=[
            pltpu.VMEM((count, 8, 32, width), pieces[0].dtype),
            pltpu.SemaphoreType.DMA((count,)),
        ],
        compiler_params=pltpu.CompilerParams(vmem_limit_bytes=24 << 20),
        name="pick",
    )(which, index, *pieces)


def memory_project(x, groups, w_key, w_value):
    rows, part = groups[0][0].shape
    width = w_key.shape[1]

    def kernel(x_ref, *rest):
        pieces, (wk, wv, ok, ov) = rest[:16], rest[16:]
        for g in range(4):
            power = jnp.zeros((rows, 1), jnp.float32)
            key = jnp.zeros((rows, width), jnp.float32)
            value = jnp.zeros((rows, width), jnp.float32)
            for k in range(ROW):
                piece = pieces[g * ROW + k][...]
                wide = piece.astype(jnp.float32)
                power += jnp.sum(wide * wide, axis=1, keepdims=True)
                depth = pl.ds(pl.multiple_of(lax.rem(x_ref[0] - k + ROW, ROW) * part, part), part)
                key += jnp.dot(piece, wk[depth], preferred_element_type=jnp.float32)
                value += jnp.dot(piece, wv[depth], preferred_element_type=jnp.float32)
            factor = lax.rsqrt(power / (part * ROW) + 1e-05)
            ok[g] = (key * factor).astype(jnp.bfloat16)
            ov[g] = (value * factor).astype(jnp.bfloat16)

    vmem = pl.BlockSpec(memory_space=pltpu.VMEM)
    return pl.pallas_call(
        kernel,
        in_specs=[pl.BlockSpec(memory_space=pltpu.SMEM)] + [vmem] * 18,
        out_specs=[vmem] * 2,
        out_shape=[jax.ShapeDtypeStruct((4, rows, width), jnp.bfloat16)] * 2,
        cost_estimate=pl.CostEstimate(
            flops=16 * rows * part * width * 4, bytes_accessed=8 << 20, transcendentals=0
        ),
        compiler_params=pltpu.CompilerParams(vmem_limit_bytes=40 << 20),
        name="memory_project",
    )(x, *[p for group in groups for p in group], w_key, w_value)


def attention(info, q, k, v, kn, vn, km, vm):
    rows, width = q.shape
    keys = 1024
    pair = 2 * HDIM

    def kernel(info_ref, q_ref, k_ref, v_ref, kn_ref, vn_ref, km_ref, vm_ref, o_ref, kc, vc):
        @pl.when(pl.program_id(0) == 0)
        def _():
            vc[:, pair:] = jnp.ones((keys, pair), jnp.bfloat16)

        for part in range(4):
            kc[part * 96 : part * 96 + 96] = km_ref[part, 0]
            vc[part * 96 : part * 96 + 96, :pair] = vm_ref[part, 0]
        kc[384:512] = kn_ref[...]
        vc[384:512, :pair] = vn_ref[...]
        kc[512:] = k_ref[...]
        vc[512:, :pair] = v_ref[...]
        lane = lax.broadcasted_iota(jnp.int32, (1, pair), 1)
        key = lax.broadcasted_iota(jnp.int32, (1, keys), 1)
        slot = lax.rem(lax.div(key, 32), 3)
        listed = jnp.where(
            key < 384,
            jnp.where(
                slot == 0,
                info_ref[1],
                jnp.where(slot == 1, info_ref[2], info_ref[3]),
            ),
            1,
        )
        for b in range(GROUP):
            here = jnp.where((key >= 384) & (key < 512), info_ref[4 + b], listed) > 0
            qb = q_ref[b * BLOCK : (b + 1) * BLOCK]
            results = []
            for h in range(2):
                mine = (lane < HDIM) if h == 0 else (lane >= HDIM)
                qh = jnp.where(mine, qb, jnp.zeros_like(qb))
                s = lax.dot_general(
                    qh, kc[...], (((1,), (1,)), ((), ())), preferred_element_type=jnp.float32
                )
                s = jnp.where(here, s, -1e30)
                m = jnp.max(s, axis=1, keepdims=True)
                p = jnp.exp2(s - m).astype(jnp.bfloat16)
                o = jnp.dot(p, vc[...], preferred_element_type=jnp.float32)
                results.append(o[:, :pair] / o[:, pair:])
            o_ref[b * BLOCK : (b + 1) * BLOCK] = jnp.where(
                lane < HDIM, results[0], results[1]
            ).astype(jnp.bfloat16)

    col = lambda h, info: (0, h)
    mem = lambda h, info: (0, info[0], 0, h)
    return pl.pallas_call(
        kernel,
        grid_spec=pltpu.PrefetchScalarGridSpec(
            num_scalar_prefetch=1,
            grid=(width // pair,),
            in_specs=[
                pl.BlockSpec((rows, pair), col),
                pl.BlockSpec((rows, pair), col),
                pl.BlockSpec((rows, pair), col),
                pl.BlockSpec((BLOCK, pair), col),
                pl.BlockSpec((BLOCK, pair), col),
                pl.BlockSpec((4, 1, 96, pair), mem),
                pl.BlockSpec((4, 1, 96, pair), mem),
            ],
            out_specs=pl.BlockSpec((rows, pair), col),
            scratch_shapes=[
                pltpu.VMEM((keys, pair), jnp.bfloat16),
                pltpu.VMEM((keys, 2 * pair), jnp.bfloat16),
            ],
        ),
        out_shape=jax.ShapeDtypeStruct((rows, width), jnp.bfloat16),
        cost_estimate=pl.CostEstimate(
            flops=rows * keys * width * 16, bytes_accessed=4 << 20, transcendentals=0
        ),
        compiler_params=pltpu.CompilerParams(vmem_limit_bytes=40 << 20),
        name="attention",
    )(info, q, k, v, kn, vn, km, vm)


def shards(frames, w_query, w_key, w_value, w_out, key_blocks):
    peers = lax.axis_size("seq")
    s = lax.axis_index("seq").astype(jnp.int32)
    t = lax.axis_index("tp").astype(jnp.int32)
    y, c, x, row = t // 2, t % 2, s % ROW, s // ROW
    scale = HDIM ** (-0.5) * LOG2E

    def project(normed, weight, by=None):
        out = jnp.dot(normed, weight, preferred_element_type=jnp.float32)
        return (out if by is None else out * by).astype(jnp.bfloat16)

    b0 = s * 8 + jnp.arange(2, dtype=jnp.int32)[:, None] * GROUP
    lists = key_blocks.reshape(2, GROUP, 8)
    first = lists[:, 0]
    valid = (first >= 0) & (first < b0)
    rank = jnp.cumsum(valid.astype(jnp.int32), axis=1) - 1
    slots = jnp.stack(
        [jnp.sum(jnp.where(valid & (rank == i), first + 1, 0), axis=1) for i in range(3)], axis=1
    ) - 1
    with_next = jnp.any(lists == (b0 + GROUP)[:, :, None], axis=2).astype(jnp.int32)
    info = jnp.concatenate(
        [jnp.arange(2, dtype=jnp.int32)[:, None], (slots >= 0).astype(jnp.int32), with_next], axis=1
    )
    tables = [slots.reshape(6)] + [
        lax.ppermute(slots, "seq", x_ring(peers, -k)).reshape(6) for k in range(1, ROW)
    ]
    wanted = jnp.concatenate(tables)
    used = wanted >= 0
    which = jnp.where(used, (row - wanted // 32) * ROW + (x - wanted // 8 % ROW) % ROW, 0)
    index = jnp.where(used, ((wanted % 8 // 2) ^ t) * 2 + wanted % 2, 0)

    halves = frames.reshape(2, 2, 64, -1)
    depth = frames.shape[1]
    core = tp_swap(frames, 1)
    across_a = tp_swap(
        lax.dynamic_index_in_dim(halves, 1 - y, 1, keepdims=False).reshape(128, depth), 2
    )
    diag_a = tp_swap(across_a, 1)
    rest = lax.dynamic_index_in_dim(halves, y, 1, keepdims=False).reshape(128, depth)
    across_b = tp_swap(after(rest, across_a), 2)
    diag_b = tp_swap(across_b, 1)

    place = jnp.stack([y * 64 + c * 32, c * 32, x])
    pieces = spread(place, frames, core, across_a, diag_a)
    row0 = [pieces[0]] + [lax.ppermute(pieces[k], "seq", x_ring(peers, k)) for k in (1, 2, 3)]
    row1 = [lax.ppermute(p, "seq", z_next(peers)) for p in row0]
    row2 = [lax.ppermute(p, "seq", z_next(peers, k)) for k, p in enumerate(row1)]
    chosen = pick(which, index, row0 + row1 + row2)
    back = [chosen[0]] + [lax.ppermute(chosen[k], "seq", x_ring(peers, k)) for k in (1, 2, 3)]
    back_y = [tp_swap(p, 2) for p in back]
    back_c = [tp_swap(p, 1) for p in back]
    back_d = [tp_swap(p, 1) for p in back_y]
    flat = [[p.reshape(192, -1) for p in group] for group in (back, back_c, back_y, back_d)]
    mem_key, mem_value = memory_project(x.reshape(1), flat, w_key, w_value)
    mem_key, mem_value = mem_key.reshape(4, 2, 96, -1), mem_value.reshape(4, 2, 96, -1)

    def natural(a, b):
        a, b = a.reshape(2, 1, 64, depth), b.reshape(2, 1, 64, depth)
        low, high = jnp.where(y == 0, a, b), jnp.where(y == 0, b, a)
        return jnp.concatenate([low, high], axis=1).reshape(256, depth)

    near = rms_rows(jnp.concatenate([frames, core], axis=0))
    far = rms_rows(
        jnp.concatenate([natural(across_a, across_b), natural(diag_a, diag_b)], axis=0)
    )
    q_near, k_near, v_near = (
        project(near, w_query, scale),
        project(near, w_key),
        project(near, w_value),
    )
    q_far, k_far, v_far = (
        project(far, w_query, scale),
        project(far, w_key),
        project(far, w_value),
    )

    def block_at(near_part, far_part, pair_index):
        both = jnp.stack([near_part.reshape(2, 256, -1), far_part.reshape(2, 256, -1)])
        both = both.reshape(4, 256, -1)[:, :BLOCK]
        return lax.dynamic_index_in_dim(both, pair_index ^ t, 0, keepdims=False)

    head = jnp.concatenate([block_at(k_near, k_far, 0), block_at(v_near, v_far, 0)], axis=1)
    following = lax.ppermute(head, "seq", [(i, i - 1) for i in range(1, peers)])
    middle = jnp.concatenate([block_at(k_near, k_far, 2), block_at(v_near, v_far, 2)], axis=1)
    next_far = jnp.where(y == 0, following, middle)
    next_near = jnp.where(y == 0, middle, following)
    width = k_near.shape[1]

    info_far = lax.dynamic_index_in_dim(info, 1 - y, 0, keepdims=False)
    info_near = lax.dynamic_index_in_dim(info, y, 0, keepdims=False)
    att_far = attention(
        info_far, q_far, k_far, v_far, next_far[:, :width], next_far[:, width:], mem_key, mem_value
    )

    def mix(rows):
        return jnp.dot(rows, w_out, preferred_element_type=jnp.float32)

    far_other = tp_swap(mix(att_far[256:]).astype(jnp.bfloat16), 1)
    far_sum = (mix(att_far[:256]) + far_other.astype(jnp.float32)).astype(jnp.bfloat16)
    from_far = tp_swap(far_sum, 2)
    att_near = attention(
        info_near,
        after(q_near, far_sum),
        k_near,
        v_near,
        next_near[:, :width],
        next_near[:, width:],
        mem_key,
        mem_value,
    )
    near_other = tp_swap(mix(att_near[256:]).astype(jnp.bfloat16), 1)
    total = mix(att_near[:256]) + near_other.astype(jnp.float32) + from_far.astype(jnp.float32)
    return total.astype(jnp.bfloat16)


def solution(mesh):
    return jax.shard_map(
        shards,
        mesh=mesh,
        in_specs=(
            P(("seq", "tp"), None),
            P(None, "tp"),
            P(None, "tp"),
            P(None, "tp"),
            P("tp", None),
            P("seq", None),
        ),
        out_specs=P(("seq", "tp"), None),
        check_vma=False,
    )
```

```python
import jax
import jax.numpy as jnp
from jax import lax
from jax.experimental import pallas as pl
from jax.experimental.pallas import tpu as pltpu
from jax.sharding import PartitionSpec as P

HDIM = 64
BLOCK = 128
GROUP = 4
ROW = 4
LOG2E = 1.4426950408889634


def x_ring(peers, by):
    return [(i, (i // ROW) * ROW + (i % ROW + by) % ROW) for i in range(peers)]


def z_next(peers, keep=None):
    return [
        (i, i + ROW)
        for i in range(peers - ROW)
        if keep is None or (i % ROW - keep) % ROW != 0
    ]


def tp_swap(x, mask):
    return lax.ppermute(x, "tp", [(i, i ^ mask) for i in range(4)])


def after(x, *others):
    return lax.optimization_barrier((x, *others))[0]


def rms_rows(rows):
    values = rows.astype(jnp.float32)
    power = jnp.mean(values * values, axis=-1, keepdims=True)
    return (values * lax.rsqrt(power + 1e-05)).astype(jnp.bfloat16)


def spread(place, own, core, across, diag):
    width = own.shape[1] // ROW

    def kernel(place_ref, own_ref, core_ref, across_ref, diag_ref, *outs):
        frame = place_ref[0]
        part = place_ref[1]
        x = place_ref[2]
        for k in range(ROW):
            cols = pl.ds(pl.multiple_of(lax.rem(x + k, ROW) * width, width), width)
            for j, ref in enumerate((own_ref, core_ref, across_ref, diag_ref)):
                for b in range(2):
                    start = b * BLOCK + frame if j < 2 else b * 64 + part
                    rows = pl.ds(pl.multiple_of(start, 32), 32)
                    outs[k][j * 2 + b] = ref[rows, cols]

    vmem = pl.BlockSpec(memory_space=pltpu.VMEM)
    return pl.pallas_call(
        kernel,
        in_specs=[pl.BlockSpec(memory_space=pltpu.SMEM)] + [vmem] * 4,
        out_specs=[vmem] * ROW,
        out_shape=[jax.ShapeDtypeStruct((8, 32, width), own.dtype)] * ROW,
        compiler_params=pltpu.CompilerParams(vmem_limit_bytes=24 << 20),
        name="spread",
    )(place, own, core, across, diag)


def pick(which, index, pieces):
    width = pieces[0].shape[2]
    count = len(pieces)

    def kernel(which_ref, index_ref, *rest):
        ins, outs = rest[:count], rest[count : count + 2 * ROW]
        held, sems = rest[count + 2 * ROW :]
        copies = [pltpu.make_async_copy(ins[a], held.at[a], sems.at[a]) for a in range(count)]
        for copy in copies:
            copy.start()
        for copy in copies:
            copy.wait()
        for k in range(ROW):
            for i in range(6):
                n = k * 6 + i
                outs[i // 3 * ROW + k][i % 3] = held[which_ref[n], index_ref[n]]

    smem = pl.BlockSpec(memory_space=pltpu.SMEM)
    outs = pl.pallas_call(
        kernel,
        in_specs=[smem] * 2 + [pl.BlockSpec(memory_space=pl.ANY)] * count,
        out_specs=[pl.BlockSpec(memory_space=pltpu.VMEM)] * (2 * ROW),
        out_shape=[jax.ShapeDtypeStruct((3, 32, width), pieces[0].dtype)] * (2 * ROW),
        scratch_shapes=[
            pltpu.VMEM((count, 8, 32, width), pieces[0].dtype),
            pltpu.SemaphoreType.DMA((count,)),
        ],
        compiler_params=pltpu.CompilerParams(vmem_limit_bytes=24 << 20),
        name="pick",
    )(which, index, *pieces)
    return outs[:ROW], outs[ROW:]


def memory_project(x, groups, w_key, w_value):
    rows, depth = groups[0].shape
    part = depth // ROW
    width = w_key.shape[1]

    def kernel(x_ref, *rest):
        pieces, (wk, wv, ok, ov) = rest[:4], rest[4:]
        held = [ref[...] for ref in pieces]
        power = [
            jnp.sum(jnp.square(h.astype(jnp.float32)), axis=1, keepdims=True) for h in held
        ]
        factor = lax.rsqrt(jnp.concatenate(power, axis=0) / depth + 1e-05)
        key = jnp.zeros((4 * rows, width), jnp.float32)
        value = jnp.zeros((4 * rows, width), jnp.float32)
        for k in range(ROW):
            piece = jnp.concatenate([h[:, k * part : (k + 1) * part] for h in held], axis=0)
            at = pl.ds(pl.multiple_of(lax.rem(x_ref[0] - k + ROW, ROW) * part, part), part)
            key += jnp.dot(piece, wk[at], preferred_element_type=jnp.float32)
            value += jnp.dot(piece, wv[at], preferred_element_type=jnp.float32)
        ok[...] = (key * factor).astype(jnp.bfloat16)
        ov[...] = (value * factor).astype(jnp.bfloat16)

    vmem = pl.BlockSpec(memory_space=pltpu.VMEM)
    return pl.pallas_call(
        kernel,
        in_specs=[pl.BlockSpec(memory_space=pltpu.SMEM)] + [vmem] * 6,
        out_specs=[vmem] * 2,
        out_shape=[jax.ShapeDtypeStruct((4 * rows, width), jnp.bfloat16)] * 2,
        cost_estimate=pl.CostEstimate(
            flops=16 * rows * depth * width, bytes_accessed=6 << 20, transcendentals=0
        ),
        compiler_params=pltpu.CompilerParams(vmem_limit_bytes=40 << 20),
        name="memory_project",
    )(x, *groups, w_key, w_value)


def attention(info, half, q, k, v, kn, vn, km, vm):
    rows, width = q.shape[0] // 2, q.shape[1]
    keys = 1024
    pair = 2 * HDIM

    def kernel(info_ref, q_ref, k_ref, v_ref, kn_ref, vn_ref, km_ref, vm_ref, o_ref, kc, vc):
        @pl.when(pl.program_id(0) == 0)
        def _():
            vc[:, pair:] = jnp.ones((keys, pair), jnp.bfloat16)

        kc[:384] = km_ref[...]
        vc[:384, :pair] = vm_ref[...]
        kc[384:512] = kn_ref[...]
        vc[384:512, :pair] = vn_ref[...]
        kc[512:] = k_ref[...]
        vc[512:, :pair] = v_ref[...]
        lane = lax.broadcasted_iota(jnp.int32, (1, pair), 1)
        key = lax.broadcasted_iota(jnp.int32, (1, 384), 1)
        slot = lax.rem(lax.div(key, 32), 3)
        listed = jnp.where(
            slot == 0, info_ref[0], jnp.where(slot == 1, info_ref[1], info_ref[2])
        )
        queries = lax.broadcasted_iota(jnp.int32, (2 * rows, 1), 0)
        follows = jnp.where(lax.rem(queries, rows) < BLOCK, info_ref[3], info_ref[4])
        held = q_ref[...]
        nothing = jnp.zeros_like(held)
        both = jnp.concatenate(
            [jnp.where(lane < HDIM, held, nothing), jnp.where(lane >= HDIM, held, nothing)], axis=0
        )
        s = lax.dot_general(
            both, kc[...], (((1,), (1,)), ((), ())), preferred_element_type=jnp.float32
        )
        s = jnp.concatenate(
            [
                jnp.where(listed > 0, s[:, :384], -1e30),
                jnp.where(follows > 0, s[:, 384:512], -1e30),
                s[:, 512:],
            ],
            axis=1,
        )
        m = jnp.max(s, axis=1, keepdims=True)
        p = jnp.exp2(s - m).astype(jnp.bfloat16)
        o = jnp.dot(p, vc[...], preferred_element_type=jnp.float32)
        o = o[:, :pair] / o[:, pair:]
        o_ref[...] = jnp.where(lane < HDIM, o[:rows], o[rows:]).astype(jnp.bfloat16)

    col = lambda h, info: (0, h)
    return pl.pallas_call(
        kernel,
        grid_spec=pltpu.PrefetchScalarGridSpec(
            num_scalar_prefetch=1,
            grid=(width // pair,),
            in_specs=[
                pl.BlockSpec((rows, pair), lambda h, info: (half, h)),
                pl.BlockSpec((2 * rows, pair), col),
                pl.BlockSpec((2 * rows, pair), col),
                pl.BlockSpec((BLOCK, pair), col),
                pl.BlockSpec((BLOCK, pair), col),
                pl.BlockSpec((384, pair), col),
                pl.BlockSpec((384, pair), col),
            ],
            out_specs=pl.BlockSpec((rows, pair), col),
            scratch_shapes=[
                pltpu.VMEM((keys, pair), jnp.bfloat16),
                pltpu.VMEM((keys, 2 * pair), jnp.bfloat16),
            ],
        ),
        out_shape=jax.ShapeDtypeStruct((rows, width), jnp.bfloat16),
        cost_estimate=pl.CostEstimate(flops=1 << 20, bytes_accessed=1 << 16, transcendentals=0),
        compiler_params=pltpu.CompilerParams(vmem_limit_bytes=40 << 20),
        name="attention",
    )(info, q, k, v, kn, vn, km, vm)


def shards(frames, w_query, w_key, w_value, w_out, key_blocks):
    peers = lax.axis_size("seq")
    s = lax.axis_index("seq").astype(jnp.int32)
    t = lax.axis_index("tp").astype(jnp.int32)
    y, c, x, row = t // 2, t % 2, s % ROW, s // ROW
    scale = HDIM ** (-0.5) * LOG2E
    depth = frames.shape[1]

    def project(normed, weight, by=None):
        out = jnp.dot(normed, weight, preferred_element_type=jnp.float32)
        return (out if by is None else out * by).astype(jnp.bfloat16)

    def by_chip(pair):
        return jnp.where(y == 0, pair, pair[::-1])

    halves = frames.reshape(2, 2, 64, depth)
    across_a = tp_swap(
        lax.dynamic_index_in_dim(halves, 1 - y, 1, keepdims=False).reshape(128, depth), 2
    )
    core = tp_swap(frames, 1)

    b0 = s * 8 + jnp.arange(2, dtype=jnp.int32)[:, None] * GROUP
    lists = key_blocks.reshape(2, GROUP, 8)
    first = lists[:, 0]
    valid = (first >= 0) & (first < b0)
    rank = jnp.cumsum(valid.astype(jnp.int32), axis=1) - 1
    slots = jnp.stack(
        [jnp.sum(jnp.where(valid & (rank == i), first + 1, 0), axis=1) for i in range(3)], axis=1
    ) - 1
    slots = by_chip(slots)
    with_next = jnp.any(lists == (b0 + GROUP)[:, :, None], axis=2).astype(jnp.int32)
    with_next = by_chip(with_next).reshape(2, 2, 2)
    with_next = jnp.where(c == 0, with_next, with_next[:, ::-1])
    listed = (slots >= 0).astype(jnp.int32)
    info = [[jnp.concatenate([listed[i], with_next[i, j]]) for j in range(2)] for i in range(2)]
    tables = [slots.reshape(6)] + [
        lax.ppermute(slots, "seq", x_ring(peers, -k)).reshape(6) for k in range(1, ROW)
    ]
    wanted = jnp.concatenate(tables)
    used = wanted >= 0
    which = jnp.where(used, (row - wanted // 32) * ROW + (x - wanted // 8 % ROW) % ROW, 0)
    index = jnp.where(used, ((wanted % 8 // 2) ^ t) * 2 + wanted % 2, 0)

    near = rms_rows(jnp.concatenate([frames, core], axis=0))
    q_near, k_near, v_near = (
        project(near, w_query, scale),
        project(near, w_key),
        project(near, w_value),
    )
    across_a, q_near, k_near, v_near, which, index = lax.optimization_barrier(
        (across_a, q_near, k_near, v_near, which, index)
    )
    diag_a = tp_swap(across_a, 1)
    rest = lax.dynamic_index_in_dim(halves, y, 1, keepdims=False).reshape(128, depth)
    across_b = tp_swap(after(rest, across_a), 2)
    diag_b = tp_swap(across_b, 1)

    place = jnp.stack([y * 64 + c * 32, c * 32, x])
    pieces = spread(place, frames, core, across_a, diag_a)
    row0 = [pieces[0]] + [lax.ppermute(pieces[k], "seq", x_ring(peers, k)) for k in (1, 2, 3)]
    row1 = [lax.ppermute(p, "seq", z_next(peers)) for p in row0]
    row2 = [lax.ppermute(p, "seq", z_next(peers, k)) for k, p in enumerate(row1)]
    chosen = pick(which, index, row0 + row1 + row2)

    def returned(parts):
        back = [parts[0]] + [lax.ppermute(parts[k], "seq", x_ring(peers, k)) for k in (1, 2, 3)]
        return jnp.concatenate([p.reshape(96, -1) for p in back], axis=1)

    here = [returned(parts) for parts in chosen]
    over = tp_swap(here[0], 2)
    over_late = tp_swap(here[1], 2)
    far_memory = [here[1], tp_swap(here[1], 1), over, tp_swap(over, 1)]
    near_memory = [here[0], tp_swap(here[0], 1), over_late, tp_swap(over_late, 1)]
    at = x.reshape(1)

    def natural(a, b):
        a, b = a.reshape(2, 1, 64, depth), b.reshape(2, 1, 64, depth)
        low, high = jnp.where(y == 0, a, b), jnp.where(y == 0, b, a)
        return jnp.concatenate([low, high], axis=1).reshape(256, depth)

    across_b, diag_b, _ = lax.optimization_barrier((across_b, diag_b, row1[2]))
    far = rms_rows(
        jnp.concatenate([natural(across_a, across_b), natural(diag_a, diag_b)], axis=0)
    )
    q_far, k_far, v_far = (
        project(far, w_query, scale),
        project(far, w_key),
        project(far, w_value),
    )

    def block_at(near_part, far_part, pair_index):
        both = jnp.stack([near_part.reshape(2, 256, -1), far_part.reshape(2, 256, -1)])
        both = both.reshape(4, 256, -1)[:, :BLOCK]
        return lax.dynamic_index_in_dim(both, pair_index ^ t, 0, keepdims=False)

    head = jnp.concatenate([block_at(k_near, k_far, 0), block_at(v_near, v_far, 0)], axis=1)
    following = lax.ppermute(head, "seq", [(i, i - 1) for i in range(1, peers)])
    middle = jnp.concatenate([block_at(k_near, k_far, 2), block_at(v_near, v_far, 2)], axis=1)
    next_far = jnp.where(y == 0, following, middle)
    next_near = jnp.where(y == 0, middle, following)
    width = k_near.shape[1]

    def mix(rows):
        return jnp.dot(rows, w_out, preferred_element_type=jnp.float32)

    far_rest = (
        k_far,
        v_far,
        next_far[:, :width],
        next_far[:, width:],
        *memory_project(at, far_memory, w_key, w_value),
    )
    far_other = mix(attention(info[1][1], 1, q_far, *far_rest)).astype(jnp.bfloat16)
    far_other = jnp.concatenate([tp_swap(part, 1) for part in jnp.split(far_other, 4)])
    far_own = mix(attention(info[1][0], 0, after(q_far, over_late), *far_rest))
    far_sum = (far_own + far_other.astype(jnp.float32)).astype(jnp.bfloat16)
    from_far = tp_swap(far_sum, 2)

    q_near, *near_memory = lax.optimization_barrier((q_near, *near_memory, far_sum))[:5]
    near_rest = (
        k_near,
        v_near,
        next_near[:, :width],
        next_near[:, width:],
        *memory_project(at, near_memory, w_key, w_value),
    )
    near_other = mix(attention(info[0][1], 1, q_near, *near_rest)).astype(jnp.bfloat16)
    near_other = jnp.concatenate([tp_swap(part, 1) for part in jnp.split(near_other, 4)])
    near_own = mix(attention(info[0][0], 0, q_near, *near_rest))
    total = near_own + near_other.astype(jnp.float32) + from_far.astype(jnp.float32)
    return total.astype(jnp.bfloat16)


def solution(mesh):
    return jax.shard_map(
        shards,
        mesh=mesh,
        in_specs=(
            P(("seq", "tp"), None),
            P(None, "tp"),
            P(None, "tp"),
            P(None, "tp"),
            P("tp", None),
            P("seq", None),
        ),
        out_specs=P(("seq", "tp"), None),
        check_vma=False,
    )
```

```python
import jax
import jax.numpy as jnp
from jax import lax
from jax.experimental import pallas as pl
from jax.experimental.pallas import tpu as pltpu
from jax.sharding import PartitionSpec as P

HDIM = 64
BLOCK = 128
GROUP = 4
ROW = 4
LOG2E = 1.4426950408889634


def x_ring(peers, by):
    return [(i, (i // ROW) * ROW + (i % ROW + by) % ROW) for i in range(peers)]


def z_next(peers, keep=None):
    return [
        (i, i + ROW)
        for i in range(peers - ROW)
        if keep is None or (i % ROW - keep) % ROW != 0
    ]


def tp_swap(x, mask):
    return lax.ppermute(x, "tp", [(i, i ^ mask) for i in range(4)])


def after(x, *others):
    return lax.optimization_barrier((x, *others))[0]


def rms_rows(rows):
    values = rows.astype(jnp.float32)
    power = jnp.mean(values * values, axis=-1, keepdims=True)
    return (values * lax.rsqrt(power + 1e-05)).astype(jnp.bfloat16)


def spread(place, own, core, across, diag):
    width = own.shape[1] // ROW

    def kernel(place_ref, own_ref, core_ref, across_ref, diag_ref, *outs):
        frame = place_ref[0]
        part = place_ref[1]
        x = place_ref[2]
        for k in range(ROW):
            cols = pl.ds(pl.multiple_of(lax.rem(x + k, ROW) * width, width), width)
            for j, ref in enumerate((own_ref, core_ref, across_ref, diag_ref)):
                for b in range(2):
                    start = b * BLOCK + frame if j < 2 else b * 64 + part
                    rows = pl.ds(pl.multiple_of(start, 32), 32)
                    outs[k][j * 2 + b] = ref[rows, cols]

    vmem = pl.BlockSpec(memory_space=pltpu.VMEM)
    return pl.pallas_call(
        kernel,
        in_specs=[pl.BlockSpec(memory_space=pltpu.SMEM)] + [vmem] * 4,
        out_specs=[vmem] * ROW,
        out_shape=[jax.ShapeDtypeStruct((8, 32, width), own.dtype)] * ROW,
        compiler_params=pltpu.CompilerParams(vmem_limit_bytes=24 << 20),
        name="spread",
    )(place, own, core, across, diag)


def pick(which, index, pieces):
    width = pieces[0].shape[2]
    count = len(pieces)

    def kernel(which_ref, index_ref, *rest):
        ins, outs = rest[:count], rest[count : count + 2 * ROW]
        held, sems = rest[count + 2 * ROW :]
        copies = [pltpu.make_async_copy(ins[a], held.at[a], sems.at[a]) for a in range(count)]
        for copy in copies:
            copy.start()
        for copy in copies:
            copy.wait()
        for k in range(ROW):
            for i in range(6):
                n = k * 6 + i
                outs[i // 3 * ROW + k][i % 3] = held[which_ref[n], index_ref[n]]

    smem = pl.BlockSpec(memory_space=pltpu.SMEM)
    outs = pl.pallas_call(
        kernel,
        in_specs=[smem] * 2 + [pl.BlockSpec(memory_space=pl.ANY)] * count,
        out_specs=[pl.BlockSpec(memory_space=pltpu.VMEM)] * (2 * ROW),
        out_shape=[jax.ShapeDtypeStruct((3, 32, width), pieces[0].dtype)] * (2 * ROW),
        scratch_shapes=[
            pltpu.VMEM((count, 8, 32, width), pieces[0].dtype),
            pltpu.SemaphoreType.DMA((count,)),
        ],
        compiler_params=pltpu.CompilerParams(vmem_limit_bytes=24 << 20),
        name="pick",
    )(which, index, *pieces)
    return outs[:ROW], outs[ROW:]


def memory_project(x, groups, w_key, w_value):
    rows, depth = groups[0].shape
    part = depth // ROW
    width = w_key.shape[1]

    def kernel(x_ref, *rest):
        pieces, (wk, wv, ok, ov) = rest[:4], rest[4:]
        held = [ref[...] for ref in pieces]
        power = [
            jnp.sum(jnp.square(h.astype(jnp.float32)), axis=1, keepdims=True) for h in held
        ]
        factor = lax.rsqrt(jnp.concatenate(power, axis=0) / depth + 1e-05)
        key = jnp.zeros((4 * rows, width), jnp.float32)
        value = jnp.zeros((4 * rows, width), jnp.float32)
        for k in range(ROW):
            piece = jnp.concatenate([h[:, k * part : (k + 1) * part] for h in held], axis=0)
            at = pl.ds(pl.multiple_of(lax.rem(x_ref[0] - k + ROW, ROW) * part, part), part)
            key += jnp.dot(piece, wk[at], preferred_element_type=jnp.float32)
            value += jnp.dot(piece, wv[at], preferred_element_type=jnp.float32)
        ok[...] = (key * factor).astype(jnp.bfloat16)
        ov[...] = (value * factor).astype(jnp.bfloat16)

    vmem = pl.BlockSpec(memory_space=pltpu.VMEM)
    return pl.pallas_call(
        kernel,
        in_specs=[pl.BlockSpec(memory_space=pltpu.SMEM)] + [vmem] * 6,
        out_specs=[vmem] * 2,
        out_shape=[jax.ShapeDtypeStruct((4 * rows, width), jnp.bfloat16)] * 2,
        cost_estimate=pl.CostEstimate(
            flops=16 * rows * depth * width, bytes_accessed=6 << 20, transcendentals=0
        ),
        compiler_params=pltpu.CompilerParams(vmem_limit_bytes=40 << 20),
        name="memory_project",
    )(x, *groups, w_key, w_value)


def head_part(lane, h, q, keys, values, hide):
    mine = (lane < HDIM) if h == 0 else (lane >= HDIM)
    s = lax.dot_general(
        jnp.where(mine, q, jnp.zeros_like(q)),
        keys,
        (((1,), (1,)), ((), ())),
        preferred_element_type=jnp.float32,
    )
    s = hide(s)
    m = jnp.max(s, axis=1, keepdims=True)
    p = jnp.exp2(s - m).astype(jnp.bfloat16)
    o = jnp.dot(p, values, preferred_element_type=jnp.float32)
    return m, o[:, : 2 * HDIM], o[:, 2 * HDIM :]


def attend_own(q, k, v):
    rows, width = q.shape
    pair = 2 * HDIM

    def kernel(q_ref, k_ref, v_ref, m_ref, o_ref, l_ref, vc):
        @pl.when(pl.program_id(0) == 0)
        def _():
            vc[:, pair:] = jnp.ones((rows, pair), jnp.bfloat16)

        vc[:, :pair] = v_ref[...]
        lane = lax.broadcasted_iota(jnp.int32, (1, pair), 1)
        for b in range(rows // BLOCK):
            at = slice(b * BLOCK, (b + 1) * BLOCK)
            parts = [
                head_part(lane, h, q_ref[at], k_ref[...], vc[...], lambda s: s) for h in range(2)
            ]
            for ref, first, second in zip((m_ref, o_ref, l_ref), *parts):
                ref[at] = jnp.where(lane < HDIM, first, second)

    spec = pl.BlockSpec((rows, pair), lambda h: (0, h))
    return pl.pallas_call(
        kernel,
        grid=(width // pair,),
        in_specs=[spec] * 3,
        out_specs=[spec] * 3,
        out_shape=[jax.ShapeDtypeStruct((rows, width), jnp.float32)] * 3,
        scratch_shapes=[pltpu.VMEM((rows, 2 * pair), jnp.bfloat16)],
        cost_estimate=pl.CostEstimate(
            flops=rows * rows * width * 12, bytes_accessed=4 << 20, transcendentals=0
        ),
        compiler_params=pltpu.CompilerParams(vmem_limit_bytes=40 << 20),
        name="attend_own",
    )(q, k, v)


def attention(info, half, q, own, kn, vn, km, vm):
    rows, width = q.shape[0] // 2, q.shape[1]
    keys = 512
    pair = 2 * HDIM

    def kernel(info_ref, q_ref, m_ref, w_ref, l_ref, kn_ref, vn_ref, km_ref, vm_ref, o_ref, kc, vc):
        @pl.when(pl.program_id(0) == 0)
        def _():
            vc[:, pair:] = jnp.ones((keys, pair), jnp.bfloat16)

        kc[:384] = km_ref[...]
        vc[:384, :pair] = vm_ref[...]
        kc[384:] = kn_ref[...]
        vc[384:, :pair] = vn_ref[...]
        lane = lax.broadcasted_iota(jnp.int32, (1, pair), 1)
        key = lax.broadcasted_iota(jnp.int32, (1, keys), 1)
        slot = lax.rem(lax.div(key, 32), 3)
        listed = jnp.where(
            slot == 0, info_ref[0], jnp.where(slot == 1, info_ref[1], info_ref[2])
        )
        for b in range(rows // BLOCK):
            at = slice(b * BLOCK, (b + 1) * BLOCK)
            usable = jnp.where(key < 384, listed, info_ref[3 + b]) > 0
            parts = [
                head_part(
                    lane,
                    h,
                    q_ref[at],
                    kc[...],
                    vc[...],
                    lambda s, usable=usable: jnp.where(usable, s, -1e30),
                )
                for h in range(2)
            ]
            m2, o2, l2 = (jnp.where(lane < HDIM, *both) for both in zip(*parts))
            m1 = m_ref[at]
            m = jnp.maximum(m1, m2)
            f1, f2 = jnp.exp2(m1 - m), jnp.exp2(m2 - m)
            total = l_ref[at] * f1 + l2 * f2
            o_ref[at] = ((w_ref[at] * f1 + o2 * f2) / total).astype(jnp.bfloat16)

    col = lambda h, info: (0, h)
    part = pl.BlockSpec((rows, pair), lambda h, info: (half, h))
    return pl.pallas_call(
        kernel,
        grid_spec=pltpu.PrefetchScalarGridSpec(
            num_scalar_prefetch=1,
            grid=(width // pair,),
            in_specs=[part] * 4
            + [
                pl.BlockSpec((BLOCK, pair), col),
                pl.BlockSpec((BLOCK, pair), col),
                pl.BlockSpec((384, pair), col),
                pl.BlockSpec((384, pair), col),
            ],
            out_specs=pl.BlockSpec((rows, pair), col),
            scratch_shapes=[
                pltpu.VMEM((keys, pair), jnp.bfloat16),
                pltpu.VMEM((keys, 2 * pair), jnp.bfloat16),
            ],
        ),
        out_shape=jax.ShapeDtypeStruct((rows, width), jnp.bfloat16),
        cost_estimate=pl.CostEstimate(flops=1 << 20, bytes_accessed=1 << 16, transcendentals=0),
        compiler_params=pltpu.CompilerParams(vmem_limit_bytes=40 << 20),
        name="attention",
    )(info, q, *own, kn, vn, km, vm)


def shards(frames, w_query, w_key, w_value, w_out, key_blocks):
    peers = lax.axis_size("seq")
    s = lax.axis_index("seq").astype(jnp.int32)
    t = lax.axis_index("tp").astype(jnp.int32)
    y, c, x, row = t // 2, t % 2, s % ROW, s // ROW
    scale = HDIM ** (-0.5) * LOG2E
    depth = frames.shape[1]

    def project(normed, weight, by=None):
        out = jnp.dot(normed, weight, preferred_element_type=jnp.float32)
        return (out if by is None else out * by).astype(jnp.bfloat16)

    def by_chip(pair):
        return jnp.where(y == 0, pair, pair[::-1])

    halves = frames.reshape(2, 2, 64, depth)
    ahead = lax.dynamic_index_in_dim(halves, 1 - y, 1, keepdims=False).reshape(128, depth)
    across_a = tp_swap(ahead, 2)
    core = tp_swap(after(frames, ahead), 1)

    near = rms_rows(jnp.concatenate([frames, core], axis=0))
    q_near, k_near, v_near = (
        project(near, w_query, scale),
        project(near, w_key),
        project(near, w_value),
    )
    across_a, q_near, k_near, v_near = lax.optimization_barrier((across_a, q_near, k_near, v_near))
    diag_a = tp_swap(across_a, 1)
    rest = lax.dynamic_index_in_dim(halves, y, 1, keepdims=False).reshape(128, depth)
    across_b = tp_swap(after(rest, across_a), 2)

    place = jnp.stack([y * 64 + c * 32, c * 32, x])
    pieces = spread(place, frames, core, across_a, diag_a)
    row0 = [pieces[0]] + [lax.ppermute(pieces[k], "seq", x_ring(peers, k)) for k in (1, 2, 3)]
    row1 = [lax.ppermute(p, "seq", z_next(peers)) for p in row0]
    row2 = [lax.ppermute(p, "seq", z_next(peers, k)) for k, p in enumerate(row1)]
    across_b, key_blocks, _ = lax.optimization_barrier((across_b, key_blocks, row1[0]))
    diag_b = tp_swap(across_b, 1)

    b0 = s * 8 + jnp.arange(2, dtype=jnp.int32)[:, None] * GROUP
    lists = key_blocks.reshape(2, GROUP, 8)
    first = lists[:, 0]
    valid = (first >= 0) & (first < b0)
    rank = jnp.cumsum(valid.astype(jnp.int32), axis=1) - 1
    slots = jnp.stack(
        [jnp.sum(jnp.where(valid & (rank == i), first + 1, 0), axis=1) for i in range(3)], axis=1
    ) - 1
    slots = by_chip(slots)
    with_next = jnp.any(lists == (b0 + GROUP)[:, :, None], axis=2).astype(jnp.int32)
    with_next = by_chip(with_next).reshape(2, 2, 2)
    with_next = jnp.where(c == 0, with_next, with_next[:, ::-1])
    listed = (slots >= 0).astype(jnp.int32)
    info = [[jnp.concatenate([listed[i], with_next[i, j]]) for j in range(2)] for i in range(2)]
    tables = [slots.reshape(6)] + [
        lax.ppermute(slots, "seq", x_ring(peers, -k)).reshape(6) for k in range(1, ROW)
    ]
    wanted = jnp.concatenate(tables)
    used = wanted >= 0
    which = jnp.where(used, (row - wanted // 32) * ROW + (x - wanted // 8 % ROW) % ROW, 0)
    index = jnp.where(used, ((wanted % 8 // 2) ^ t) * 2 + wanted % 2, 0)

    def natural(a, b):
        a, b = a.reshape(2, 1, 64, depth), b.reshape(2, 1, 64, depth)
        low, high = jnp.where(y == 0, a, b), jnp.where(y == 0, b, a)
        return jnp.concatenate([low, high], axis=1).reshape(256, depth)

    across_b, diag_b, _ = lax.optimization_barrier((across_b, diag_b, row1[2]))
    far = rms_rows(
        jnp.concatenate([natural(across_a, across_b), natural(diag_a, diag_b)], axis=0)
    )
    q_far, k_far, v_far = (
        project(far, w_query, scale),
        project(far, w_key),
        project(far, w_value),
    )

    def block_at(near_part, far_part, pair_index):
        both = jnp.stack([near_part.reshape(2, 256, -1), far_part.reshape(2, 256, -1)])
        both = both.reshape(4, 256, -1)[:, :BLOCK]
        return lax.dynamic_index_in_dim(both, pair_index ^ t, 0, keepdims=False)

    head = jnp.concatenate([block_at(k_near, k_far, 0), block_at(v_near, v_far, 0)], axis=1)
    index = lax.optimization_barrier((index, q_far, head))[0]
    following = lax.ppermute(head, "seq", [(i, i - 1) for i in range(1, peers)])
    chosen = pick(which, index, row0 + row1 + row2)

    def returned(parts):
        back = [parts[0]] + [lax.ppermute(parts[k], "seq", x_ring(peers, k)) for k in (1, 2, 3)]
        return jnp.concatenate([p.reshape(96, -1) for p in back], axis=1)

    here = [returned(chosen[0])]
    here.append(returned(lax.optimization_barrier((*chosen[1], here[0]))[:ROW]))
    over = tp_swap(here[0], 2)
    over_late = tp_swap(here[1], 2)
    far_memory = [here[1], tp_swap(here[1], 1), over, tp_swap(over, 1)]
    near_memory = [here[0], tp_swap(here[0], 1), over_late, tp_swap(over_late, 1)]
    at = x.reshape(1)

    middle = jnp.concatenate([block_at(k_near, k_far, 2), block_at(v_near, v_far, 2)], axis=1)
    next_far = jnp.where(y == 0, following, middle)
    next_near = jnp.where(y == 0, middle, following)
    width = k_near.shape[1]

    def mix(rows):
        return jnp.dot(rows, w_out, preferred_element_type=jnp.float32)

    far_rest = (
        attend_own(q_far, k_far, v_far),
        next_far[:, :width],
        next_far[:, width:],
        *memory_project(at, far_memory, w_key, w_value),
    )
    far_other = mix(attention(info[1][1], 1, q_far, *far_rest)).astype(jnp.bfloat16)
    far_other = jnp.concatenate([tp_swap(part, 1) for part in jnp.split(far_other, 4)])
    far_own = mix(attention(info[1][0], 0, after(q_far, over_late), *far_rest))
    far_sum = (far_own + far_other.astype(jnp.float32)).astype(jnp.bfloat16)
    from_far = tp_swap(far_sum, 2)

    q_near, *near_memory = lax.optimization_barrier((q_near, *near_memory, far_sum))[:5]
    near_rest = (
        attend_own(q_near, k_near, v_near),
        next_near[:, :width],
        next_near[:, width:],
        *memory_project(at, near_memory, w_key, w_value),
    )
    near_other = mix(attention(info[0][1], 1, q_near, *near_rest)).astype(jnp.bfloat16)
    near_other = jnp.concatenate([tp_swap(part, 1) for part in jnp.split(near_other, 4)])
    near_own = mix(attention(info[0][0], 0, q_near, *near_rest))
    total = near_own + near_other.astype(jnp.float32) + from_far.astype(jnp.float32)
    return total.astype(jnp.bfloat16)


def solution(mesh):
    return jax.shard_map(
        shards,
        mesh=mesh,
        in_specs=(
            P(("seq", "tp"), None),
            P(None, "tp"),
            P(None, "tp"),
            P(None, "tp"),
            P("tp", None),
            P("seq", None),
        ),
        out_specs=P(("seq", "tp"), None),
        check_vma=False,
    )
```

```python
import jax
import jax.numpy as jnp
from jax import lax
from jax.experimental import pallas as pl
from jax.experimental.pallas import tpu as pltpu
from jax.sharding import PartitionSpec as P

HDIM = 64
BLOCK = 128
GROUP = 4
ROW = 4
LOG2E = 1.4426950408889634


def x_ring(peers, by):
    return [(i, (i // ROW) * ROW + (i % ROW + by) % ROW) for i in range(peers)]


def z_next(peers, keep=None):
    return [
        (i, i + ROW)
        for i in range(peers - ROW)
        if keep is None or (i % ROW - keep) % ROW != 0
    ]


def tp_swap(x, mask):
    return lax.ppermute(x, "tp", [(i, i ^ mask) for i in range(4)])


def after(x, *others):
    return lax.optimization_barrier((x, *others))[0]


def rms_rows(rows):
    values = rows.astype(jnp.float32)
    power = jnp.mean(values * values, axis=-1, keepdims=True)
    return (values * lax.rsqrt(power + 1e-05)).astype(jnp.bfloat16)


def spread(place, own, core, across, diag):
    width = own.shape[1] // ROW

    def kernel(place_ref, own_ref, core_ref, across_ref, diag_ref, *outs):
        frame = place_ref[0]
        part = place_ref[1]
        x = place_ref[2]
        for k in range(ROW):
            cols = pl.ds(pl.multiple_of(lax.rem(x + k, ROW) * width, width), width)
            for j, ref in enumerate((own_ref, core_ref, across_ref, diag_ref)):
                for b in range(2):
                    start = b * BLOCK + frame if j < 2 else b * 64 + part
                    rows = pl.ds(pl.multiple_of(start, 32), 32)
                    outs[k][j * 2 + b] = ref[rows, cols]

    vmem = pl.BlockSpec(memory_space=pltpu.VMEM)
    return pl.pallas_call(
        kernel,
        in_specs=[pl.BlockSpec(memory_space=pltpu.SMEM)] + [vmem] * 4,
        out_specs=[vmem] * ROW,
        out_shape=[jax.ShapeDtypeStruct((8, 32, width), own.dtype)] * ROW,
        compiler_params=pltpu.CompilerParams(vmem_limit_bytes=24 << 20),
        name="spread",
    )(place, own, core, across, diag)


def pick(which, index, pieces):
    width = pieces[0].shape[2]
    count = len(pieces)

    def kernel(which_ref, index_ref, *rest):
        ins, outs = rest[:count], rest[count : count + 2 * ROW]
        held, sems = rest[count + 2 * ROW :]
        copies = [pltpu.make_async_copy(ins[a], held.at[a], sems.at[a]) for a in range(count)]
        for copy in copies:
            copy.start()
        for copy in copies:
            copy.wait()
        for k in range(ROW):
            for i in range(6):
                n = k * 6 + i
                outs[i // 3 * ROW + k][i % 3] = held[which_ref[n], index_ref[n]]

    smem = pl.BlockSpec(memory_space=pltpu.SMEM)
    outs = pl.pallas_call(
        kernel,
        in_specs=[smem] * 2 + [pl.BlockSpec(memory_space=pl.ANY)] * count,
        out_specs=[pl.BlockSpec(memory_space=pltpu.VMEM)] * (2 * ROW),
        out_shape=[jax.ShapeDtypeStruct((3, 32, width), pieces[0].dtype)] * (2 * ROW),
        scratch_shapes=[
            pltpu.VMEM((count, 8, 32, width), pieces[0].dtype),
            pltpu.SemaphoreType.DMA((count,)),
        ],
        compiler_params=pltpu.CompilerParams(vmem_limit_bytes=24 << 20),
        name="pick",
    )(which, index, *pieces)
    return outs[:ROW], outs[ROW:]


def memory_project(x, groups, w_key, w_value):
    rows, depth = groups[0].shape
    part = depth // ROW
    width = w_key.shape[1]

    def kernel(x_ref, *rest):
        pieces, (wk, wv, ok, ov) = rest[:4], rest[4:]
        held = [ref[...] for ref in pieces]
        power = [
            jnp.sum(jnp.square(h.astype(jnp.float32)), axis=1, keepdims=True) for h in held
        ]
        factor = lax.rsqrt(jnp.concatenate(power, axis=0) / depth + 1e-05)
        key = jnp.zeros((4 * rows, width), jnp.float32)
        value = jnp.zeros((4 * rows, width), jnp.float32)
        for k in range(ROW):
            piece = jnp.concatenate([h[:, k * part : (k + 1) * part] for h in held], axis=0)
            at = pl.ds(pl.multiple_of(lax.rem(x_ref[0] - k + ROW, ROW) * part, part), part)
            key += jnp.dot(piece, wk[at], preferred_element_type=jnp.float32)
            value += jnp.dot(piece, wv[at], preferred_element_type=jnp.float32)
        ok[...] = (key * factor).astype(jnp.bfloat16)
        ov[...] = (value * factor).astype(jnp.bfloat16)

    vmem = pl.BlockSpec(memory_space=pltpu.VMEM)
    return pl.pallas_call(
        kernel,
        in_specs=[pl.BlockSpec(memory_space=pltpu.SMEM)] + [vmem] * 6,
        out_specs=[vmem] * 2,
        out_shape=[jax.ShapeDtypeStruct((4 * rows, width), jnp.bfloat16)] * 2,
        cost_estimate=pl.CostEstimate(
            flops=16 * rows * depth * width, bytes_accessed=6 << 20, transcendentals=0
        ),
        compiler_params=pltpu.CompilerParams(vmem_limit_bytes=40 << 20),
        name="memory_project",
    )(x, *groups, w_key, w_value)


def head_part(lane, h, q, keys, values, hide):
    mine = (lane < HDIM) if h == 0 else (lane >= HDIM)
    s = lax.dot_general(
        jnp.where(mine, q, jnp.zeros_like(q)),
        keys,
        (((1,), (1,)), ((), ())),
        preferred_element_type=jnp.float32,
    )
    s = hide(s)
    m = jnp.max(s, axis=1, keepdims=True)
    p = jnp.exp2(s - m).astype(jnp.bfloat16)
    o = jnp.dot(p, values, preferred_element_type=jnp.float32)
    return m, o[:, : 2 * HDIM], o[:, 2 * HDIM :]


def attend_own(q, k, v):
    rows, width = q.shape
    pair = 2 * HDIM

    def kernel(q_ref, k_ref, v_ref, m_ref, o_ref, l_ref, vc):
        @pl.when(pl.program_id(0) == 0)
        def _():
            vc[:, pair:] = jnp.ones((rows, pair), jnp.bfloat16)

        vc[:, :pair] = v_ref[...]
        lane = lax.broadcasted_iota(jnp.int32, (1, pair), 1)
        for b in range(rows // BLOCK):
            at = slice(b * BLOCK, (b + 1) * BLOCK)
            parts = [
                head_part(lane, h, q_ref[at], k_ref[...], vc[...], lambda s: s) for h in range(2)
            ]
            for ref, first, second in zip((m_ref, o_ref, l_ref), *parts):
                ref[at] = jnp.where(lane < HDIM, first, second)

    spec = pl.BlockSpec((rows, pair), lambda h: (0, h))
    return pl.pallas_call(
        kernel,
        grid=(width // pair,),
        in_specs=[spec] * 3,
        out_specs=[spec] * 3,
        out_shape=[jax.ShapeDtypeStruct((rows, width), jnp.float32)] * 3,
        scratch_shapes=[pltpu.VMEM((rows, 2 * pair), jnp.bfloat16)],
        cost_estimate=pl.CostEstimate(
            flops=rows * rows * width * 12, bytes_accessed=4 << 20, transcendentals=0
        ),
        compiler_params=pltpu.CompilerParams(vmem_limit_bytes=40 << 20),
        name="attend_own",
    )(q, k, v)


def attention(info, half, q, own, kn, vn, km, vm):
    rows, width = q.shape[0] // 2, q.shape[1]
    keys = 512
    pair = 2 * HDIM

    def kernel(info_ref, q_ref, m_ref, w_ref, l_ref, kn_ref, vn_ref, km_ref, vm_ref, o_ref, kc, vc):
        @pl.when(pl.program_id(0) == 0)
        def _():
            vc[:, pair:] = jnp.ones((keys, pair), jnp.bfloat16)

        kc[:384] = km_ref[...]
        vc[:384, :pair] = vm_ref[...]
        kc[384:] = kn_ref[...]
        vc[384:, :pair] = vn_ref[...]
        lane = lax.broadcasted_iota(jnp.int32, (1, pair), 1)
        key = lax.broadcasted_iota(jnp.int32, (1, keys), 1)
        slot = lax.rem(lax.div(key, 32), 3)
        listed = jnp.where(
            slot == 0, info_ref[0], jnp.where(slot == 1, info_ref[1], info_ref[2])
        )
        for b in range(rows // BLOCK):
            at = slice(b * BLOCK, (b + 1) * BLOCK)
            usable = jnp.where(key < 384, listed, info_ref[3 + b]) > 0
            parts = [
                head_part(
                    lane,
                    h,
                    q_ref[at],
                    kc[...],
                    vc[...],
                    lambda s, usable=usable: jnp.where(usable, s, -1e30),
                )
                for h in range(2)
            ]
            m2, o2, l2 = (jnp.where(lane < HDIM, *both) for both in zip(*parts))
            m1 = m_ref[at]
            m = jnp.maximum(m1, m2)
            f1, f2 = jnp.exp2(m1 - m), jnp.exp2(m2 - m)
            total = l_ref[at] * f1 + l2 * f2
            o_ref[at] = ((w_ref[at] * f1 + o2 * f2) / total).astype(jnp.bfloat16)

    col = lambda h, info: (0, h)
    part = pl.BlockSpec((rows, pair), lambda h, info: (half, h))
    return pl.pallas_call(
        kernel,
        grid_spec=pltpu.PrefetchScalarGridSpec(
            num_scalar_prefetch=1,
            grid=(width // pair,),
            in_specs=[part] * 4
            + [
                pl.BlockSpec((BLOCK, pair), col),
                pl.BlockSpec((BLOCK, pair), col),
                pl.BlockSpec((384, pair), col),
                pl.BlockSpec((384, pair), col),
            ],
            out_specs=pl.BlockSpec((rows, pair), col),
            scratch_shapes=[
                pltpu.VMEM((keys, pair), jnp.bfloat16),
                pltpu.VMEM((keys, 2 * pair), jnp.bfloat16),
            ],
        ),
        out_shape=jax.ShapeDtypeStruct((rows, width), jnp.bfloat16),
        cost_estimate=pl.CostEstimate(flops=1 << 20, bytes_accessed=1 << 16, transcendentals=0),
        compiler_params=pltpu.CompilerParams(vmem_limit_bytes=40 << 20),
        name="attention",
    )(info, q, *own, kn, vn, km, vm)


def shards(frames, w_query, w_key, w_value, w_out, key_blocks):
    peers = lax.axis_size("seq")
    s = lax.axis_index("seq").astype(jnp.int32)
    t = lax.axis_index("tp").astype(jnp.int32)
    y, c, x, row = t // 2, t % 2, s % ROW, s // ROW
    scale = HDIM ** (-0.5) * LOG2E
    depth = frames.shape[1]

    def project(normed, weight, by=None):
        out = jnp.dot(normed, weight, preferred_element_type=jnp.float32)
        return (out if by is None else out * by).astype(jnp.bfloat16)

    def by_chip(pair):
        return jnp.where(y == 0, pair, pair[::-1])

    halves = frames.reshape(2, 2, 64, depth)
    ahead = lax.dynamic_index_in_dim(halves, 1 - y, 1, keepdims=False).reshape(128, depth)
    across_a = tp_swap(ahead, 2)
    core = tp_swap(after(frames, ahead), 1)

    near = rms_rows(jnp.concatenate([frames, core], axis=0))
    q_near, k_near, v_near = (
        project(near, w_query, scale),
        project(near, w_key),
        project(near, w_value),
    )
    key_blocks = after(key_blocks, k_near)

    b0 = s * 8 + jnp.arange(2, dtype=jnp.int32)[:, None] * GROUP
    lists = key_blocks.reshape(2, GROUP, 8)
    first = lists[:, 0]
    valid = (first >= 0) & (first < b0)
    rank = jnp.cumsum(valid.astype(jnp.int32), axis=1) - 1
    slots = jnp.stack(
        [jnp.sum(jnp.where(valid & (rank == i), first + 1, 0), axis=1) for i in range(3)], axis=1
    ) - 1
    slots = by_chip(slots)
    with_next = jnp.any(lists == (b0 + GROUP)[:, :, None], axis=2).astype(jnp.int32)
    with_next = by_chip(with_next).reshape(2, 2, 2)
    with_next = jnp.where(c == 0, with_next, with_next[:, ::-1])
    listed = (slots >= 0).astype(jnp.int32)
    info = [[jnp.concatenate([listed[i], with_next[i, j]]) for j in range(2)] for i in range(2)]
    tables = [slots.reshape(6)] + [
        lax.ppermute(slots, "seq", x_ring(peers, -k)).reshape(6) for k in range(1, ROW)
    ]
    wanted = jnp.concatenate(tables)
    used = wanted >= 0
    which = jnp.where(used, (row - wanted // 32) * ROW + (x - wanted // 8 % ROW) % ROW, 0)
    index = jnp.where(used, ((wanted % 8 // 2) ^ t) * 2 + wanted % 2, 0)

    across_a, q_near, k_near, v_near, which, index = lax.optimization_barrier(
        (across_a, q_near, k_near, v_near, which, index)
    )
    diag_a = tp_swap(across_a, 1)
    rest = lax.dynamic_index_in_dim(halves, y, 1, keepdims=False).reshape(128, depth)
    across_b = tp_swap(after(rest, across_a), 2)

    place = jnp.stack([y * 64 + c * 32, c * 32, x])
    pieces = spread(place, frames, core, across_a, diag_a)
    row0 = [pieces[0]] + [lax.ppermute(pieces[k], "seq", x_ring(peers, k)) for k in (1, 2, 3)]
    row1 = [lax.ppermute(p, "seq", z_next(peers)) for p in row0]
    across_b = after(across_b, row1[0])
    diag_b = tp_swap(across_b, 1)

    def natural(a, b):
        a, b = a.reshape(2, 1, 64, depth), b.reshape(2, 1, 64, depth)
        low, high = jnp.where(y == 0, a, b), jnp.where(y == 0, b, a)
        return jnp.concatenate([low, high], axis=1).reshape(256, depth)

    far = rms_rows(
        jnp.concatenate([natural(across_a, across_b), natural(diag_a, diag_b)], axis=0)
    )
    q_far, k_far, v_far = (
        project(far, w_query, scale),
        project(far, w_key),
        project(far, w_value),
    )

    def block_at(near_part, far_part, pair_index):
        both = jnp.stack([near_part.reshape(2, 256, -1), far_part.reshape(2, 256, -1)])
        both = both.reshape(4, 256, -1)[:, :BLOCK]
        return lax.dynamic_index_in_dim(both, pair_index ^ t, 0, keepdims=False)

    head = jnp.concatenate([block_at(k_near, k_far, 0), block_at(v_near, v_far, 0)], axis=1)
    following = lax.ppermute(head, "seq", [(i, i - 1) for i in range(1, peers)])
    passing = [*row1[:3], after(row1[3], q_far, head)]
    row2 = [lax.ppermute(p, "seq", z_next(peers, k)) for k, p in enumerate(passing)]
    far_part = attend_own(q_far, k_far, v_far)
    index, following, *far_part = lax.optimization_barrier((index, following, *far_part))
    chosen = pick(which, index, row0 + row1 + row2)

    def returned(parts):
        back = [parts[0]] + [lax.ppermute(parts[k], "seq", x_ring(peers, k)) for k in (1, 2, 3)]
        return jnp.concatenate([p.reshape(96, -1) for p in back], axis=1)

    here = [returned(chosen[0])]
    here.append(returned(lax.optimization_barrier((*chosen[1], here[0]))[:ROW]))
    over = tp_swap(here[0], 2)
    over_late = tp_swap(here[1], 2)
    far_memory = [here[1], tp_swap(here[1], 1), over, tp_swap(over, 1)]
    near_memory = [here[0], tp_swap(here[0], 1), over_late, tp_swap(over_late, 1)]
    at = x.reshape(1)

    middle = jnp.concatenate([block_at(k_near, k_far, 2), block_at(v_near, v_far, 2)], axis=1)
    next_far = jnp.where(y == 0, following, middle)
    next_near = jnp.where(y == 0, middle, following)
    width = k_near.shape[1]

    def mix(rows):
        return jnp.dot(rows, w_out, preferred_element_type=jnp.float32)

    far_rest = (
        far_part,
        next_far[:, :width],
        next_far[:, width:],
        *memory_project(at, far_memory, w_key, w_value),
    )
    far_other = mix(attention(info[1][1], 1, q_far, *far_rest)).astype(jnp.bfloat16)
    far_other = jnp.concatenate([tp_swap(part, 1) for part in jnp.split(far_other, 4)])
    far_own = mix(attention(info[1][0], 0, after(q_far, over_late), *far_rest))
    far_sum = (far_own + far_other.astype(jnp.float32)).astype(jnp.bfloat16)
    from_far = tp_swap(far_sum, 2)

    q_near, *near_memory = lax.optimization_barrier((q_near, *near_memory, far_sum))[:5]
    near_rest = (
        attend_own(q_near, k_near, v_near),
        next_near[:, :width],
        next_near[:, width:],
        *memory_project(at, near_memory, w_key, w_value),
    )
    near_other = mix(attention(info[0][1], 1, q_near, *near_rest)).astype(jnp.bfloat16)
    near_other = jnp.concatenate([tp_swap(part, 1) for part in jnp.split(near_other, 4)])
    near_own = mix(attention(info[0][0], 0, q_near, *near_rest))
    total = near_own + near_other.astype(jnp.float32) + from_far.astype(jnp.float32)
    return total.astype(jnp.bfloat16)


def solution(mesh):
    return jax.shard_map(
        shards,
        mesh=mesh,
        in_specs=(
            P(("seq", "tp"), None),
            P(None, "tp"),
            P(None, "tp"),
            P(None, "tp"),
            P("tp", None),
            P("seq", None),
        ),
        out_specs=P(("seq", "tp"), None),
        check_vma=False,
    )
```

```python
import jax
import jax.numpy as jnp
from jax import lax
from jax.experimental import pallas as pl
from jax.experimental.pallas import tpu as pltpu
from jax.sharding import PartitionSpec as P

HDIM = 64
BLOCK = 128
GROUP = 4
ROW = 4
LOG2E = 1.4426950408889634


def x_ring(peers, by):
    return [(i, (i // ROW) * ROW + (i % ROW + by) % ROW) for i in range(peers)]


def z_hop(x, peers, keep=None):
    half = peers // 2
    pairs = [
        (i * 4 + t, (i + ROW) * 4 + (t ^ 2 if i < half <= i + ROW else t))
        for i in range(peers - ROW)
        if keep is None or (i % ROW - keep) % ROW != 0
        for t in range(4)
    ]
    return lax.ppermute(x, ("seq", "tp"), pairs)


def tp_swap(x, mask):
    return lax.ppermute(x, "tp", [(i, i ^ mask) for i in range(4)])


def after(x, *others):
    return lax.optimization_barrier((x, *others))[0]


def rms_rows(rows):
    values = rows.astype(jnp.float32)
    power = jnp.mean(values * values, axis=-1, keepdims=True)
    return (values * lax.rsqrt(power + 1e-05)).astype(jnp.bfloat16)


def spread(place, own, core, across, diag):
    width = own.shape[1] // ROW

    def kernel(place_ref, own_ref, core_ref, across_ref, diag_ref, *outs):
        frame = place_ref[0]
        part = place_ref[1]
        x = place_ref[2]
        for k in range(ROW):
            cols = pl.ds(pl.multiple_of(lax.rem(x + k, ROW) * width, width), width)
            for j, ref in enumerate((own_ref, core_ref, across_ref, diag_ref)):
                for b in range(2):
                    start = b * BLOCK + frame if j < 2 else b * 64 + part
                    rows = pl.ds(pl.multiple_of(start, 32), 32)
                    outs[k][j * 2 + b] = ref[rows, cols]

    vmem = pl.BlockSpec(memory_space=pltpu.VMEM)
    return pl.pallas_call(
        kernel,
        in_specs=[pl.BlockSpec(memory_space=pltpu.SMEM)] + [vmem] * 4,
        out_specs=[vmem] * ROW,
        out_shape=[jax.ShapeDtypeStruct((8, 32, width), own.dtype)] * ROW,
        compiler_params=pltpu.CompilerParams(vmem_limit_bytes=24 << 20),
        name="spread",
    )(place, own, core, across, diag)


def pick(which, index, pieces):
    width = pieces[0].shape[2]
    count = len(pieces)

    def kernel(which_ref, index_ref, *rest):
        ins, outs = rest[:count], rest[count : count + 2 * ROW]
        held, sems = rest[count + 2 * ROW :]
        copies = [pltpu.make_async_copy(ins[a], held.at[a], sems.at[a]) for a in range(count)]
        for copy in copies:
            copy.start()
        for copy in copies:
            copy.wait()
        for k in range(ROW):
            for i in range(6):
                n = k * 6 + i
                outs[i // 3 * ROW + k][i % 3] = held[which_ref[n], index_ref[n]]

    smem = pl.BlockSpec(memory_space=pltpu.SMEM)
    outs = pl.pallas_call(
        kernel,
        in_specs=[smem] * 2 + [pl.BlockSpec(memory_space=pl.ANY)] * count,
        out_specs=[pl.BlockSpec(memory_space=pltpu.VMEM)] * (2 * ROW),
        out_shape=[jax.ShapeDtypeStruct((3, 32, width), pieces[0].dtype)] * (2 * ROW),
        scratch_shapes=[
            pltpu.VMEM((count, 8, 32, width), pieces[0].dtype),
            pltpu.SemaphoreType.DMA((count,)),
        ],
        compiler_params=pltpu.CompilerParams(vmem_limit_bytes=24 << 20),
        name="pick",
    )(which, index, *pieces)
    return outs[:ROW], outs[ROW:]


def memory_project(x, groups, w_key, w_value):
    rows, depth = groups[0].shape
    part = depth // ROW
    width = w_key.shape[1]

    def kernel(x_ref, *rest):
        pieces, (wk, wv, ok, ov) = rest[:4], rest[4:]
        held = [ref[...] for ref in pieces]
        power = [
            jnp.sum(jnp.square(h.astype(jnp.float32)), axis=1, keepdims=True) for h in held
        ]
        factor = lax.rsqrt(jnp.concatenate(power, axis=0) / depth + 1e-05)
        key = jnp.zeros((4 * rows, width), jnp.float32)
        value = jnp.zeros((4 * rows, width), jnp.float32)
        for k in range(ROW):
            piece = jnp.concatenate([h[:, k * part : (k + 1) * part] for h in held], axis=0)
            at = pl.ds(pl.multiple_of(lax.rem(x_ref[0] - k + ROW, ROW) * part, part), part)
            key += jnp.dot(piece, wk[at], preferred_element_type=jnp.float32)
            value += jnp.dot(piece, wv[at], preferred_element_type=jnp.float32)
        ok[...] = (key * factor).astype(jnp.bfloat16)
        ov[...] = (value * factor).astype(jnp.bfloat16)

    vmem = pl.BlockSpec(memory_space=pltpu.VMEM)
    return pl.pallas_call(
        kernel,
        in_specs=[pl.BlockSpec(memory_space=pltpu.SMEM)] + [vmem] * 6,
        out_specs=[vmem] * 2,
        out_shape=[jax.ShapeDtypeStruct((4 * rows, width), jnp.bfloat16)] * 2,
        cost_estimate=pl.CostEstimate(
            flops=16 * rows * depth * width, bytes_accessed=6 << 20, transcendentals=0
        ),
        compiler_params=pltpu.CompilerParams(vmem_limit_bytes=40 << 20),
        name="memory_project",
    )(x, *groups, w_key, w_value)


def head_parts(lane, queries, keys, values, hide):
    scores = []
    for q in queries:
        for mine in (lane < HDIM, lane >= HDIM):
            scores.append(
                lax.dot_general(
                    jnp.where(mine, q, jnp.zeros_like(q)),
                    keys,
                    (((1,), (1,)), ((), ())),
                    preferred_element_type=jnp.float32,
                )
            )
    scores = [hide(s, i // 2) for i, s in enumerate(scores)]
    most = [jnp.max(s, axis=1, keepdims=True) for s in scores]
    weights = [jnp.exp2(s - m).astype(jnp.bfloat16) for s, m in zip(scores, most)]
    sums = [jnp.dot(p, values, preferred_element_type=jnp.float32) for p in weights]
    pair = 2 * HDIM
    parts = [(m, o[:, :pair], o[:, pair:]) for m, o in zip(most, sums)]
    return [
        [jnp.where(lane < HDIM, one, two) for one, two in zip(parts[i], parts[i + 1])]
        for i in range(0, len(parts), 2)
    ]


def attend_own(q, k, v):
    rows, width = q.shape
    pair = 2 * HDIM

    def kernel(q_ref, k_ref, v_ref, m_ref, o_ref, l_ref, vc):
        @pl.when(pl.program_id(0) == 0)
        def _():
            vc[:, pair:] = jnp.ones((rows, pair), jnp.bfloat16)

        vc[:, :pair] = v_ref[...]
        lane = lax.broadcasted_iota(jnp.int32, (1, pair), 1)
        for b in range(0, rows, 2 * BLOCK):
            at = [slice(b, b + BLOCK), slice(b + BLOCK, b + 2 * BLOCK)]
            parts = head_parts(
                lane, [q_ref[i] for i in at], k_ref[...], vc[...], lambda s, i: s
            )
            for i, part in zip(at, parts):
                m_ref[i], o_ref[i], l_ref[i] = part

    spec = pl.BlockSpec((rows, pair), lambda h: (0, h))
    return pl.pallas_call(
        kernel,
        grid=(width // pair,),
        in_specs=[spec] * 3,
        out_specs=[spec] * 3,
        out_shape=[jax.ShapeDtypeStruct((rows, width), jnp.float32)] * 3,
        scratch_shapes=[pltpu.VMEM((rows, 2 * pair), jnp.bfloat16)],
        cost_estimate=pl.CostEstimate(
            flops=rows * rows * width * 12, bytes_accessed=4 << 20, transcendentals=0
        ),
        compiler_params=pltpu.CompilerParams(vmem_limit_bytes=40 << 20),
        name="attend_own",
    )(q, k, v)


def attention(info, half, q, own, kn, vn, km, vm):
    rows, width = q.shape[0] // 2, q.shape[1]
    keys = 512
    pair = 2 * HDIM

    def kernel(info_ref, q_ref, m_ref, w_ref, l_ref, kn_ref, vn_ref, km_ref, vm_ref, o_ref, kc, vc):
        @pl.when(pl.program_id(0) == 0)
        def _():
            vc[:, pair:] = jnp.ones((keys, pair), jnp.bfloat16)

        kc[:384] = km_ref[...]
        vc[:384, :pair] = vm_ref[...]
        kc[384:] = kn_ref[...]
        vc[384:, :pair] = vn_ref[...]
        lane = lax.broadcasted_iota(jnp.int32, (1, pair), 1)
        key = lax.broadcasted_iota(jnp.int32, (1, keys), 1)
        slot = lax.rem(lax.div(key, 32), 3)
        listed = jnp.where(
            slot == 0, info_ref[0], jnp.where(slot == 1, info_ref[1], info_ref[2])
        )
        usable = [jnp.where(key < 384, listed, info_ref[3 + b]) > 0 for b in range(2)]
        at = [slice(0, BLOCK), slice(BLOCK, 2 * BLOCK)]
        parts = head_parts(
            lane,
            [q_ref[i] for i in at],
            kc[...],
            vc[...],
            lambda s, b: jnp.where(usable[b], s, -1e30),
        )
        for i, (m2, o2, l2) in zip(at, parts):
            m1 = m_ref[i]
            m = jnp.maximum(m1, m2)
            f1, f2 = jnp.exp2(m1 - m), jnp.exp2(m2 - m)
            total = l_ref[i] * f1 + l2 * f2
            o_ref[i] = ((w_ref[i] * f1 + o2 * f2) / total).astype(jnp.bfloat16)

    col = lambda h, info: (0, h)
    part = pl.BlockSpec((rows, pair), lambda h, info: (half, h))
    return pl.pallas_call(
        kernel,
        grid_spec=pltpu.PrefetchScalarGridSpec(
            num_scalar_prefetch=1,
            grid=(width // pair,),
            in_specs=[part] * 4
            + [
                pl.BlockSpec((BLOCK, pair), col),
                pl.BlockSpec((BLOCK, pair), col),
                pl.BlockSpec((384, pair), col),
                pl.BlockSpec((384, pair), col),
            ],
            out_specs=pl.BlockSpec((rows, pair), col),
            scratch_shapes=[
                pltpu.VMEM((keys, pair), jnp.bfloat16),
                pltpu.VMEM((keys, 2 * pair), jnp.bfloat16),
            ],
        ),
        out_shape=jax.ShapeDtypeStruct((rows, width), jnp.bfloat16),
        cost_estimate=pl.CostEstimate(flops=1 << 20, bytes_accessed=1 << 16, transcendentals=0),
        compiler_params=pltpu.CompilerParams(vmem_limit_bytes=40 << 20),
        name="attention",
    )(info, q, *own, kn, vn, km, vm)


def shards(frames, w_query, w_key, w_value, w_out, key_blocks):
    peers = lax.axis_size("seq")
    s = lax.axis_index("seq").astype(jnp.int32)
    t = lax.axis_index("tp").astype(jnp.int32)
    y, c, x, row = t // 2, t % 2, s % ROW, s // ROW
    scale = HDIM ** (-0.5) * LOG2E
    depth = frames.shape[1]

    def project(normed, weight, by=None):
        out = jnp.dot(normed, weight, preferred_element_type=jnp.float32)
        return (out if by is None else out * by).astype(jnp.bfloat16)

    def by_chip(pair):
        return jnp.where(y == 0, pair, pair[::-1])

    halves = frames.reshape(2, 2, 64, depth)
    ahead = lax.dynamic_index_in_dim(halves, 1 - y, 1, keepdims=False).reshape(128, depth)
    across_a = tp_swap(ahead, 2)
    core = tp_swap(after(frames, ahead), 1)

    near = rms_rows(jnp.concatenate([frames, core], axis=0))
    q_near, k_near, v_near = (
        project(near, w_query, scale),
        project(near, w_key),
        project(near, w_value),
    )
    key_blocks = after(key_blocks, q_near, k_near, v_near)

    b0 = s * 8 + jnp.arange(2, dtype=jnp.int32)[:, None] * GROUP
    lists = key_blocks.reshape(2, GROUP, 8)
    first = lists[:, 0]
    valid = (first >= 0) & (first < b0)
    rank = jnp.cumsum(valid.astype(jnp.int32), axis=1) - 1
    slots = jnp.stack(
        [jnp.sum(jnp.where(valid & (rank == i), first + 1, 0), axis=1) for i in range(3)], axis=1
    ) - 1
    slots = by_chip(slots)
    with_next = jnp.any(lists == (b0 + GROUP)[:, :, None], axis=2).astype(jnp.int32)
    with_next = by_chip(with_next).reshape(2, 2, 2)
    with_next = jnp.where(c == 0, with_next, with_next[:, ::-1])
    listed = (slots >= 0).astype(jnp.int32)
    info = [[jnp.concatenate([listed[i], with_next[i, j]]) for j in range(2)] for i in range(2)]
    tables = [slots.reshape(6)] + [
        lax.ppermute(slots, "seq", x_ring(peers, -k)).reshape(6) for k in range(1, ROW)
    ]
    wanted = jnp.concatenate(tables)
    used = wanted >= 0
    which = jnp.where(used, (row - wanted // 32) * ROW + (x - wanted // 8 % ROW) % ROW, 0)
    half = peers // 2
    turned = jnp.where((wanted < half * 8) & (s >= half), 2, 0)
    index = jnp.where(used, ((wanted % 8 // 2) ^ t ^ turned) * 2 + wanted % 2, 0)

    across_a, q_near, k_near, v_near, which, index = lax.optimization_barrier(
        (across_a, q_near, k_near, v_near, which, index)
    )
    diag_a = tp_swap(across_a, 1)
    rest = lax.dynamic_index_in_dim(halves, y, 1, keepdims=False).reshape(128, depth)
    across_b = tp_swap(after(rest, across_a), 2)

    place = jnp.stack([y * 64 + c * 32, c * 32, x])
    pieces = spread(place, frames, core, across_a, diag_a)
    row0 = [pieces[0]] + [lax.ppermute(pieces[k], "seq", x_ring(peers, k)) for k in (1, 2, 3)]
    row1 = [z_hop(p, peers) for p in row0]
    across_b = after(across_b, row1[0])
    diag_b = tp_swap(across_b, 1)

    def natural(a, b):
        a, b = a.reshape(2, 1, 64, depth), b.reshape(2, 1, 64, depth)
        low, high = jnp.where(y == 0, a, b), jnp.where(y == 0, b, a)
        return jnp.concatenate([low, high], axis=1).reshape(256, depth)

    far = rms_rows(
        jnp.concatenate([natural(across_a, across_b), natural(diag_a, diag_b)], axis=0)
    )
    q_far, k_far, v_far = (
        project(far, w_query, scale),
        project(far, w_key),
        project(far, w_value),
    )

    def block_at(near_part, far_part, pair_index):
        both = jnp.stack([near_part.reshape(2, 256, -1), far_part.reshape(2, 256, -1)])
        both = both.reshape(4, 256, -1)[:, :BLOCK]
        return lax.dynamic_index_in_dim(both, pair_index ^ t, 0, keepdims=False)

    head = jnp.concatenate([block_at(k_near, k_far, 0), block_at(v_near, v_far, 0)], axis=1)
    passing = [*row1[:2], after(row1[2], q_far, k_far, v_far), after(row1[3], q_far, k_far, v_far)]
    row2 = [z_hop(p, peers, k) for k, p in enumerate(passing)]
    following = lax.ppermute(
        after(head, row2[0]), "seq", [(i, i - 1) for i in range(1, peers)]
    )
    far_part = attend_own(q_far, k_far, v_far)
    index, following, *far_part = lax.optimization_barrier((index, following, *far_part))
    chosen = pick(which, index, row0 + row1 + row2)

    def returned(parts):
        back = [parts[0]] + [lax.ppermute(parts[k], "seq", x_ring(peers, k)) for k in (1, 2, 3)]
        return jnp.concatenate([p.reshape(96, -1) for p in back], axis=1)

    here = [returned(chosen[0])]
    here.append(returned(lax.optimization_barrier((*chosen[1], here[0]))[:ROW]))
    over = tp_swap(here[0], 2)
    over_late = tp_swap(here[1], 2)
    far_memory = [here[1], tp_swap(here[1], 1), over, tp_swap(over, 1)]
    near_memory = [here[0], tp_swap(here[0], 1), over_late, tp_swap(over_late, 1)]
    at = x.reshape(1)

    middle = jnp.concatenate([block_at(k_near, k_far, 2), block_at(v_near, v_far, 2)], axis=1)
    next_far = jnp.where(y == 0, following, middle)
    next_near = jnp.where(y == 0, middle, following)
    width = k_near.shape[1]

    def mix(rows):
        return jnp.dot(rows, w_out, preferred_element_type=jnp.float32)

    far_rest = (
        far_part,
        next_far[:, :width],
        next_far[:, width:],
        *memory_project(at, far_memory, w_key, w_value),
    )
    far_other = mix(attention(info[1][1], 1, q_far, *far_rest)).astype(jnp.bfloat16)
    far_other = jnp.concatenate([tp_swap(part, 1) for part in jnp.split(far_other, 4)])
    far_own = mix(attention(info[1][0], 0, after(q_far, over_late), *far_rest))
    far_sum = (far_own + far_other.astype(jnp.float32)).astype(jnp.bfloat16)
    from_far = tp_swap(far_sum, 2)

    q_near, *near_memory = lax.optimization_barrier((q_near, *near_memory, far_sum))[:5]
    near_rest = (
        attend_own(q_near, k_near, v_near),
        next_near[:, :width],
        next_near[:, width:],
        *memory_project(at, near_memory, w_key, w_value),
    )
    near_other = mix(attention(info[0][1], 1, q_near, *near_rest)).astype(jnp.bfloat16)
    near_other = jnp.concatenate([tp_swap(part, 1) for part in jnp.split(near_other, 4)])
    near_own = mix(attention(info[0][0], 0, q_near, *near_rest))
    total = near_own + near_other.astype(jnp.float32) + from_far.astype(jnp.float32)
    return total.astype(jnp.bfloat16)


def solution(mesh):
    return jax.shard_map(
        shards,
        mesh=mesh,
        in_specs=(
            P(("seq", "tp"), None),
            P(None, "tp"),
            P(None, "tp"),
            P(None, "tp"),
            P("tp", None),
            P("seq", None),
        ),
        out_specs=P(("seq", "tp"), None),
        check_vma=False,
    )
```

```python
import jax
import jax.numpy as jnp
from jax import lax
from jax.experimental import pallas as pl
from jax.experimental.pallas import tpu as pltpu
from jax.sharding import PartitionSpec as P

HDIM = 64
BLOCK = 128
GROUP = 4
ROW = 4
LOG2E = 1.4426950408889634


def x_ring(peers, by):
    return [(i, (i // ROW) * ROW + (i % ROW + by) % ROW) for i in range(peers)]


def z_hop(x, peers, keep=None):
    half = peers // 2
    pairs = [
        (i * 4 + t, (i + ROW) * 4 + (t ^ 2 if i < half <= i + ROW else t))
        for i in range(peers - ROW)
        if keep is None or (i % ROW - keep) % ROW != 0
        for t in range(4)
    ]
    return lax.ppermute(x, ("seq", "tp"), pairs)


def tp_swap(x, mask):
    return lax.ppermute(x, "tp", [(i, i ^ mask) for i in range(4)])


def after(x, *others):
    return lax.optimization_barrier((x, *others))[0]


def rms_rows(rows):
    values = rows.astype(jnp.float32)
    power = jnp.mean(values * values, axis=-1, keepdims=True)
    return (values * lax.rsqrt(power + 1e-05)).astype(jnp.bfloat16)


def spread(place, own, core, across, diag):
    width = own.shape[1] // ROW

    def kernel(place_ref, own_ref, core_ref, across_ref, diag_ref, *outs):
        frame = place_ref[0]
        part = place_ref[1]
        x = place_ref[2]
        for k in range(ROW):
            cols = pl.ds(pl.multiple_of(lax.rem(x + k, ROW) * width, width), width)
            for j, ref in enumerate((own_ref, core_ref, across_ref, diag_ref)):
                for b in range(2):
                    start = b * BLOCK + frame if j < 2 else b * 64 + part
                    rows = pl.ds(pl.multiple_of(start, 32), 32)
                    outs[k][j * 2 + b] = ref[rows, cols]

    vmem = pl.BlockSpec(memory_space=pltpu.VMEM)
    return pl.pallas_call(
        kernel,
        in_specs=[pl.BlockSpec(memory_space=pltpu.SMEM)] + [vmem] * 4,
        out_specs=[vmem] * ROW,
        out_shape=[jax.ShapeDtypeStruct((8, 32, width), own.dtype)] * ROW,
        compiler_params=pltpu.CompilerParams(vmem_limit_bytes=24 << 20),
        name="spread",
    )(place, own, core, across, diag)


def pick(which, index, pieces):
    width = pieces[0].shape[2]
    count = len(pieces)

    def kernel(which_ref, index_ref, *rest):
        ins, outs = rest[:count], rest[count : count + 2 * ROW]
        held, sems = rest[count + 2 * ROW :]
        copies = [pltpu.make_async_copy(ins[a], held.at[a], sems.at[a]) for a in range(count)]
        for copy in copies:
            copy.start()
        for copy in copies:
            copy.wait()
        for k in range(ROW):
            for i in range(6):
                n = k * 6 + i
                outs[i // 3 * ROW + k][i % 3] = held[which_ref[n], index_ref[n]]

    smem = pl.BlockSpec(memory_space=pltpu.SMEM)
    outs = pl.pallas_call(
        kernel,
        in_specs=[smem] * 2 + [pl.BlockSpec(memory_space=pl.ANY)] * count,
        out_specs=[pl.BlockSpec(memory_space=pltpu.VMEM)] * (2 * ROW),
        out_shape=[jax.ShapeDtypeStruct((3, 32, width), pieces[0].dtype)] * (2 * ROW),
        scratch_shapes=[
            pltpu.VMEM((count, 8, 32, width), pieces[0].dtype),
            pltpu.SemaphoreType.DMA((count,)),
        ],
        compiler_params=pltpu.CompilerParams(vmem_limit_bytes=24 << 20),
        name="pick",
    )(which, index, *pieces)
    return outs[:ROW], outs[ROW:]


def memory_project(x, groups, w_key, w_value):
    rows, depth = groups[0].shape
    part = depth // ROW
    width = w_key.shape[1]

    def kernel(x_ref, *rest):
        pieces, (wk, wv, ok, ov) = rest[:4], rest[4:]
        held = [ref[...] for ref in pieces]
        power = [
            jnp.sum(jnp.square(h.astype(jnp.float32)), axis=1, keepdims=True) for h in held
        ]
        factor = lax.rsqrt(jnp.concatenate(power, axis=0) / depth + 1e-05)
        key = jnp.zeros((4 * rows, width), jnp.float32)
        value = jnp.zeros((4 * rows, width), jnp.float32)
        for k in range(ROW):
            piece = jnp.concatenate([h[:, k * part : (k + 1) * part] for h in held], axis=0)
            at = pl.ds(pl.multiple_of(lax.rem(x_ref[0] - k + ROW, ROW) * part, part), part)
            key += jnp.dot(piece, wk[at], preferred_element_type=jnp.float32)
            value += jnp.dot(piece, wv[at], preferred_element_type=jnp.float32)
        ok[...] = (key * factor).astype(jnp.bfloat16)
        ov[...] = (value * factor).astype(jnp.bfloat16)

    vmem = pl.BlockSpec(memory_space=pltpu.VMEM)
    return pl.pallas_call(
        kernel,
        in_specs=[pl.BlockSpec(memory_space=pltpu.SMEM)] + [vmem] * 6,
        out_specs=[vmem] * 2,
        out_shape=[jax.ShapeDtypeStruct((4 * rows, width), jnp.bfloat16)] * 2,
        cost_estimate=pl.CostEstimate(
            flops=16 * rows * depth * width, bytes_accessed=6 << 20, transcendentals=0
        ),
        compiler_params=pltpu.CompilerParams(vmem_limit_bytes=40 << 20),
        name="memory_project",
    )(x, *groups, w_key, w_value)


def attention(info, half, q, k, v, kn, vn, km, vm):
    rows, width = q.shape[0] // 2, q.shape[1]
    keys = 1024
    pair = 2 * HDIM

    def kernel(info_ref, q_ref, k_ref, v_ref, kn_ref, vn_ref, km_ref, vm_ref, o_ref, kc, vc):
        @pl.when(pl.program_id(0) == 0)
        def _():
            vc[:, pair:] = jnp.ones((keys, pair), jnp.bfloat16)

        kc[:384] = km_ref[...]
        vc[:384, :pair] = vm_ref[...]
        kc[384:512] = kn_ref[...]
        vc[384:512, :pair] = vn_ref[...]
        kc[512:] = k_ref[...]
        vc[512:, :pair] = v_ref[...]
        lane = lax.broadcasted_iota(jnp.int32, (1, pair), 1)
        key = lax.broadcasted_iota(jnp.int32, (1, keys), 1)
        slot = lax.rem(lax.div(key, 32), 3)
        listed = jnp.where(
            slot == 0, info_ref[0], jnp.where(slot == 1, info_ref[1], info_ref[2])
        )
        listed = jnp.where(key < 384, listed, 1)
        tiles = [(b, h) for b in range(rows // BLOCK) for h in range(2)]

        def scores(b, h):
            q = q_ref[b * BLOCK : (b + 1) * BLOCK]
            mine = (lane < HDIM) if h == 0 else (lane >= HDIM)
            s = lax.dot_general(
                jnp.where(mine, q, jnp.zeros_like(q)),
                kc[...],
                (((1,), (1,)), ((), ())),
                preferred_element_type=jnp.float32,
            )
            here = jnp.where((key >= 384) & (key < 512), info_ref[3 + b], listed) > 0
            return jnp.where(here, s, -1e30)

        ahead = scores(*tiles[0])
        results = []
        for i in range(len(tiles)):
            s = ahead
            if i + 1 < len(tiles):
                ahead = scores(*tiles[i + 1])
            m = jnp.max(s, axis=1, keepdims=True)
            p = jnp.exp2(s - m).astype(jnp.bfloat16)
            o = jnp.dot(p, vc[...], preferred_element_type=jnp.float32)
            results.append(o[:, :pair] / o[:, pair:])
        for b in range(rows // BLOCK):
            o_ref[b * BLOCK : (b + 1) * BLOCK] = jnp.where(
                lane < HDIM, results[2 * b], results[2 * b + 1]
            ).astype(jnp.bfloat16)

    col = lambda h, info: (0, h)
    return pl.pallas_call(
        kernel,
        grid_spec=pltpu.PrefetchScalarGridSpec(
            num_scalar_prefetch=1,
            grid=(width // pair,),
            in_specs=[
                pl.BlockSpec((rows, pair), lambda h, info: (half, h)),
                pl.BlockSpec((2 * rows, pair), col),
                pl.BlockSpec((2 * rows, pair), col),
                pl.BlockSpec((BLOCK, pair), col),
                pl.BlockSpec((BLOCK, pair), col),
                pl.BlockSpec((384, pair), col),
                pl.BlockSpec((384, pair), col),
            ],
            out_specs=pl.BlockSpec((rows, pair), col),
            scratch_shapes=[
                pltpu.VMEM((keys, pair), jnp.bfloat16),
                pltpu.VMEM((keys, 2 * pair), jnp.bfloat16),
            ],
        ),
        out_shape=jax.ShapeDtypeStruct((rows, width), jnp.bfloat16),
        cost_estimate=pl.CostEstimate(flops=1 << 20, bytes_accessed=1 << 16, transcendentals=0),
        compiler_params=pltpu.CompilerParams(vmem_limit_bytes=40 << 20),
        name="attention",
    )(info, q, k, v, kn, vn, km, vm)


def shards(frames, w_query, w_key, w_value, w_out, key_blocks):
    peers = lax.axis_size("seq")
    s = lax.axis_index("seq").astype(jnp.int32)
    t = lax.axis_index("tp").astype(jnp.int32)
    y, c, x, row = t // 2, t % 2, s % ROW, s // ROW
    scale = HDIM ** (-0.5) * LOG2E
    depth = frames.shape[1]

    def project(normed, weight, by=None):
        out = jnp.dot(normed, weight, preferred_element_type=jnp.float32)
        return (out if by is None else out * by).astype(jnp.bfloat16)

    def by_chip(pair):
        return jnp.where(y == 0, pair, pair[::-1])

    halves = frames.reshape(2, 2, 64, depth)
    ahead = lax.dynamic_index_in_dim(halves, 1 - y, 1, keepdims=False).reshape(128, depth)
    across_a = tp_swap(ahead, 2)
    core = tp_swap(after(frames, ahead), 1)

    near = rms_rows(jnp.concatenate([frames, core], axis=0))
    q_near, k_near, v_near = (
        project(near, w_query, scale),
        project(near, w_key),
        project(near, w_value),
    )
    key_blocks = after(key_blocks, core)

    b0 = s * 8 + jnp.arange(2, dtype=jnp.int32)[:, None] * GROUP
    lists = key_blocks.reshape(2, GROUP, 8)
    first = lists[:, 0]
    valid = (first >= 0) & (first < b0)
    rank = jnp.cumsum(valid.astype(jnp.int32), axis=1) - 1
    slots = jnp.stack(
        [jnp.sum(jnp.where(valid & (rank == i), first + 1, 0), axis=1) for i in range(3)], axis=1
    ) - 1
    slots = by_chip(slots)
    with_next = jnp.any(lists == (b0 + GROUP)[:, :, None], axis=2).astype(jnp.int32)
    with_next = by_chip(with_next).reshape(2, 2, 2)
    with_next = jnp.where(c == 0, with_next, with_next[:, ::-1])
    listed = (slots >= 0).astype(jnp.int32)
    info = [[jnp.concatenate([listed[i], with_next[i, j]]) for j in range(2)] for i in range(2)]
    tables = [slots.reshape(6)] + [
        lax.ppermute(slots, "seq", x_ring(peers, -k)).reshape(6) for k in range(1, ROW)
    ]
    wanted = jnp.concatenate(tables)
    used = wanted >= 0
    which = jnp.where(used, (row - wanted // 32) * ROW + (x - wanted // 8 % ROW) % ROW, 0)
    half = peers // 2
    turned = jnp.where((wanted < half * 8) & (s >= half), 2, 0)
    index = jnp.where(used, ((wanted % 8 // 2) ^ t ^ turned) * 2 + wanted % 2, 0)

    across_a, k_near, v_near, which, index = lax.optimization_barrier(
        (across_a, k_near, v_near, which, index)
    )
    diag_a = tp_swap(across_a, 1)
    rest = lax.dynamic_index_in_dim(halves, y, 1, keepdims=False).reshape(128, depth)
    across_b = tp_swap(after(rest, across_a), 2)

    place = jnp.stack([y * 64 + c * 32, c * 32, x])
    pieces = spread(place, frames, core, across_a, diag_a)
    row0 = [pieces[0]] + [lax.ppermute(pieces[k], "seq", x_ring(peers, k)) for k in (1, 2, 3)]
    row1 = [z_hop(p, peers) for p in row0]
    across_b = after(across_b, row0[2])
    diag_b = tp_swap(across_b, 1)

    def natural(a, b):
        a, b = a.reshape(2, 1, 64, depth), b.reshape(2, 1, 64, depth)
        low, high = jnp.where(y == 0, a, b), jnp.where(y == 0, b, a)
        return jnp.concatenate([low, high], axis=1).reshape(256, depth)

    far = rms_rows(
        jnp.concatenate([natural(across_a, across_b), natural(diag_a, diag_b)], axis=0)
    )
    q_far, k_far, v_far = (
        project(far, w_query, scale),
        project(far, w_key),
        project(far, w_value),
    )

    def block_at(near_part, far_part, pair_index):
        both = jnp.stack([near_part.reshape(2, 256, -1), far_part.reshape(2, 256, -1)])
        both = both.reshape(4, 256, -1)[:, :BLOCK]
        return lax.dynamic_index_in_dim(both, pair_index ^ t, 0, keepdims=False)

    head = jnp.concatenate([block_at(k_near, k_far, 0), block_at(v_near, v_far, 0)], axis=1)
    passing = [*row1[:2], after(row1[2], q_far, k_far, v_far), after(row1[3], q_far, k_far, v_far)]
    row2 = [z_hop(p, peers, k) for k, p in enumerate(passing)]
    chosen = pick(which, index, row0 + row1 + row2)

    def returned(parts):
        back = [parts[0]] + [lax.ppermute(parts[k], "seq", x_ring(peers, k)) for k in (1, 2, 3)]
        return jnp.concatenate([p.reshape(96, -1) for p in back], axis=1)

    here = [returned(chosen[0])]
    here.append(returned(lax.optimization_barrier((*chosen[1], here[0]))[:ROW]))
    following = lax.ppermute(
        after(head, here[0]), "seq", [(i, i - 1) for i in range(1, peers)]
    )
    over = tp_swap(here[0], 2)
    over_late = tp_swap(here[1], 2)
    far_memory = [here[1], tp_swap(here[1], 1), over, tp_swap(over, 1)]
    near_memory = [here[0], tp_swap(here[0], 1), over_late, tp_swap(over_late, 1)]
    at = x.reshape(1)

    middle = jnp.concatenate([block_at(k_near, k_far, 2), block_at(v_near, v_far, 2)], axis=1)
    next_far = jnp.where(y == 0, following, middle)
    next_near = jnp.where(y == 0, middle, following)
    width = k_near.shape[1]

    def mix(rows):
        return jnp.dot(rows, w_out, preferred_element_type=jnp.float32)

    far_rest = (
        k_far,
        v_far,
        next_far[:, :width],
        next_far[:, width:],
        *memory_project(at, far_memory, w_key, w_value),
    )
    far_other = mix(attention(info[1][1], 1, q_far, *far_rest)).astype(jnp.bfloat16)
    far_other = jnp.concatenate([tp_swap(part, 1) for part in jnp.split(far_other, 4)])
    far_own = mix(attention(info[1][0], 0, after(q_far, over_late), *far_rest))
    far_sum = (far_own + far_other.astype(jnp.float32)).astype(jnp.bfloat16)
    from_far = tp_swap(far_sum, 2)

    q_near, *near_memory = lax.optimization_barrier((q_near, *near_memory, far_sum))[:5]
    near_rest = (
        k_near,
        v_near,
        next_near[:, :width],
        next_near[:, width:],
        *memory_project(at, near_memory, w_key, w_value),
    )
    near_other = mix(attention(info[0][1], 1, q_near, *near_rest)).astype(jnp.bfloat16)
    near_other = jnp.concatenate([tp_swap(part, 1) for part in jnp.split(near_other, 4)])
    near_own = mix(attention(info[0][0], 0, q_near, *near_rest))
    total = near_own + near_other.astype(jnp.float32) + from_far.astype(jnp.float32)
    return total.astype(jnp.bfloat16)


def solution(mesh):
    return jax.shard_map(
        shards,
        mesh=mesh,
        in_specs=(
            P(("seq", "tp"), None),
            P(None, "tp"),
            P(None, "tp"),
            P(None, "tp"),
            P("tp", None),
            P("seq", None),
        ),
        out_specs=P(("seq", "tp"), None),
        check_vma=False,
    )
```

```python
import jax
import jax.numpy as jnp
from jax import lax
from jax.experimental import pallas as pl
from jax.experimental.pallas import tpu as pltpu
from jax.sharding import PartitionSpec as P

HDIM = 64
BLOCK = 128
GROUP = 4
ROW = 4
LOG2E = 1.4426950408889634


def x_ring(peers, by):
    return [(i, (i // ROW) * ROW + (i % ROW + by) % ROW) for i in range(peers)]


def z_hop(x, peers, keep=None):
    half = peers // 2
    pairs = [
        (i * 4 + t, (i + ROW) * 4 + (t ^ 2 if i < half <= i + ROW else t))
        for i in range(peers - ROW)
        if keep is None or (i % ROW - keep) % ROW != 0
        for t in range(4)
    ]
    return lax.ppermute(x, ("seq", "tp"), pairs)


def tp_swap(x, mask):
    return lax.ppermute(x, "tp", [(i, i ^ mask) for i in range(4)])


def after(x, *others):
    return lax.optimization_barrier((x, *others))[0]


def rms_rows(rows):
    values = rows.astype(jnp.float32)
    power = jnp.mean(values * values, axis=-1, keepdims=True)
    return (values * lax.rsqrt(power + 1e-05)).astype(jnp.bfloat16)


def spread(place, own, core, across, diag):
    width = own.shape[1] // ROW

    def kernel(place_ref, own_ref, core_ref, across_ref, diag_ref, *outs):
        frame = place_ref[0]
        part = place_ref[1]
        x = place_ref[2]
        for k in range(ROW):
            cols = pl.ds(pl.multiple_of(lax.rem(x + k, ROW) * width, width), width)
            for j, ref in enumerate((own_ref, core_ref, across_ref, diag_ref)):
                for b in range(2):
                    start = b * BLOCK + frame if j < 2 else b * 64 + part
                    rows = pl.ds(pl.multiple_of(start, 32), 32)
                    outs[k][j * 2 + b] = ref[rows, cols]

    vmem = pl.BlockSpec(memory_space=pltpu.VMEM)
    return pl.pallas_call(
        kernel,
        in_specs=[pl.BlockSpec(memory_space=pltpu.SMEM)] + [vmem] * 4,
        out_specs=[vmem] * ROW,
        out_shape=[jax.ShapeDtypeStruct((8, 32, width), own.dtype)] * ROW,
        compiler_params=pltpu.CompilerParams(vmem_limit_bytes=24 << 20),
        name="spread",
    )(place, own, core, across, diag)


def pick(which, index, pieces):
    width = pieces[0].shape[2]
    count = len(pieces)

    def kernel(which_ref, index_ref, *rest):
        ins, outs = rest[:count], rest[count : count + 2 * ROW]
        held, sems = rest[count + 2 * ROW :]
        copies = [pltpu.make_async_copy(ins[a], held.at[a], sems.at[a]) for a in range(count)]
        for copy in copies:
            copy.start()
        for copy in copies:
            copy.wait()
        for k in range(ROW):
            for i in range(6):
                n = k * 6 + i
                outs[i // 3 * ROW + k][i % 3] = held[which_ref[n], index_ref[n]]

    smem = pl.BlockSpec(memory_space=pltpu.SMEM)
    outs = pl.pallas_call(
        kernel,
        in_specs=[smem] * 2 + [pl.BlockSpec(memory_space=pl.ANY)] * count,
        out_specs=[pl.BlockSpec(memory_space=pltpu.VMEM)] * (2 * ROW),
        out_shape=[jax.ShapeDtypeStruct((3, 32, width), pieces[0].dtype)] * (2 * ROW),
        scratch_shapes=[
            pltpu.VMEM((count, 8, 32, width), pieces[0].dtype),
            pltpu.SemaphoreType.DMA((count,)),
        ],
        compiler_params=pltpu.CompilerParams(vmem_limit_bytes=24 << 20),
        name="pick",
    )(which, index, *pieces)
    return outs[:ROW], outs[ROW:]


def memory_project(x, groups, w_key, w_value):
    rows, depth = groups[0].shape
    part = depth // ROW
    width = w_key.shape[1]

    def kernel(x_ref, *rest):
        pieces, (wk, wv, ok, ov) = rest[:4], rest[4:]
        held = [ref[...] for ref in pieces]
        power = [
            jnp.sum(jnp.square(h.astype(jnp.float32)), axis=1, keepdims=True) for h in held
        ]
        factor = lax.rsqrt(jnp.concatenate(power, axis=0) / depth + 1e-05)
        key = jnp.zeros((4 * rows, width), jnp.float32)
        value = jnp.zeros((4 * rows, width), jnp.float32)
        for k in range(ROW):
            piece = jnp.concatenate([h[:, k * part : (k + 1) * part] for h in held], axis=0)
            at = pl.ds(pl.multiple_of(lax.rem(x_ref[0] - k + ROW, ROW) * part, part), part)
            key += jnp.dot(piece, wk[at], preferred_element_type=jnp.float32)
            value += jnp.dot(piece, wv[at], preferred_element_type=jnp.float32)
        ok[...] = (key * factor).astype(jnp.bfloat16)
        ov[...] = (value * factor).astype(jnp.bfloat16)

    vmem = pl.BlockSpec(memory_space=pltpu.VMEM)
    return pl.pallas_call(
        kernel,
        in_specs=[pl.BlockSpec(memory_space=pltpu.SMEM)] + [vmem] * 6,
        out_specs=[vmem] * 2,
        out_shape=[jax.ShapeDtypeStruct((4 * rows, width), jnp.bfloat16)] * 2,
        cost_estimate=pl.CostEstimate(
            flops=16 * rows * depth * width, bytes_accessed=6 << 20, transcendentals=0
        ),
        compiler_params=pltpu.CompilerParams(vmem_limit_bytes=40 << 20),
        name="memory_project",
    )(x, *groups, w_key, w_value)


def attention(info, half, q, k, v, kn, vn, km, vm):
    rows, width = q.shape[0] // 2, q.shape[1]
    keys = 1024
    pair = 2 * HDIM

    def kernel(info_ref, q_ref, k_ref, v_ref, kn_ref, vn_ref, km_ref, vm_ref, o_ref, kc, vc):
        lane = lax.broadcasted_iota(jnp.int32, (1, pair), 1)
        key = lax.broadcasted_iota(jnp.int32, (1, keys), 1)
        slot = lax.rem(lax.div(key, 32), 3)
        listed = jnp.where(
            slot == 0, info_ref[0], jnp.where(slot == 1, info_ref[1], info_ref[2])
        )
        listed = jnp.where(key < 384, listed, 1)
        vc[:, pair:] = jnp.ones((keys, pair), jnp.bfloat16)
        for n in range(width // pair):
            col = slice(n * pair, (n + 1) * pair)
            kc[:384] = km_ref[:, col]
            vc[:384, :pair] = vm_ref[:, col]
            kc[384:512] = kn_ref[:, col]
            vc[384:512, :pair] = vn_ref[:, col]
            kc[512:] = k_ref[:, col]
            vc[512:, :pair] = v_ref[:, col]
            for b in range(rows // BLOCK):
                qb = q_ref[half * rows + b * BLOCK : half * rows + (b + 1) * BLOCK, col]
                here = jnp.where((key >= 384) & (key < 512), info_ref[3 + b], listed) > 0
                results = []
                for h in range(2):
                    mine = (lane < HDIM) if h == 0 else (lane >= HDIM)
                    s = lax.dot_general(
                        jnp.where(mine, qb, jnp.zeros_like(qb)),
                        kc[...],
                        (((1,), (1,)), ((), ())),
                        preferred_element_type=jnp.float32,
                    )
                    s = jnp.where(here, s, -1e30)
                    m = jnp.max(s, axis=1, keepdims=True)
                    p = jnp.exp2(s - m).astype(jnp.bfloat16)
                    o = jnp.dot(p, vc[...], preferred_element_type=jnp.float32)
                    results.append(o[:, :pair] / o[:, pair:])
                o_ref[b * BLOCK : (b + 1) * BLOCK, col] = jnp.where(
                    lane < HDIM, results[0], results[1]
                ).astype(jnp.bfloat16)

    vmem = pl.BlockSpec(memory_space=pltpu.VMEM)
    return pl.pallas_call(
        kernel,
        in_specs=[pl.BlockSpec(memory_space=pltpu.SMEM)] + [vmem] * 7,
        out_specs=vmem,
        out_shape=jax.ShapeDtypeStruct((rows, width), jnp.bfloat16),
        scratch_shapes=[
            pltpu.VMEM((keys, pair), jnp.bfloat16),
            pltpu.VMEM((keys, 2 * pair), jnp.bfloat16),
        ],
        cost_estimate=pl.CostEstimate(flops=1 << 20, bytes_accessed=1 << 16, transcendentals=0),
        compiler_params=pltpu.CompilerParams(vmem_limit_bytes=32 << 20),
        name="attention",
    )(info, q, k, v, kn, vn, km, vm)


def shards(frames, w_query, w_key, w_value, w_out, key_blocks):
    peers = lax.axis_size("seq")
    s = lax.axis_index("seq").astype(jnp.int32)
    t = lax.axis_index("tp").astype(jnp.int32)
    y, c, x, row = t // 2, t % 2, s % ROW, s // ROW
    scale = HDIM ** (-0.5) * LOG2E
    depth = frames.shape[1]

    def project(normed, weight, by=None):
        out = jnp.dot(normed, weight, preferred_element_type=jnp.float32)
        return (out if by is None else out * by).astype(jnp.bfloat16)

    def by_chip(pair):
        return jnp.where(y == 0, pair, pair[::-1])

    halves = frames.reshape(2, 2, 64, depth)
    ahead = lax.dynamic_index_in_dim(halves, 1 - y, 1, keepdims=False).reshape(128, depth)
    across_a = tp_swap(ahead, 2)
    core = tp_swap(after(frames, ahead), 1)

    v_near = project(rms_rows(jnp.concatenate([frames, core], axis=0)), w_value)
    key_blocks = after(key_blocks, core)

    b0 = s * 8 + jnp.arange(2, dtype=jnp.int32)[:, None] * GROUP
    lists = key_blocks.reshape(2, GROUP, 8)
    first = lists[:, 0]
    valid = (first >= 0) & (first < b0)
    rank = jnp.cumsum(valid.astype(jnp.int32), axis=1) - 1
    slots = jnp.stack(
        [jnp.sum(jnp.where(valid & (rank == i), first + 1, 0), axis=1) for i in range(3)], axis=1
    ) - 1
    slots = by_chip(slots)
    with_next = jnp.any(lists == (b0 + GROUP)[:, :, None], axis=2).astype(jnp.int32)
    with_next = by_chip(with_next).reshape(2, 2, 2)
    with_next = jnp.where(c == 0, with_next, with_next[:, ::-1])
    listed = (slots >= 0).astype(jnp.int32)
    info = [[jnp.concatenate([listed[i], with_next[i, j]]) for j in range(2)] for i in range(2)]
    tables = [slots.reshape(6)] + [
        lax.ppermute(slots, "seq", x_ring(peers, -k)).reshape(6) for k in range(1, ROW)
    ]
    wanted = jnp.concatenate(tables)
    used = wanted >= 0
    which = jnp.where(used, (row - wanted // 32) * ROW + (x - wanted // 8 % ROW) % ROW, 0)
    half = peers // 2
    turned = jnp.where((wanted < half * 8) & (s >= half), 2, 0)
    index = jnp.where(used, ((wanted % 8 // 2) ^ t ^ turned) * 2 + wanted % 2, 0)

    across_a, v_near, which, index = lax.optimization_barrier((across_a, v_near, which, index))
    diag_a = tp_swap(across_a, 1)
    rest = lax.dynamic_index_in_dim(halves, y, 1, keepdims=False).reshape(128, depth)
    across_b = tp_swap(after(rest, across_a), 2)

    place = jnp.stack([y * 64 + c * 32, c * 32, x])
    pieces = spread(place, frames, core, across_a, diag_a)
    row0 = [pieces[0]] + [lax.ppermute(pieces[k], "seq", x_ring(peers, k)) for k in (1, 2, 3)]
    row1 = [z_hop(p, peers) for p in row0]
    across_b = after(across_b, row0[2])
    diag_b = tp_swap(across_b, 1)

    def natural(a, b):
        a, b = a.reshape(2, 1, 64, depth), b.reshape(2, 1, 64, depth)
        low, high = jnp.where(y == 0, a, b), jnp.where(y == 0, b, a)
        return jnp.concatenate([low, high], axis=1).reshape(256, depth)

    far = rms_rows(
        jnp.concatenate([natural(across_a, across_b), natural(diag_a, diag_b)], axis=0)
    )
    q_far, k_far, v_far = (
        project(far, w_query, scale),
        project(far, w_key),
        project(far, w_value),
    )

    passing = [*row1[:2], after(row1[2], q_far, k_far, v_far), after(row1[3], q_far, k_far, v_far)]
    row2 = [z_hop(p, peers, k) for k, p in enumerate(passing)]

    near = rms_rows(jnp.concatenate(lax.optimization_barrier((frames, core, q_far))[:2], axis=0))
    q_near, k_near = project(near, w_query, scale), project(near, w_key)

    def block_at(near_part, far_part, pair_index):
        both = jnp.stack([near_part.reshape(2, 256, -1), far_part.reshape(2, 256, -1)])
        both = both.reshape(4, 256, -1)[:, :BLOCK]
        return lax.dynamic_index_in_dim(both, pair_index ^ t, 0, keepdims=False)

    head = jnp.concatenate([block_at(k_near, k_far, 0), block_at(v_near, v_far, 0)], axis=1)
    index, q_near = lax.optimization_barrier((index, q_near, q_far, head))[:2]
    chosen = pick(which, index, row0 + row1 + row2)

    def returned(parts):
        back = [parts[0]] + [lax.ppermute(parts[k], "seq", x_ring(peers, k)) for k in (1, 2, 3)]
        return jnp.concatenate([p.reshape(96, -1) for p in back], axis=1)

    here = [returned(chosen[0])]
    here.append(returned(lax.optimization_barrier((*chosen[1], here[0]))[:ROW]))
    following = lax.ppermute(
        after(head, here[0]), "seq", [(i, i - 1) for i in range(1, peers)]
    )
    over = tp_swap(here[0], 2)
    over_late = tp_swap(here[1], 2)
    far_memory = [here[1], tp_swap(here[1], 1), over, tp_swap(over, 1)]
    near_memory = [here[0], tp_swap(here[0], 1), over_late, tp_swap(over_late, 1)]
    at = x.reshape(1)

    middle = jnp.concatenate([block_at(k_near, k_far, 2), block_at(v_near, v_far, 2)], axis=1)
    next_far = jnp.where(y == 0, following, middle)
    next_near = jnp.where(y == 0, middle, following)
    width = k_near.shape[1]

    def mix(rows):
        return jnp.dot(rows, w_out, preferred_element_type=jnp.float32)

    far_rest = (
        k_far,
        v_far,
        next_far[:, :width],
        next_far[:, width:],
        *memory_project(at, far_memory, w_key, w_value),
    )
    far_other = mix(attention(info[1][1], 1, q_far, *far_rest)).astype(jnp.bfloat16)
    far_other = jnp.concatenate([tp_swap(part, 1) for part in jnp.split(far_other, 4)])
    far_own = mix(attention(info[1][0], 0, after(q_far, over_late), *far_rest))
    far_sum = (far_own + far_other.astype(jnp.float32)).astype(jnp.bfloat16)
    from_far = tp_swap(far_sum, 2)

    q_near, *near_memory = lax.optimization_barrier((q_near, *near_memory, far_sum))[:5]
    near_rest = (
        k_near,
        v_near,
        next_near[:, :width],
        next_near[:, width:],
        *memory_project(at, near_memory, w_key, w_value),
    )
    near_other = mix(attention(info[0][1], 1, q_near, *near_rest)).astype(jnp.bfloat16)
    near_other = jnp.concatenate([tp_swap(part, 1) for part in jnp.split(near_other, 4)])
    near_own = mix(attention(info[0][0], 0, q_near, *near_rest))
    total = near_own + near_other.astype(jnp.float32) + from_far.astype(jnp.float32)
    return total.astype(jnp.bfloat16)


def solution(mesh):
    return jax.shard_map(
        shards,
        mesh=mesh,
        in_specs=(
            P(("seq", "tp"), None),
            P(None, "tp"),
            P(None, "tp"),
            P(None, "tp"),
            P("tp", None),
            P("seq", None),
        ),
        out_specs=P(("seq", "tp"), None),
        check_vma=False,
    )
```

```python
import jax
import jax.numpy as jnp
from jax import lax
from jax.experimental import pallas as pl
from jax.experimental.pallas import tpu as pltpu
from jax.sharding import PartitionSpec as P

HDIM = 64
BLOCK = 128
GROUP = 4
ROW = 4
LOG2E = 1.4426950408889634


def x_ring(peers, by):
    return [(i, (i // ROW) * ROW + (i % ROW + by) % ROW) for i in range(peers)]


def z_hop(x, peers, keep=None):
    half = peers // 2
    pairs = [
        (i * 4 + t, (i + ROW) * 4 + (t ^ 2 if i < half <= i + ROW else t))
        for i in range(peers - ROW)
        if keep is None or (i % ROW - keep) % ROW != 0
        for t in range(4)
    ]
    return lax.ppermute(x, ("seq", "tp"), pairs)


def tp_swap(x, mask):
    return lax.ppermute(x, "tp", [(i, i ^ mask) for i in range(4)])


def after(x, *others):
    return lax.optimization_barrier((x, *others))[0]


def rms_rows(rows):
    values = rows.astype(jnp.float32)
    power = jnp.mean(values * values, axis=-1, keepdims=True)
    return (values * lax.rsqrt(power + 1e-05)).astype(jnp.bfloat16)


def spread(place, own, core, across, diag):
    width = own.shape[1] // ROW

    def kernel(place_ref, own_ref, core_ref, across_ref, diag_ref, *outs):
        frame = place_ref[0]
        part = place_ref[1]
        x = place_ref[2]
        for k in range(ROW):
            cols = pl.ds(pl.multiple_of(lax.rem(x + k, ROW) * width, width), width)
            for j, ref in enumerate((own_ref, core_ref, across_ref, diag_ref)):
                for b in range(2):
                    start = b * BLOCK + frame if j < 2 else b * 64 + part
                    rows = pl.ds(pl.multiple_of(start, 32), 32)
                    outs[k][j * 2 + b] = ref[rows, cols]

    vmem = pl.BlockSpec(memory_space=pltpu.VMEM)
    return pl.pallas_call(
        kernel,
        in_specs=[pl.BlockSpec(memory_space=pltpu.SMEM)] + [vmem] * 4,
        out_specs=[vmem] * ROW,
        out_shape=[jax.ShapeDtypeStruct((8, 32, width), own.dtype)] * ROW,
        compiler_params=pltpu.CompilerParams(vmem_limit_bytes=24 << 20),
        name="spread",
    )(place, own, core, across, diag)


def pick(which, index, pieces):
    width = pieces[0].shape[2]
    count = len(pieces)

    def kernel(which_ref, index_ref, *rest):
        ins, outs = rest[:count], rest[count : count + 2 * ROW]
        held, sems = rest[count + 2 * ROW :]
        copies = [pltpu.make_async_copy(ins[a], held.at[a], sems.at[a]) for a in range(count)]
        for copy in copies:
            copy.start()
        for copy in copies:
            copy.wait()
        for k in range(ROW):
            for i in range(6):
                n = k * 6 + i
                outs[i // 3 * ROW + k][i % 3] = held[which_ref[n], index_ref[n]]

    smem = pl.BlockSpec(memory_space=pltpu.SMEM)
    outs = pl.pallas_call(
        kernel,
        in_specs=[smem] * 2 + [pl.BlockSpec(memory_space=pl.ANY)] * count,
        out_specs=[pl.BlockSpec(memory_space=pltpu.VMEM)] * (2 * ROW),
        out_shape=[jax.ShapeDtypeStruct((3, 32, width), pieces[0].dtype)] * (2 * ROW),
        scratch_shapes=[
            pltpu.VMEM((count, 8, 32, width), pieces[0].dtype),
            pltpu.SemaphoreType.DMA((count,)),
        ],
        compiler_params=pltpu.CompilerParams(vmem_limit_bytes=24 << 20),
        name="pick",
    )(which, index, *pieces)
    return outs[:ROW], outs[ROW:]


def memory_project(x, groups, w_key, w_value):
    rows, depth = groups[0].shape
    part = depth // ROW
    width = w_key.shape[1]

    def kernel(x_ref, *rest):
        pieces, (wk, wv, ok, ov) = rest[:4], rest[4:]
        held = [ref[...] for ref in pieces]
        power = [
            jnp.sum(jnp.square(h.astype(jnp.float32)), axis=1, keepdims=True) for h in held
        ]
        factor = lax.rsqrt(jnp.concatenate(power, axis=0) / depth + 1e-05)
        key = jnp.zeros((4 * rows, width), jnp.float32)
        value = jnp.zeros((4 * rows, width), jnp.float32)
        for k in range(ROW):
            piece = jnp.concatenate([h[:, k * part : (k + 1) * part] for h in held], axis=0)
            at = pl.ds(pl.multiple_of(lax.rem(x_ref[0] - k + ROW, ROW) * part, part), part)
            key += jnp.dot(piece, wk[at], preferred_element_type=jnp.float32)
            value += jnp.dot(piece, wv[at], preferred_element_type=jnp.float32)
        ok[...] = (key * factor).astype(jnp.bfloat16)
        ov[...] = (value * factor).astype(jnp.bfloat16)

    vmem = pl.BlockSpec(memory_space=pltpu.VMEM)
    return pl.pallas_call(
        kernel,
        in_specs=[pl.BlockSpec(memory_space=pltpu.SMEM)] + [vmem] * 6,
        out_specs=[vmem] * 2,
        out_shape=[jax.ShapeDtypeStruct((4 * rows, width), jnp.bfloat16)] * 2,
        cost_estimate=pl.CostEstimate(
            flops=16 * rows * depth * width, bytes_accessed=6 << 20, transcendentals=0
        ),
        compiler_params=pltpu.CompilerParams(vmem_limit_bytes=40 << 20),
        name="memory_project",
    )(x, *groups, w_key, w_value)


def attention(info, half, q, k, v, kn, vn, km, vm):
    rows, width = q.shape[0] // 2, q.shape[1]
    keys = 1024
    pair = 2 * HDIM

    def kernel(info_ref, q_ref, k_ref, v_ref, kn_ref, vn_ref, km_ref, vm_ref, o_ref, kc, vc):
        lane = lax.broadcasted_iota(jnp.int32, (1, pair), 1)
        key = lax.broadcasted_iota(jnp.int32, (1, keys), 1)
        slot = lax.rem(lax.div(key, 32), 3)
        listed = jnp.where(
            slot == 0, info_ref[0], jnp.where(slot == 1, info_ref[1], info_ref[2])
        )
        listed = jnp.where(key < 384, listed, 1)
        vc[:, pair:] = jnp.ones((keys, pair), jnp.bfloat16)
        for n in range(width // pair):
            col = slice(n * pair, (n + 1) * pair)
            kc[:384] = km_ref[:, col]
            vc[:384, :pair] = vm_ref[:, col]
            kc[384:512] = kn_ref[:, col]
            vc[384:512, :pair] = vn_ref[:, col]
            kc[512:] = k_ref[:, col]
            vc[512:, :pair] = v_ref[:, col]
            for b in range(rows // BLOCK):
                qb = q_ref[half * rows + b * BLOCK : half * rows + (b + 1) * BLOCK, col]
                here = jnp.where((key >= 384) & (key < 512), info_ref[3 + b], listed) > 0
                results = []
                for h in range(2):
                    mine = (lane < HDIM) if h == 0 else (lane >= HDIM)
                    s = lax.dot_general(
                        jnp.where(mine, qb, jnp.zeros_like(qb)),
                        kc[...],
                        (((1,), (1,)), ((), ())),
                        preferred_element_type=jnp.float32,
                    )
                    s = jnp.where(here, s, -1e30)
                    m = jnp.max(s, axis=1, keepdims=True)
                    p = jnp.exp2(s - m).astype(jnp.bfloat16)
                    o = jnp.dot(p, vc[...], preferred_element_type=jnp.float32)
                    results.append(o[:, :pair] / o[:, pair:])
                o_ref[b * BLOCK : (b + 1) * BLOCK, col] = jnp.where(
                    lane < HDIM, results[0], results[1]
                ).astype(jnp.bfloat16)

    vmem = pl.BlockSpec(memory_space=pltpu.VMEM)
    return pl.pallas_call(
        kernel,
        in_specs=[pl.BlockSpec(memory_space=pltpu.SMEM)] + [vmem] * 7,
        out_specs=vmem,
        out_shape=jax.ShapeDtypeStruct((rows, width), jnp.bfloat16),
        scratch_shapes=[
            pltpu.VMEM((keys, pair), jnp.bfloat16),
            pltpu.VMEM((keys, 2 * pair), jnp.bfloat16),
        ],
        cost_estimate=pl.CostEstimate(flops=1 << 20, bytes_accessed=1 << 16, transcendentals=0),
        compiler_params=pltpu.CompilerParams(vmem_limit_bytes=32 << 20),
        name="attention",
    )(info, q, k, v, kn, vn, km, vm)


def shards(frames, w_query, w_key, w_value, w_out, key_blocks):
    peers = lax.axis_size("seq")
    s = lax.axis_index("seq").astype(jnp.int32)
    t = lax.axis_index("tp").astype(jnp.int32)
    y, c, x, row = t // 2, t % 2, s % ROW, s // ROW
    scale = HDIM ** (-0.5) * LOG2E
    depth = frames.shape[1]

    def project(normed, weight, by=None):
        out = jnp.dot(normed, weight, preferred_element_type=jnp.float32)
        return (out if by is None else out * by).astype(jnp.bfloat16)

    def by_chip(pair):
        return jnp.where(y == 0, pair, pair[::-1])

    halves = frames.reshape(2, 2, 64, depth)
    ahead = lax.dynamic_index_in_dim(halves, 1 - y, 1, keepdims=False).reshape(128, depth)
    across_a = tp_swap(ahead, 2)
    core = tp_swap(after(frames, ahead), 1)

    near = rms_rows(jnp.concatenate([frames, core], axis=0))
    k_near, v_near = project(near, w_key), project(near, w_value)
    key_blocks = after(key_blocks, core)

    b0 = s * 8 + jnp.arange(2, dtype=jnp.int32)[:, None] * GROUP
    lists = key_blocks.reshape(2, GROUP, 8)
    first = lists[:, 0]
    valid = (first >= 0) & (first < b0)
    rank = jnp.cumsum(valid.astype(jnp.int32), axis=1) - 1
    slots = jnp.stack(
        [jnp.sum(jnp.where(valid & (rank == i), first + 1, 0), axis=1) for i in range(3)], axis=1
    ) - 1
    slots = by_chip(slots)
    with_next = jnp.any(lists == (b0 + GROUP)[:, :, None], axis=2).astype(jnp.int32)
    with_next = by_chip(with_next).reshape(2, 2, 2)
    with_next = jnp.where(c == 0, with_next, with_next[:, ::-1])
    listed = (slots >= 0).astype(jnp.int32)
    info = [[jnp.concatenate([listed[i], with_next[i, j]]) for j in range(2)] for i in range(2)]
    tables = [slots.reshape(6)] + [
        lax.ppermute(slots, "seq", x_ring(peers, -k)).reshape(6) for k in range(1, ROW)
    ]
    wanted = jnp.concatenate(tables)
    used = wanted >= 0
    which = jnp.where(used, (row - wanted // 32) * ROW + (x - wanted // 8 % ROW) % ROW, 0)
    half = peers // 2
    turned = jnp.where((wanted < half * 8) & (s >= half), 2, 0)
    index = jnp.where(used, ((wanted % 8 // 2) ^ t ^ turned) * 2 + wanted % 2, 0)

    across_a, k_near, v_near, which, index = lax.optimization_barrier(
        (across_a, k_near, v_near, which, index)
    )
    diag_a = tp_swap(across_a, 1)
    rest = lax.dynamic_index_in_dim(halves, y, 1, keepdims=False).reshape(128, depth)
    across_b = tp_swap(after(rest, across_a), 2)

    place = jnp.stack([y * 64 + c * 32, c * 32, x])
    pieces = spread(place, frames, core, across_a, diag_a)
    row0 = [pieces[0]] + [lax.ppermute(pieces[k], "seq", x_ring(peers, k)) for k in (1, 2, 3)]
    row1 = [z_hop(p, peers) for p in row0]
    across_b = after(across_b, row0[2])
    diag_b = tp_swap(across_b, 1)

    def natural(a, b):
        a, b = a.reshape(2, 1, 64, depth), b.reshape(2, 1, 64, depth)
        low, high = jnp.where(y == 0, a, b), jnp.where(y == 0, b, a)
        return jnp.concatenate([low, high], axis=1).reshape(256, depth)

    far = rms_rows(
        jnp.concatenate([natural(across_a, across_b), natural(diag_a, diag_b)], axis=0)
    )
    q_far, k_far, v_far = (
        project(far, w_query, scale),
        project(far, w_key),
        project(far, w_value),
    )

    passing = [*row1[:2], after(row1[2], q_far, k_far, v_far), after(row1[3], q_far, k_far, v_far)]
    row2 = [z_hop(p, peers, k) for k, p in enumerate(passing)]

    def block_at(near_part, far_part, pair_index):
        both = jnp.stack([near_part.reshape(2, 256, -1), far_part.reshape(2, 256, -1)])
        both = both.reshape(4, 256, -1)[:, :BLOCK]
        return lax.dynamic_index_in_dim(both, pair_index ^ t, 0, keepdims=False)

    head = jnp.concatenate([block_at(k_near, k_far, 0), block_at(v_near, v_far, 0)], axis=1)
    following = lax.ppermute(
        after(head, row2[0]), "seq", [(i, i - 1) for i in range(1, peers)]
    )
    index, following = lax.optimization_barrier((index, following))
    chosen = pick(which, index, row0 + row1 + row2)

    def returned(parts):
        back = [parts[0]] + [lax.ppermute(parts[k], "seq", x_ring(peers, k)) for k in (1, 2, 3)]
        return jnp.concatenate([p.reshape(96, -1) for p in back], axis=1)

    here = [returned(chosen[0])]
    here.append(returned(lax.optimization_barrier((*chosen[1], here[0]))[:ROW]))
    over = tp_swap(here[0], 2)
    over_late = tp_swap(here[1], 2)
    far_memory = [here[1], tp_swap(here[1], 1), over, tp_swap(over, 1)]
    near_memory = [here[0], tp_swap(here[0], 1), over_late, tp_swap(over_late, 1)]
    at = x.reshape(1)

    middle = jnp.concatenate([block_at(k_near, k_far, 2), block_at(v_near, v_far, 2)], axis=1)
    next_far = jnp.where(y == 0, following, middle)
    next_near = jnp.where(y == 0, middle, following)
    width = k_near.shape[1]

    def mix(rows):
        return jnp.dot(rows, w_out, preferred_element_type=jnp.float32)

    far_rest = (
        k_far,
        v_far,
        next_far[:, :width],
        next_far[:, width:],
        *memory_project(at, far_memory, w_key, w_value),
    )
    far_other = mix(attention(info[1][1], 1, q_far, *far_rest)).astype(jnp.bfloat16)
    far_other = jnp.concatenate([tp_swap(part, 1) for part in jnp.split(far_other, 4)])
    far_own = mix(attention(info[1][0], 0, after(q_far, over_late), *far_rest))
    far_sum = (far_own + far_other.astype(jnp.float32)).astype(jnp.bfloat16)
    from_far = tp_swap(far_sum, 2)

    frames, core, *near_memory = lax.optimization_barrier((frames, core, *near_memory, far_sum))[:6]
    q_near = project(rms_rows(jnp.concatenate([frames, core], axis=0)), w_query, scale)
    near_rest = (
        k_near,
        v_near,
        next_near[:, :width],
        next_near[:, width:],
        *memory_project(at, near_memory, w_key, w_value),
    )
    near_other = mix(attention(info[0][1], 1, q_near, *near_rest)).astype(jnp.bfloat16)
    near_other = jnp.concatenate([tp_swap(part, 1) for part in jnp.split(near_other, 4)])
    near_own = mix(attention(info[0][0], 0, q_near, *near_rest))
    total = near_own + near_other.astype(jnp.float32) + from_far.astype(jnp.float32)
    return total.astype(jnp.bfloat16)


def solution(mesh):
    return jax.shard_map(
        shards,
        mesh=mesh,
        in_specs=(
            P(("seq", "tp"), None),
            P(None, "tp"),
            P(None, "tp"),
            P(None, "tp"),
            P("tp", None),
            P("seq", None),
        ),
        out_specs=P(("seq", "tp"), None),
        check_vma=False,
    )
```

```python
import jax
import jax.numpy as jnp
from jax import lax
from jax.experimental import pallas as pl
from jax.experimental.pallas import tpu as pltpu
from jax.sharding import PartitionSpec as P

HDIM = 64
BLOCK = 128
GROUP = 4
ROW = 4
LOG2E = 1.4426950408889634


def x_ring(peers, by):
    return [(i, (i // ROW) * ROW + (i % ROW + by) % ROW) for i in range(peers)]


def z_hop(x, peers, keep=None):
    half = peers // 2
    pairs = [
        (i * 4 + t, (i + ROW) * 4 + (t ^ 2 if i < half <= i + ROW else t))
        for i in range(peers - ROW)
        if keep is None or (i % ROW - keep) % ROW != 0
        for t in range(4)
    ]
    return lax.ppermute(x, ("seq", "tp"), pairs)


def tp_swap(x, mask):
    return lax.ppermute(x, "tp", [(i, i ^ mask) for i in range(4)])


def after(x, *others):
    return lax.optimization_barrier((x, *others))[0]


def rms_rows(rows):
    values = rows.astype(jnp.float32)
    power = jnp.mean(values * values, axis=-1, keepdims=True)
    return (values * lax.rsqrt(power + 1e-05)).astype(jnp.bfloat16)


def spread(place, own, core, across, diag):
    width = own.shape[1] // ROW

    def kernel(place_ref, own_ref, core_ref, across_ref, diag_ref, *outs):
        frame = place_ref[0]
        part = place_ref[1]
        x = place_ref[2]
        for k in range(ROW):
            cols = pl.ds(pl.multiple_of(lax.rem(x + k, ROW) * width, width), width)
            for j, ref in enumerate((own_ref, core_ref, across_ref, diag_ref)):
                for b in range(2):
                    start = b * BLOCK + frame if j < 2 else b * 64 + part
                    rows = pl.ds(pl.multiple_of(start, 32), 32)
                    outs[k][j * 2 + b] = ref[rows, cols]

    vmem = pl.BlockSpec(memory_space=pltpu.VMEM)
    return pl.pallas_call(
        kernel,
        in_specs=[pl.BlockSpec(memory_space=pltpu.SMEM)] + [vmem] * 4,
        out_specs=[vmem] * ROW,
        out_shape=[jax.ShapeDtypeStruct((8, 32, width), own.dtype)] * ROW,
        compiler_params=pltpu.CompilerParams(vmem_limit_bytes=24 << 20),
        name="spread",
    )(place, own, core, across, diag)


def pick(which, index, pieces):
    width = pieces[0].shape[2]
    count = len(pieces)

    def kernel(which_ref, index_ref, *rest):
        ins, outs = rest[:count], rest[count : count + 2 * ROW]
        held, sems = rest[count + 2 * ROW :]
        copies = [pltpu.make_async_copy(ins[a], held.at[a], sems.at[a]) for a in range(count)]
        for copy in copies:
            copy.start()
        for copy in copies:
            copy.wait()
        for k in range(ROW):
            for i in range(6):
                n = k * 6 + i
                outs[i // 3 * ROW + k][i % 3] = held[which_ref[n], index_ref[n]]

    smem = pl.BlockSpec(memory_space=pltpu.SMEM)
    outs = pl.pallas_call(
        kernel,
        in_specs=[smem] * 2 + [pl.BlockSpec(memory_space=pl.ANY)] * count,
        out_specs=[pl.BlockSpec(memory_space=pltpu.VMEM)] * (2 * ROW),
        out_shape=[jax.ShapeDtypeStruct((3, 32, width), pieces[0].dtype)] * (2 * ROW),
        scratch_shapes=[
            pltpu.VMEM((count, 8, 32, width), pieces[0].dtype),
            pltpu.SemaphoreType.DMA((count,)),
        ],
        compiler_params=pltpu.CompilerParams(vmem_limit_bytes=24 << 20),
        name="pick",
    )(which, index, *pieces)
    return outs[:ROW], outs[ROW:]


def memory_project(x, groups, w_key, w_value):
    rows, depth = groups[0].shape
    part = depth // ROW
    width = w_key.shape[1]

    def kernel(x_ref, *rest):
        pieces, (wk, wv, ok, ov) = rest[:4], rest[4:]
        held = [ref[...] for ref in pieces]
        power = [
            jnp.sum(jnp.square(h.astype(jnp.float32)), axis=1, keepdims=True) for h in held
        ]
        factor = lax.rsqrt(jnp.concatenate(power, axis=0) / depth + 1e-05)
        key = jnp.zeros((4 * rows, width), jnp.float32)
        value = jnp.zeros((4 * rows, width), jnp.float32)
        for k in range(ROW):
            piece = jnp.concatenate([h[:, k * part : (k + 1) * part] for h in held], axis=0)
            at = pl.ds(pl.multiple_of(lax.rem(x_ref[0] - k + ROW, ROW) * part, part), part)
            key += jnp.dot(piece, wk[at], preferred_element_type=jnp.float32)
            value += jnp.dot(piece, wv[at], preferred_element_type=jnp.float32)
        ok[...] = (key * factor).astype(jnp.bfloat16)
        ov[...] = (value * factor).astype(jnp.bfloat16)

    vmem = pl.BlockSpec(memory_space=pltpu.VMEM)
    return pl.pallas_call(
        kernel,
        in_specs=[pl.BlockSpec(memory_space=pltpu.SMEM)] + [vmem] * 6,
        out_specs=[vmem] * 2,
        out_shape=[jax.ShapeDtypeStruct((4 * rows, width), jnp.bfloat16)] * 2,
        cost_estimate=pl.CostEstimate(
            flops=16 * rows * depth * width, bytes_accessed=6 << 20, transcendentals=0
        ),
        compiler_params=pltpu.CompilerParams(vmem_limit_bytes=40 << 20),
        name="memory_project",
    )(x, *groups, w_key, w_value)


def attention(info, half, q, k, v, kn, vn, km, vm):
    rows, width = q.shape[0] // 2, q.shape[1]
    keys = 1024
    pair = 2 * HDIM

    def kernel(info_ref, q_ref, k_ref, v_ref, kn_ref, vn_ref, km_ref, vm_ref, o_ref, kc, vc):
        lane = lax.broadcasted_iota(jnp.int32, (1, pair), 1)
        key = lax.broadcasted_iota(jnp.int32, (1, keys), 1)
        slot = lax.rem(lax.div(key, 32), 3)
        listed = jnp.where(
            slot == 0, info_ref[0], jnp.where(slot == 1, info_ref[1], info_ref[2])
        )
        listed = jnp.where(key < 384, listed, 1)
        vc[:, pair:] = jnp.ones((keys, pair), jnp.bfloat16)
        for n in range(width // pair):
            col = slice(n * pair, (n + 1) * pair)
            kc[:384] = km_ref[:, col]
            vc[:384, :pair] = vm_ref[:, col]
            kc[384:512] = kn_ref[:, col]
            vc[384:512, :pair] = vn_ref[:, col]
            kc[512:] = k_ref[:, col]
            vc[512:, :pair] = v_ref[:, col]
            for b in range(rows // BLOCK):
                qb = q_ref[half * rows + b * BLOCK : half * rows + (b + 1) * BLOCK, col]
                here = jnp.where((key >= 384) & (key < 512), info_ref[3 + b], listed) > 0
                results = []
                for h in range(2):
                    mine = (lane < HDIM) if h == 0 else (lane >= HDIM)
                    s = lax.dot_general(
                        jnp.where(mine, qb, jnp.zeros_like(qb)),
                        kc[...],
                        (((1,), (1,)), ((), ())),
                        preferred_element_type=jnp.float32,
                    )
                    s = jnp.where(here, s, -1e30)
                    m = jnp.max(s, axis=1, keepdims=True)
                    p = jnp.exp2(s - m).astype(jnp.bfloat16)
                    o = jnp.dot(p, vc[...], preferred_element_type=jnp.float32)
                    results.append(o[:, :pair] / o[:, pair:])
                o_ref[b * BLOCK : (b + 1) * BLOCK, col] = jnp.where(
                    lane < HDIM, results[0], results[1]
                ).astype(jnp.bfloat16)

    vmem = pl.BlockSpec(memory_space=pltpu.VMEM)
    return pl.pallas_call(
        kernel,
        in_specs=[pl.BlockSpec(memory_space=pltpu.SMEM)] + [vmem] * 7,
        out_specs=vmem,
        out_shape=jax.ShapeDtypeStruct((rows, width), jnp.bfloat16),
        scratch_shapes=[
            pltpu.VMEM((keys, pair), jnp.bfloat16),
            pltpu.VMEM((keys, 2 * pair), jnp.bfloat16),
        ],
        cost_estimate=pl.CostEstimate(flops=1 << 20, bytes_accessed=1 << 16, transcendentals=0),
        compiler_params=pltpu.CompilerParams(vmem_limit_bytes=32 << 20),
        name="attention",
    )(info, q, k, v, kn, vn, km, vm)


def shards(frames, w_query, w_key, w_value, w_out, key_blocks):
    peers = lax.axis_size("seq")
    s = lax.axis_index("seq").astype(jnp.int32)
    t = lax.axis_index("tp").astype(jnp.int32)
    y, c, x, row = t // 2, t % 2, s % ROW, s // ROW
    scale = HDIM ** (-0.5) * LOG2E
    depth = frames.shape[1]

    def project(normed, weight, by=None):
        out = jnp.dot(normed, weight, preferred_element_type=jnp.float32)
        return (out if by is None else out * by).astype(jnp.bfloat16)

    def by_chip(pair):
        return jnp.where(y == 0, pair, pair[::-1])

    halves = frames.reshape(2, 2, 64, depth)
    ahead = lax.dynamic_index_in_dim(halves, 1 - y, 1, keepdims=False).reshape(128, depth)
    across_a = tp_swap(ahead, 2)
    core = tp_swap(after(frames, ahead), 1)

    near = rms_rows(jnp.concatenate([frames, core], axis=0))
    k_near, v_near = project(near, w_key), project(near, w_value)
    key_blocks = after(key_blocks, core)

    b0 = s * 8 + jnp.arange(2, dtype=jnp.int32)[:, None] * GROUP
    lists = key_blocks.reshape(2, GROUP, 8)
    first = lists[:, 0]
    valid = (first >= 0) & (first < b0)
    rank = jnp.cumsum(valid.astype(jnp.int32), axis=1) - 1
    slots = jnp.stack(
        [jnp.sum(jnp.where(valid & (rank == i), first + 1, 0), axis=1) for i in range(3)], axis=1
    ) - 1
    slots = by_chip(slots)
    with_next = jnp.any(lists == (b0 + GROUP)[:, :, None], axis=2).astype(jnp.int32)
    with_next = by_chip(with_next).reshape(2, 2, 2)
    with_next = jnp.where(c == 0, with_next, with_next[:, ::-1])
    listed = (slots >= 0).astype(jnp.int32)
    info = [[jnp.concatenate([listed[i], with_next[i, j]]) for j in range(2)] for i in range(2)]
    tables = [slots.reshape(6)] + [
        lax.ppermute(slots, "seq", x_ring(peers, -k)).reshape(6) for k in range(1, ROW)
    ]
    wanted = jnp.concatenate(tables)
    used = wanted >= 0
    which = jnp.where(used, (row - wanted // 32) * ROW + (x - wanted // 8 % ROW) % ROW, 0)
    half = peers // 2
    turned = jnp.where((wanted < half * 8) & (s >= half), 2, 0)
    index = jnp.where(used, ((wanted % 8 // 2) ^ t ^ turned) * 2 + wanted % 2, 0)

    across_a, k_near, v_near, which, index = lax.optimization_barrier(
        (across_a, k_near, v_near, which, index)
    )
    diag_a = tp_swap(across_a, 1)
    rest = lax.dynamic_index_in_dim(halves, y, 1, keepdims=False).reshape(128, depth)
    across_b = tp_swap(after(rest, across_a), 2)

    place = jnp.stack([y * 64 + c * 32, c * 32, x])
    pieces = spread(place, frames, core, across_a, diag_a)
    row0 = [pieces[0]] + [lax.ppermute(pieces[k], "seq", x_ring(peers, k)) for k in (1, 2, 3)]
    row1 = [z_hop(p, peers) for p in row0]
    across_b = after(across_b, row0[2])
    diag_b = tp_swap(across_b, 1)

    def natural(a, b):
        a, b = a.reshape(2, 1, 64, depth), b.reshape(2, 1, 64, depth)
        low, high = jnp.where(y == 0, a, b), jnp.where(y == 0, b, a)
        return jnp.concatenate([low, high], axis=1).reshape(256, depth)

    far = rms_rows(
        jnp.concatenate([natural(across_a, across_b), natural(diag_a, diag_b)], axis=0)
    )
    q_far, k_far, v_far = (
        project(far, w_query, scale),
        project(far, w_key),
        project(far, w_value),
    )

    passing = [*row1[:2], after(row1[2], q_far, k_far, v_far), after(row1[3], q_far, k_far, v_far)]
    row2 = [z_hop(p, peers, k) for k, p in enumerate(passing)]

    def block_at(near_part, far_part, pair_index):
        both = jnp.stack([near_part.reshape(2, 256, -1), far_part.reshape(2, 256, -1)])
        both = both.reshape(4, 256, -1)[:, :BLOCK]
        return lax.dynamic_index_in_dim(both, pair_index ^ t, 0, keepdims=False)

    head = jnp.concatenate([block_at(k_near, k_far, 0), block_at(v_near, v_far, 0)], axis=1)
    index = after(index, q_far, head)
    chosen = pick(which, index, row0 + row1 + row2)

    def returned(parts):
        back = [parts[0]] + [lax.ppermute(parts[k], "seq", x_ring(peers, k)) for k in (1, 2, 3)]
        return jnp.concatenate([p.reshape(96, -1) for p in back], axis=1)

    here = [returned(chosen[0])]
    here.append(returned(lax.optimization_barrier((*chosen[1], here[0]))[:ROW]))
    following = lax.ppermute(
        after(head, here[0]), "seq", [(i, i - 1) for i in range(1, peers)]
    )
    over = tp_swap(here[0], 2)
    over_late = tp_swap(here[1], 2)
    far_memory = [here[1], tp_swap(here[1], 1), over, tp_swap(over, 1)]
    near_memory = [here[0], tp_swap(here[0], 1), over_late, tp_swap(over_late, 1)]
    at = x.reshape(1)

    middle = jnp.concatenate([block_at(k_near, k_far, 2), block_at(v_near, v_far, 2)], axis=1)
    far_memory = memory_project(at, far_memory, w_key, w_value)
    next_far = jnp.where(y == 0, following, middle)
    next_near = jnp.where(y == 0, middle, following)
    width = k_near.shape[1]

    def mix(rows):
        return jnp.dot(rows, w_out, preferred_element_type=jnp.float32)

    far_rest = (
        k_far,
        v_far,
        next_far[:, :width],
        next_far[:, width:],
        *far_memory,
    )
    far_other = mix(attention(info[1][1], 1, q_far, *far_rest)).astype(jnp.bfloat16)
    far_other = jnp.concatenate([tp_swap(part, 1) for part in jnp.split(far_other, 4)])
    far_own = mix(attention(info[1][0], 0, after(q_far, over_late), *far_rest))
    far_sum = (far_own + far_other.astype(jnp.float32)).astype(jnp.bfloat16)
    from_far = tp_swap(far_sum, 2)

    frames, core, *near_memory = lax.optimization_barrier((frames, core, *near_memory, far_sum))[:6]
    q_near = project(rms_rows(jnp.concatenate([frames, core], axis=0)), w_query, scale)
    near_rest = (
        k_near,
        v_near,
        next_near[:, :width],
        next_near[:, width:],
        *memory_project(at, near_memory, w_key, w_value),
    )
    near_other = mix(attention(info[0][1], 1, q_near, *near_rest)).astype(jnp.bfloat16)
    near_other = jnp.concatenate([tp_swap(part, 1) for part in jnp.split(near_other, 4)])
    near_own = mix(attention(info[0][0], 0, q_near, *near_rest))
    total = near_own + near_other.astype(jnp.float32) + from_far.astype(jnp.float32)
    return total.astype(jnp.bfloat16)


def solution(mesh):
    return jax.shard_map(
        shards,
        mesh=mesh,
        in_specs=(
            P(("seq", "tp"), None),
            P(None, "tp"),
            P(None, "tp"),
            P(None, "tp"),
            P("tp", None),
            P("seq", None),
        ),
        out_specs=P(("seq", "tp"), None),
        check_vma=False,
    )
```

```python
import jax
import jax.numpy as jnp
from jax import lax
from jax.experimental import pallas as pl
from jax.experimental.pallas import tpu as pltpu
from jax.sharding import PartitionSpec as P

HDIM = 64
BLOCK = 128
GROUP = 4
ROW = 4
LOG2E = 1.4426950408889634


def x_ring(peers, by):
    return [(i, (i // ROW) * ROW + (i % ROW + by) % ROW) for i in range(peers)]


def z_hop(x, peers, keep=None):
    half = peers // 2
    pairs = [
        (i * 4 + t, (i + ROW) * 4 + (t ^ 2 if i < half <= i + ROW else t))
        for i in range(peers - ROW)
        if keep is None or (i % ROW - keep) % ROW != 0
        for t in range(4)
    ]
    return lax.ppermute(x, ("seq", "tp"), pairs)


def tp_swap(x, mask):
    return lax.ppermute(x, "tp", [(i, i ^ mask) for i in range(4)])


def after(x, *others):
    return lax.optimization_barrier((x, *others))[0]


def rms_rows(rows):
    values = rows.astype(jnp.float32)
    power = jnp.mean(values * values, axis=-1, keepdims=True)
    return (values * lax.rsqrt(power + 1e-05)).astype(jnp.bfloat16)


def spread(place, own, core, across, diag):
    width = own.shape[1] // ROW

    def kernel(place_ref, own_ref, core_ref, across_ref, diag_ref, *outs):
        frame = place_ref[0]
        part = place_ref[1]
        x = place_ref[2]
        for k in range(ROW):
            cols = pl.ds(pl.multiple_of(lax.rem(x + k, ROW) * width, width), width)
            for j, ref in enumerate((own_ref, core_ref, across_ref, diag_ref)):
                for b in range(2):
                    start = b * BLOCK + frame if j < 2 else b * 64 + part
                    rows = pl.ds(pl.multiple_of(start, 32), 32)
                    outs[k][j * 2 + b] = ref[rows, cols]

    vmem = pl.BlockSpec(memory_space=pltpu.VMEM)
    return pl.pallas_call(
        kernel,
        in_specs=[pl.BlockSpec(memory_space=pltpu.SMEM)] + [vmem] * 4,
        out_specs=[vmem] * ROW,
        out_shape=[jax.ShapeDtypeStruct((8, 32, width), own.dtype)] * ROW,
        compiler_params=pltpu.CompilerParams(vmem_limit_bytes=24 << 20),
        name="spread",
    )(place, own, core, across, diag)


def pick(which, index, pieces):
    width = pieces[0].shape[2]
    count = len(pieces)

    def kernel(which_ref, index_ref, *rest):
        ins, outs = rest[:count], rest[count : count + 2 * ROW]
        held, sems = rest[count + 2 * ROW :]
        copies = [pltpu.make_async_copy(ins[a], held.at[a], sems.at[a]) for a in range(count)]
        for copy in copies:
            copy.start()
        for copy in copies:
            copy.wait()
        for k in range(ROW):
            for i in range(6):
                n = k * 6 + i
                outs[i // 3 * ROW + k][i % 3] = held[which_ref[n], index_ref[n]]

    smem = pl.BlockSpec(memory_space=pltpu.SMEM)
    outs = pl.pallas_call(
        kernel,
        in_specs=[smem] * 2 + [pl.BlockSpec(memory_space=pl.ANY)] * count,
        out_specs=[pl.BlockSpec(memory_space=pltpu.VMEM)] * (2 * ROW),
        out_shape=[jax.ShapeDtypeStruct((3, 32, width), pieces[0].dtype)] * (2 * ROW),
        scratch_shapes=[
            pltpu.VMEM((count, 8, 32, width), pieces[0].dtype),
            pltpu.SemaphoreType.DMA((count,)),
        ],
        compiler_params=pltpu.CompilerParams(vmem_limit_bytes=24 << 20),
        name="pick",
    )(which, index, *pieces)
    return outs[:ROW], outs[ROW:]


def memory_project(x, groups, w_key, w_value):
    rows, depth = groups[0].shape
    part = depth // ROW
    width = w_key.shape[1]

    def kernel(x_ref, *rest):
        pieces, (wk, wv, ok, ov) = rest[:4], rest[4:]
        held = [ref[...] for ref in pieces]
        power = [
            jnp.sum(jnp.square(h.astype(jnp.float32)), axis=1, keepdims=True) for h in held
        ]
        factor = lax.rsqrt(jnp.concatenate(power, axis=0) / depth + 1e-05)
        key = jnp.zeros((4 * rows, width), jnp.float32)
        value = jnp.zeros((4 * rows, width), jnp.float32)
        for k in range(ROW):
            piece = jnp.concatenate([h[:, k * part : (k + 1) * part] for h in held], axis=0)
            at = pl.ds(pl.multiple_of(lax.rem(x_ref[0] - k + ROW, ROW) * part, part), part)
            key += jnp.dot(piece, wk[at], preferred_element_type=jnp.float32)
            value += jnp.dot(piece, wv[at], preferred_element_type=jnp.float32)
        ok[...] = (key * factor).astype(jnp.bfloat16)
        ov[...] = (value * factor).astype(jnp.bfloat16)

    vmem = pl.BlockSpec(memory_space=pltpu.VMEM)
    return pl.pallas_call(
        kernel,
        in_specs=[pl.BlockSpec(memory_space=pltpu.SMEM)] + [vmem] * 6,
        out_specs=[vmem] * 2,
        out_shape=[jax.ShapeDtypeStruct((4 * rows, width), jnp.bfloat16)] * 2,
        cost_estimate=pl.CostEstimate(
            flops=16 * rows * depth * width, bytes_accessed=6 << 20, transcendentals=0
        ),
        compiler_params=pltpu.CompilerParams(vmem_limit_bytes=40 << 20),
        name="memory_project",
    )(x, *groups, w_key, w_value)


def attention(info, half, q, k, v, kn, vn, km, vm):
    rows, width = q.shape[0] // 2, q.shape[1]
    keys = 1024
    pair = 2 * HDIM

    def kernel(info_ref, q_ref, k_ref, v_ref, kn_ref, vn_ref, km_ref, vm_ref, o_ref, kc, vc):
        lane = lax.broadcasted_iota(jnp.int32, (1, pair), 1)
        key = lax.broadcasted_iota(jnp.int32, (1, keys), 1)
        slot = lax.rem(lax.div(key, 32), 3)
        listed = jnp.where(
            slot == 0, info_ref[0], jnp.where(slot == 1, info_ref[1], info_ref[2])
        )
        listed = jnp.where(key < 384, listed, 1)
        vc[:, pair:] = jnp.ones((keys, pair), jnp.bfloat16)
        for n in range(width // pair):
            col = slice(n * pair, (n + 1) * pair)
            kc[:384] = km_ref[:, col]
            vc[:384, :pair] = vm_ref[:, col]
            kc[384:512] = kn_ref[:, col]
            vc[384:512, :pair] = vn_ref[:, col]
            kc[512:] = k_ref[:, col]
            vc[512:, :pair] = v_ref[:, col]
            for b in range(rows // BLOCK):
                qb = q_ref[half * rows + b * BLOCK : half * rows + (b + 1) * BLOCK, col]
                here = jnp.where((key >= 384) & (key < 512), info_ref[3 + b], listed) > 0
                results = []
                for h in range(2):
                    mine = (lane < HDIM) if h == 0 else (lane >= HDIM)
                    s = lax.dot_general(
                        jnp.where(mine, qb, jnp.zeros_like(qb)),
                        kc[...],
                        (((1,), (1,)), ((), ())),
                        preferred_element_type=jnp.float32,
                    )
                    s = jnp.where(here, s, -1e30)
                    m = jnp.max(s, axis=1, keepdims=True)
                    p = jnp.exp2(s - m).astype(jnp.bfloat16)
                    o = jnp.dot(p, vc[...], preferred_element_type=jnp.float32)
                    results.append(o[:, :pair] / o[:, pair:])
                o_ref[b * BLOCK : (b + 1) * BLOCK, col] = jnp.where(
                    lane < HDIM, results[0], results[1]
                ).astype(jnp.bfloat16)

    vmem = pl.BlockSpec(memory_space=pltpu.VMEM)
    return pl.pallas_call(
        kernel,
        in_specs=[pl.BlockSpec(memory_space=pltpu.SMEM)] + [vmem] * 7,
        out_specs=vmem,
        out_shape=jax.ShapeDtypeStruct((rows, width), jnp.bfloat16),
        scratch_shapes=[
            pltpu.VMEM((keys, pair), jnp.bfloat16),
            pltpu.VMEM((keys, 2 * pair), jnp.bfloat16),
        ],
        cost_estimate=pl.CostEstimate(flops=1 << 20, bytes_accessed=1 << 16, transcendentals=0),
        compiler_params=pltpu.CompilerParams(vmem_limit_bytes=32 << 20),
        name="attention",
    )(info, q, k, v, kn, vn, km, vm)


def shards(frames, w_query, w_key, w_value, w_out, key_blocks):
    peers = lax.axis_size("seq")
    s = lax.axis_index("seq").astype(jnp.int32)
    t = lax.axis_index("tp").astype(jnp.int32)
    y, c, x, row = t // 2, t % 2, s % ROW, s // ROW
    scale = HDIM ** (-0.5) * LOG2E
    depth = frames.shape[1]

    def project(normed, weight, by=None):
        out = jnp.dot(normed, weight, preferred_element_type=jnp.float32)
        return (out if by is None else out * by).astype(jnp.bfloat16)

    def by_chip(pair):
        return jnp.where(y == 0, pair, pair[::-1])

    halves = frames.reshape(2, 2, 64, depth)
    ahead = lax.dynamic_index_in_dim(halves, 1 - y, 1, keepdims=False).reshape(128, depth)
    across_a = tp_swap(ahead, 2)
    core = tp_swap(after(frames, ahead), 1)

    v_near = project(rms_rows(jnp.concatenate([frames, core], axis=0)), w_value)
    key_blocks = after(key_blocks, core)

    b0 = s * 8 + jnp.arange(2, dtype=jnp.int32)[:, None] * GROUP
    lists = key_blocks.reshape(2, GROUP, 8)
    first = lists[:, 0]
    valid = (first >= 0) & (first < b0)
    rank = jnp.cumsum(valid.astype(jnp.int32), axis=1) - 1
    slots = jnp.stack(
        [jnp.sum(jnp.where(valid & (rank == i), first + 1, 0), axis=1) for i in range(3)], axis=1
    ) - 1
    slots = by_chip(slots)
    with_next = jnp.any(lists == (b0 + GROUP)[:, :, None], axis=2).astype(jnp.int32)
    with_next = by_chip(with_next).reshape(2, 2, 2)
    with_next = jnp.where(c == 0, with_next, with_next[:, ::-1])
    listed = (slots >= 0).astype(jnp.int32)
    info = [[jnp.concatenate([listed[i], with_next[i, j]]) for j in range(2)] for i in range(2)]
    tables = [slots.reshape(6)] + [
        lax.ppermute(slots, "seq", x_ring(peers, -k)).reshape(6) for k in range(1, ROW)
    ]
    wanted = jnp.concatenate(tables)
    used = wanted >= 0
    which = jnp.where(used, (row - wanted // 32) * ROW + (x - wanted // 8 % ROW) % ROW, 0)
    half = peers // 2
    turned = jnp.where((wanted < half * 8) & (s >= half), 2, 0)
    index = jnp.where(used, ((wanted % 8 // 2) ^ t ^ turned) * 2 + wanted % 2, 0)

    across_a, v_near, which, index = lax.optimization_barrier((across_a, v_near, which, index))
    diag_a = tp_swap(across_a, 1)
    rest = lax.dynamic_index_in_dim(halves, y, 1, keepdims=False).reshape(128, depth)
    across_b = tp_swap(after(rest, across_a), 2)

    place = jnp.stack([y * 64 + c * 32, c * 32, x])
    pieces = spread(place, frames, core, across_a, diag_a)
    row0 = [pieces[0]] + [lax.ppermute(pieces[k], "seq", x_ring(peers, k)) for k in (1, 2, 3)]
    row1 = [z_hop(p, peers) for p in row0]
    across_b = after(across_b, row0[2])
    diag_b = tp_swap(across_b, 1)

    def natural(a, b):
        a, b = a.reshape(2, 1, 64, depth), b.reshape(2, 1, 64, depth)
        low, high = jnp.where(y == 0, a, b), jnp.where(y == 0, b, a)
        return jnp.concatenate([low, high], axis=1).reshape(256, depth)

    far = rms_rows(
        jnp.concatenate([natural(across_a, across_b), natural(diag_a, diag_b)], axis=0)
    )
    q_far, k_far, v_far = (
        project(far, w_query, scale),
        project(far, w_key),
        project(far, w_value),
    )

    passing = [*row1[:2], after(row1[2], q_far, k_far, v_far), after(row1[3], q_far, k_far, v_far)]
    row2 = [z_hop(p, peers, k) for k, p in enumerate(passing)]

    near = jnp.concatenate(lax.optimization_barrier((frames, core, q_far))[:2], axis=0)
    k_near = project(rms_rows(near), w_key)

    def block_at(near_part, far_part, pair_index):
        both = jnp.stack([near_part.reshape(2, 256, -1), far_part.reshape(2, 256, -1)])
        both = both.reshape(4, 256, -1)[:, :BLOCK]
        return lax.dynamic_index_in_dim(both, pair_index ^ t, 0, keepdims=False)

    head = jnp.concatenate([block_at(k_near, k_far, 0), block_at(v_near, v_far, 0)], axis=1)
    index = after(index, q_far, head)
    chosen = pick(which, index, row0 + row1 + row2)

    def returned(parts):
        back = [parts[0]] + [lax.ppermute(parts[k], "seq", x_ring(peers, k)) for k in (1, 2, 3)]
        return jnp.concatenate([p.reshape(96, -1) for p in back], axis=1)

    here = [returned(chosen[0])]
    here.append(returned(lax.optimization_barrier((*chosen[1], here[0]))[:ROW]))
    following = lax.ppermute(
        after(head, here[0]), "seq", [(i, i - 1) for i in range(1, peers)]
    )
    over = tp_swap(here[0], 2)
    over_late = tp_swap(here[1], 2)
    far_memory = [here[1], tp_swap(here[1], 1), over, tp_swap(over, 1)]
    near_memory = [here[0], tp_swap(here[0], 1), over_late, tp_swap(over_late, 1)]
    at = x.reshape(1)

    middle = jnp.concatenate([block_at(k_near, k_far, 2), block_at(v_near, v_far, 2)], axis=1)
    far_memory = memory_project(at, far_memory, w_key, w_value)
    next_far = jnp.where(y == 0, following, middle)
    next_near = jnp.where(y == 0, middle, following)
    width = k_near.shape[1]

    def mix(rows):
        return jnp.dot(rows, w_out, preferred_element_type=jnp.float32)

    far_rest = (
        k_far,
        v_far,
        next_far[:, :width],
        next_far[:, width:],
        *far_memory,
    )
    far_other = mix(attention(info[1][1], 1, q_far, *far_rest)).astype(jnp.bfloat16)
    far_other = jnp.concatenate([tp_swap(part, 1) for part in jnp.split(far_other, 4)])
    far_own = mix(attention(info[1][0], 0, after(q_far, over_late), *far_rest))
    far_sum = (far_own + far_other.astype(jnp.float32)).astype(jnp.bfloat16)
    from_far = tp_swap(far_sum, 2)

    frames, core, *near_memory = lax.optimization_barrier((frames, core, *near_memory, far_sum))[:6]
    q_near = project(rms_rows(jnp.concatenate([frames, core], axis=0)), w_query, scale)
    near_rest = (
        k_near,
        v_near,
        next_near[:, :width],
        next_near[:, width:],
        *memory_project(at, near_memory, w_key, w_value),
    )
    near_other = mix(attention(info[0][1], 1, q_near, *near_rest)).astype(jnp.bfloat16)
    near_other = jnp.concatenate([tp_swap(part, 1) for part in jnp.split(near_other, 4)])
    near_own = mix(attention(info[0][0], 0, q_near, *near_rest))
    total = near_own + near_other.astype(jnp.float32) + from_far.astype(jnp.float32)
    return total.astype(jnp.bfloat16)


def solution(mesh):
    return jax.shard_map(
        shards,
        mesh=mesh,
        in_specs=(
            P(("seq", "tp"), None),
            P(None, "tp"),
            P(None, "tp"),
            P(None, "tp"),
            P("tp", None),
            P("seq", None),
        ),
        out_specs=P(("seq", "tp"), None),
        check_vma=False,
    )
```

```python
import jax
import jax.numpy as jnp
from jax import lax
from jax.experimental import pallas as pl
from jax.experimental.pallas import tpu as pltpu
from jax.sharding import PartitionSpec as P

HDIM = 64
BLOCK = 128
GROUP = 4
ROW = 4
LOG2E = 1.4426950408889634


def x_ring(peers, by):
    return [(i, (i // ROW) * ROW + (i % ROW + by) % ROW) for i in range(peers)]


def z_hop(x, peers, keep=None):
    half = peers // 2
    pairs = [
        (i * 4 + t, (i + ROW) * 4 + (t ^ 2 if i < half <= i + ROW else t))
        for i in range(peers - ROW)
        if keep is None or (i % ROW - keep) % ROW != 0
        for t in range(4)
    ]
    return lax.ppermute(x, ("seq", "tp"), pairs)


def tp_swap(x, mask):
    return lax.ppermute(x, "tp", [(i, i ^ mask) for i in range(4)])


def after(x, *others):
    return lax.optimization_barrier((x, *others))[0]


def rms_rows(rows):
    values = rows.astype(jnp.float32)
    power = jnp.mean(values * values, axis=-1, keepdims=True)
    return (values * lax.rsqrt(power + 1e-05)).astype(jnp.bfloat16)


def spread(place, own, core, across, diag):
    width = own.shape[1] // ROW

    def kernel(place_ref, own_ref, core_ref, across_ref, diag_ref, *outs):
        frame = place_ref[0]
        part = place_ref[1]
        x = place_ref[2]
        for k in range(ROW):
            cols = pl.ds(pl.multiple_of(lax.rem(x + k, ROW) * width, width), width)
            for j, ref in enumerate((own_ref, core_ref, across_ref, diag_ref)):
                for b in range(2):
                    start = b * BLOCK + frame if j < 2 else b * 64 + part
                    rows = pl.ds(pl.multiple_of(start, 32), 32)
                    outs[k][j * 2 + b] = ref[rows, cols]

    vmem = pl.BlockSpec(memory_space=pltpu.VMEM)
    return pl.pallas_call(
        kernel,
        in_specs=[pl.BlockSpec(memory_space=pltpu.SMEM)] + [vmem] * 4,
        out_specs=[vmem] * ROW,
        out_shape=[jax.ShapeDtypeStruct((8, 32, width), own.dtype)] * ROW,
        compiler_params=pltpu.CompilerParams(vmem_limit_bytes=24 << 20),
        name="spread",
    )(place, own, core, across, diag)


def pick(which, index, pieces):
    width = pieces[0].shape[2]
    count = len(pieces)

    def kernel(which_ref, index_ref, *rest):
        ins, outs = rest[:count], rest[count : count + 2 * ROW]
        held, sems = rest[count + 2 * ROW :]
        copies = [pltpu.make_async_copy(ins[a], held.at[a], sems.at[a]) for a in range(count)]
        for copy in copies:
            copy.start()
        for copy in copies:
            copy.wait()
        for k in range(ROW):
            for i in range(6):
                n = k * 6 + i
                outs[i // 3 * ROW + k][i % 3] = held[which_ref[n], index_ref[n]]

    smem = pl.BlockSpec(memory_space=pltpu.SMEM)
    outs = pl.pallas_call(
        kernel,
        in_specs=[smem] * 2 + [pl.BlockSpec(memory_space=pl.ANY)] * count,
        out_specs=[pl.BlockSpec(memory_space=pltpu.VMEM)] * (2 * ROW),
        out_shape=[jax.ShapeDtypeStruct((3, 32, width), pieces[0].dtype)] * (2 * ROW),
        scratch_shapes=[
            pltpu.VMEM((count, 8, 32, width), pieces[0].dtype),
            pltpu.SemaphoreType.DMA((count,)),
        ],
        compiler_params=pltpu.CompilerParams(vmem_limit_bytes=24 << 20),
        name="pick",
    )(which, index, *pieces)
    return outs[:ROW], outs[ROW:]


def memory_project(x, groups, w_key, w_value):
    rows, depth = groups[0].shape
    part = depth // ROW
    width = w_key.shape[1]

    def kernel(x_ref, *rest):
        pieces, (wk, wv, ok, ov) = rest[:4], rest[4:]
        held = [ref[...] for ref in pieces]
        power = [
            jnp.sum(jnp.square(h.astype(jnp.float32)), axis=1, keepdims=True) for h in held
        ]
        factor = lax.rsqrt(jnp.concatenate(power, axis=0) / depth + 1e-05)
        key = jnp.zeros((4 * rows, width), jnp.float32)
        value = jnp.zeros((4 * rows, width), jnp.float32)
        for k in range(ROW):
            piece = jnp.concatenate([h[:, k * part : (k + 1) * part] for h in held], axis=0)
            at = pl.ds(pl.multiple_of(lax.rem(x_ref[0] - k + ROW, ROW) * part, part), part)
            key += jnp.dot(piece, wk[at], preferred_element_type=jnp.float32)
            value += jnp.dot(piece, wv[at], preferred_element_type=jnp.float32)
        ok[...] = (key * factor).astype(jnp.bfloat16)
        ov[...] = (value * factor).astype(jnp.bfloat16)

    vmem = pl.BlockSpec(memory_space=pltpu.VMEM)
    return pl.pallas_call(
        kernel,
        in_specs=[pl.BlockSpec(memory_space=pltpu.SMEM)] + [vmem] * 6,
        out_specs=[vmem] * 2,
        out_shape=[jax.ShapeDtypeStruct((4 * rows, width), jnp.bfloat16)] * 2,
        cost_estimate=pl.CostEstimate(
            flops=16 * rows * depth * width, bytes_accessed=6 << 20, transcendentals=0
        ),
        compiler_params=pltpu.CompilerParams(vmem_limit_bytes=40 << 20),
        name="memory_project",
    )(x, *groups, w_key, w_value)


def attention(info, half, q, k, v, kn, vn, km, vm):
    rows, width = q.shape[0] // 2, q.shape[1]
    keys = 1024
    pair = 2 * HDIM

    def kernel(info_ref, q_ref, k_ref, v_ref, kn_ref, vn_ref, km_ref, vm_ref, o_ref, kc, vc):
        lane = lax.broadcasted_iota(jnp.int32, (1, pair), 1)
        key = lax.broadcasted_iota(jnp.int32, (1, keys), 1)
        slot = lax.rem(lax.div(key, 32), 3)
        listed = jnp.where(
            slot == 0, info_ref[0], jnp.where(slot == 1, info_ref[1], info_ref[2])
        )
        listed = jnp.where(key < 384, listed, 1)
        vc[:, pair:] = jnp.ones((keys, pair), jnp.bfloat16)
        for n in range(width // pair):
            col = slice(n * pair, (n + 1) * pair)
            kc[:384] = km_ref[:, col]
            vc[:384, :pair] = vm_ref[:, col]
            kc[384:512] = kn_ref[:, col]
            vc[384:512, :pair] = vn_ref[:, col]
            kc[512:] = k_ref[:, col]
            vc[512:, :pair] = v_ref[:, col]
            for b in range(rows // BLOCK):
                qb = q_ref[half * rows + b * BLOCK : half * rows + (b + 1) * BLOCK, col]
                here = jnp.where((key >= 384) & (key < 512), info_ref[3 + b], listed) > 0
                results = []
                for h in range(2):
                    mine = (lane < HDIM) if h == 0 else (lane >= HDIM)
                    s = lax.dot_general(
                        jnp.where(mine, qb, jnp.zeros_like(qb)),
                        kc[...],
                        (((1,), (1,)), ((), ())),
                        preferred_element_type=jnp.float32,
                    )
                    s = jnp.where(here, s, -1e30)
                    m = jnp.max(s, axis=1, keepdims=True)
                    p = jnp.exp2(s - m).astype(jnp.bfloat16)
                    o = jnp.dot(p, vc[...], preferred_element_type=jnp.float32)
                    results.append(o[:, :pair] / o[:, pair:])
                o_ref[b * BLOCK : (b + 1) * BLOCK, col] = jnp.where(
                    lane < HDIM, results[0], results[1]
                ).astype(jnp.bfloat16)

    vmem = pl.BlockSpec(memory_space=pltpu.VMEM)
    return pl.pallas_call(
        kernel,
        in_specs=[pl.BlockSpec(memory_space=pltpu.SMEM)] + [vmem] * 7,
        out_specs=vmem,
        out_shape=jax.ShapeDtypeStruct((rows, width), jnp.bfloat16),
        scratch_shapes=[
            pltpu.VMEM((keys, pair), jnp.bfloat16),
            pltpu.VMEM((keys, 2 * pair), jnp.bfloat16),
        ],
        cost_estimate=pl.CostEstimate(flops=1 << 20, bytes_accessed=1 << 16, transcendentals=0),
        compiler_params=pltpu.CompilerParams(vmem_limit_bytes=32 << 20),
        name="attention",
    )(info, q, k, v, kn, vn, km, vm)


def shards(frames, w_query, w_key, w_value, w_out, key_blocks):
    peers = lax.axis_size("seq")
    s = lax.axis_index("seq").astype(jnp.int32)
    t = lax.axis_index("tp").astype(jnp.int32)
    y, c, x, row = t // 2, t % 2, s % ROW, s // ROW
    scale = HDIM ** (-0.5) * LOG2E
    depth = frames.shape[1]

    def project(normed, weight, by=None):
        out = jnp.dot(normed, weight, preferred_element_type=jnp.float32)
        return (out if by is None else out * by).astype(jnp.bfloat16)

    def by_chip(pair):
        return jnp.where(y == 0, pair, pair[::-1])

    halves = frames.reshape(2, 2, 64, depth)
    ahead = lax.dynamic_index_in_dim(halves, 1 - y, 1, keepdims=False).reshape(128, depth)
    across_a = tp_swap(ahead, 2)
    core = tp_swap(after(frames, ahead), 1)

    v_near = project(rms_rows(jnp.concatenate([frames, core], axis=0)), w_value)
    key_blocks = after(key_blocks, core)

    b0 = s * 8 + jnp.arange(2, dtype=jnp.int32)[:, None] * GROUP
    lists = key_blocks.reshape(2, GROUP, 8)
    first = lists[:, 0]
    valid = (first >= 0) & (first < b0)
    rank = jnp.cumsum(valid.astype(jnp.int32), axis=1) - 1
    slots = jnp.stack(
        [jnp.sum(jnp.where(valid & (rank == i), first + 1, 0), axis=1) for i in range(3)], axis=1
    ) - 1
    slots = by_chip(slots)
    with_next = jnp.any(lists == (b0 + GROUP)[:, :, None], axis=2).astype(jnp.int32)
    with_next = by_chip(with_next).reshape(2, 2, 2)
    with_next = jnp.where(c == 0, with_next, with_next[:, ::-1])
    listed = (slots >= 0).astype(jnp.int32)
    info = [[jnp.concatenate([listed[i], with_next[i, j]]) for j in range(2)] for i in range(2)]
    tables = [slots.reshape(6)] + [
        lax.ppermute(slots, "seq", x_ring(peers, -k)).reshape(6) for k in range(1, ROW)
    ]
    wanted = jnp.concatenate(tables)
    used = wanted >= 0
    which = jnp.where(used, (row - wanted // 32) * ROW + (x - wanted // 8 % ROW) % ROW, 0)
    half = peers // 2
    turned = jnp.where((wanted < half * 8) & (s >= half), 2, 0)
    index = jnp.where(used, ((wanted % 8 // 2) ^ t ^ turned) * 2 + wanted % 2, 0)

    rest = after(frames, core).reshape(halves.shape)
    rest = lax.dynamic_index_in_dim(rest, y, 1, keepdims=False).reshape(128, depth)
    across_a, v_near, which, index, rest = lax.optimization_barrier(
        (across_a, v_near, which, index, rest)
    )
    diag_a = tp_swap(across_a, 1)
    across_b = tp_swap(rest, 2)

    place = jnp.stack([y * 64 + c * 32, c * 32, x])
    pieces = spread(place, frames, core, across_a, diag_a)
    row0 = [pieces[0]] + [lax.ppermute(pieces[k], "seq", x_ring(peers, k)) for k in (1, 2, 3)]
    row1 = [z_hop(p, peers) for p in row0]
    across_b = after(across_b, row0[2])
    diag_b = tp_swap(across_b, 1)

    def natural(a, b):
        a, b = a.reshape(2, 1, 64, depth), b.reshape(2, 1, 64, depth)
        low, high = jnp.where(y == 0, a, b), jnp.where(y == 0, b, a)
        return jnp.concatenate([low, high], axis=1).reshape(256, depth)

    far = rms_rows(
        jnp.concatenate([natural(across_a, across_b), natural(diag_a, diag_b)], axis=0)
    )
    q_far, k_far, v_far = (
        project(far, w_query, scale),
        project(far, w_key),
        project(far, w_value),
    )

    passing = [*row1[:2], after(row1[2], q_far, k_far, v_far), after(row1[3], q_far, k_far, v_far)]
    row2 = [z_hop(p, peers, k) for k, p in enumerate(passing)]

    near = jnp.concatenate(lax.optimization_barrier((frames, core, q_far))[:2], axis=0)
    k_near = project(rms_rows(near), w_key)

    def block_at(near_part, far_part, pair_index):
        both = jnp.stack([near_part.reshape(2, 256, -1), far_part.reshape(2, 256, -1)])
        both = both.reshape(4, 256, -1)[:, :BLOCK]
        return lax.dynamic_index_in_dim(both, pair_index ^ t, 0, keepdims=False)

    head = jnp.concatenate([block_at(k_near, k_far, 0), block_at(v_near, v_far, 0)], axis=1)
    index = after(index, q_far, head)
    chosen = pick(which, index, row0 + row1 + row2)

    def returned(parts):
        back = [parts[0]] + [lax.ppermute(parts[k], "seq", x_ring(peers, k)) for k in (1, 2, 3)]
        return jnp.concatenate([p.reshape(96, -1) for p in back], axis=1)

    here = [returned(chosen[0])]
    here.append(returned(lax.optimization_barrier((*chosen[1], here[0]))[:ROW]))
    following = lax.ppermute(
        after(head, here[0]), "seq", [(i, i - 1) for i in range(1, peers)]
    )
    over = tp_swap(here[0], 2)
    over_late = tp_swap(here[1], 2)
    far_memory = [here[1], tp_swap(here[1], 1), over, tp_swap(over, 1)]
    near_memory = [here[0], tp_swap(here[0], 1), over_late, tp_swap(over_late, 1)]
    at = x.reshape(1)

    middle = jnp.concatenate([block_at(k_near, k_far, 2), block_at(v_near, v_far, 2)], axis=1)
    far_memory = memory_project(at, far_memory, w_key, w_value)
    next_far = jnp.where(y == 0, following, middle)
    next_near = jnp.where(y == 0, middle, following)
    width = k_near.shape[1]

    def mix(rows):
        return jnp.dot(rows, w_out, preferred_element_type=jnp.float32)

    far_rest = (
        k_far,
        v_far,
        next_far[:, :width],
        next_far[:, width:],
        *far_memory,
    )
    far_other = mix(attention(info[1][1], 1, q_far, *far_rest)).astype(jnp.bfloat16)
    far_other = jnp.concatenate([tp_swap(part, 1) for part in jnp.split(far_other, 4)])
    far_own = mix(attention(info[1][0], 0, after(q_far, over_late), *far_rest))
    far_sum = (far_own + far_other.astype(jnp.float32)).astype(jnp.bfloat16)
    from_far = tp_swap(far_sum, 2)

    frames, core, *near_memory = lax.optimization_barrier((frames, core, *near_memory, far_sum))[:6]
    q_near = project(rms_rows(jnp.concatenate([frames, core], axis=0)), w_query, scale)
    near_rest = (
        k_near,
        v_near,
        next_near[:, :width],
        next_near[:, width:],
        *memory_project(at, near_memory, w_key, w_value),
    )
    near_other = mix(attention(info[0][1], 1, q_near, *near_rest)).astype(jnp.bfloat16)
    near_other = jnp.concatenate([tp_swap(part, 1) for part in jnp.split(near_other, 4)])
    near_own = mix(attention(info[0][0], 0, q_near, *near_rest))
    total = near_own + near_other.astype(jnp.float32) + from_far.astype(jnp.float32)
    return total.astype(jnp.bfloat16)


def solution(mesh):
    return jax.shard_map(
        shards,
        mesh=mesh,
        in_specs=(
            P(("seq", "tp"), None),
            P(None, "tp"),
            P(None, "tp"),
            P(None, "tp"),
            P("tp", None),
            P("seq", None),
        ),
        out_specs=P(("seq", "tp"), None),
        check_vma=False,
    )
```
